32 devices in a mesh: height: 8 (over z, x), cols: 4 (over y, core).
Axes of the slice: x: 2, y: 2, z: 4, core: 2. Of those that a mesh axis runs over, the one named last changes fastest.
Arguments:
- positions: float32 [3, 16, 32, 128], P(None, 'height', 'cols'), may hold values from -0.5 to 0.5
- velocities: float32 [3, 16, 32, 128], P(None, 'height', 'cols'), may hold values from -3 to 3
- contacts: int32 [9, 16, 32], P(None, 'height', 'cols'), may hold values 0 or 1
- exit_flags: int32 [16, 32], P('height', 'cols'), may hold values from 0 to 1, as said below
- inlet_slots: int32 [8, 32], P('height', 'cols'), may hold values from 0 to 7, as said below
- cell_blocks: int32 [16, 32], P('height', 'cols'), may hold values from 0 to 511
- cell_slots: int32 [16, 32, 128], P('height', 'cols'), may hold values from 0 to 127
- gas_source: float32 [16, 256, 512], P('height', 'cols'), may hold values from -12 to 12
- diagonal: float32 [16, 256, 512], P('height', 'cols'), may hold values from 0.25 to 2
Outputs:
- positions_out: float32 [3, 16, 32, 128], P(None, 'height', 'cols')
- velocities_out: float32 [3, 16, 32, 128], P(None, 'height', 'cols')
- pressure: float32 [16, 256, 512], P('height', 'cols')
- residual: float32 [16, 256, 512], P('height', 'cols')
The draws below stay inside these ranges and needn't reach their ends.
Inputs may be any that keep to these rules, and one draw needn't show every extreme that they name: `exit_flags`: only the top tile row of each device's 2 tile rows holds ones; at most 8 ones on one device, exactly 8 on some device. `inlet_slots`: each device's 8 entries are a permutation of 0 to 7.
All inputs are finite; a program needn't handle non-finite values. No bound on the sum of `contacts` on one device may be relied on, other than what follows from the above.
Results may differ from the reference program's by a relative error of at most 0.0003.
Values sent between devices are 32-bit elements; how exact they have to be, the bound alone decides.
No kernel may reach another device: no remote copies, remote signals or barrier semaphores. Data moves between devices by JAX's collectives and lax.ppermute only.
A program may use at most 64 MiB of HBM per device.

```python
import jax
import jax.numpy as jnp
from jax import lax

P_SIZE = 128
TH = 2
TC = 8
GH = 2
GX = 64
GY = 512
ITERS = 2
SLABS = 8
COL_GROUPS = 4
TILE_ROWS = 16
TILE_COLS = 32
NZ = 16
NXC = 256
BLOCKS = 512


def draw_exit_flags(key, part):
    count_key, pick_key, order_key = jax.random.split(key, 3)
    counts = jax.random.randint(count_key, (SLABS, COL_GROUPS), 0, TC + 1)
    chosen = jax.random.randint(pick_key, (), 0, SLABS * COL_GROUPS)
    device_ids = jnp.arange(SLABS * COL_GROUPS, dtype=jnp.int32).reshape(SLABS, COL_GROUPS)
    counts = jnp.where(device_ids == chosen, TC, counts)
    scores = jax.random.randint(order_key, (SLABS, COL_GROUPS, TC), 0, 1 << 20) * TC + jnp.arange(TC, dtype=jnp.int32)
    ranks = jnp.argsort(jnp.argsort(scores, axis=-1), axis=-1)
    top_row = (ranks < counts[:, :, None]).astype(jnp.int32)
    whole = jnp.zeros((SLABS, TH, COL_GROUPS, TC), jnp.int32)
    whole = whole.at[:, TH - 1].set(top_row)
    return whole.reshape(SLABS * TH, COL_GROUPS * TC)


def draw_inlet_slots(key, part):
    scores = jax.random.randint(key, (SLABS, COL_GROUPS, TC), 0, 1 << 20) * TC + jnp.arange(TC, dtype=jnp.int32)
    order = jnp.argsort(scores, axis=-1).astype(jnp.int32)
    return order.reshape(SLABS, COL_GROUPS * TC)


def draw_gas_source(key, part):
    heights = jnp.arange(NZ, dtype=jnp.float32) / max(NZ - 1, 1)
    rising = (1.0 + 2.0 * heights)[:, None, None]
    rough = jnp.clip(jax.random.normal(key, (NZ, NXC, GY), jnp.float32), -4.0, 4.0)
    return rising * rough


def place_ends(result, stream_key, smallest, largest):
    longest = result.shape.index(max(result.shape))
    spots = []
    for shift in (0, 1):
        where = [jax.random.randint(jax.random.fold_in(stream_key, axis), (), 0, length) for axis, length in enumerate(result.shape)]
        where[longest] = (where[longest] + shift) % result.shape[longest]
        spots.append(tuple(where))
    return result.at[spots[0]].set(smallest).at[spots[1]].set(largest)


def shard_levels(own_key, extent, shards, low, largest):
    factor_of = 1.0
    for dim, blocks in shards:
        draws = jax.random.uniform(jax.random.fold_in(jax.random.fold_in(own_key, 6), dim), (blocks,), jnp.float32, low / len(shards), largest / len(shards))
        factor_of = factor_of * jnp.repeat(jnp.exp(draws), extent[dim] // blocks).reshape((-1,) + (1,) * (len(extent) - 1 - dim))
    return factor_of


def normal_values(rng, shape, scale, reach, cuts=(), kind=jnp.bfloat16):
    entries = scale * jax.random.normal(rng, shape, jnp.float32)
    if cuts:
        entries = entries * shard_levels(rng, shape, cuts, -0.22, 0.18)
    return jnp.clip(entries, -reach, reach).astype(kind)


def setup_inputs(seed: int = 0) -> dict:
    key_of = jax.random.split(jax.random.key(seed), 10)
    return {
        "positions": jnp.clip(jax.random.uniform(key_of[0], (3, TILE_ROWS, TILE_COLS, P_SIZE), jnp.float32, -0.5, 0.5) * shard_levels(key_of[0], (3, TILE_ROWS, TILE_COLS, P_SIZE), ((1, 8), (2, 4)), -0.4, 0.0), -0.5, 0.5),
        "velocities": normal_values(key_of[1], (3, TILE_ROWS, TILE_COLS, P_SIZE), 0.5, 3.0, ((1, 8), (2, 4)), jnp.float32),
        "contacts": place_ends((jax.random.randint(key_of[2], (9, TILE_ROWS, TILE_COLS), 0, 4) < 3).astype(jnp.int32), jax.random.fold_in(key_of[2], 1), 0, 1),
        "exit_flags": draw_exit_flags(jax.random.fold_in(key_of[9], 71), 0),
        "inlet_slots": draw_inlet_slots(jax.random.fold_in(key_of[9], 71), 0),
        "cell_blocks": place_ends(jax.random.randint(key_of[5], (TILE_ROWS, TILE_COLS), 0, BLOCKS), jax.random.fold_in(key_of[5], 1), 0, BLOCKS - 1).astype(jnp.int32),
        "cell_slots": place_ends(jax.random.randint(key_of[6], (TILE_ROWS, TILE_COLS, P_SIZE), 0, P_SIZE), jax.random.fold_in(key_of[6], 1), 0, P_SIZE - 1).astype(jnp.int32),
        "gas_source": draw_gas_source(jax.random.fold_in(key_of[9], 71), 0),
        "diagonal": jnp.clip(0.25 + 1.75 * jax.random.uniform(key_of[8], (NZ, NXC, GY), jnp.float32) ** shard_levels(key_of[8], (NZ, NXC, GY), ((0, 8), (1, 4)), -0.2, 0.2), 0.25, 2.0),
    }


spring = 0.05
cutoff_sq = 1.44
damping = 0.5
step_dt = 0.05
gravity = 1.0
deposit_gain = 2.0
highest = lax.Precision.HIGHEST


def row_forces(window, flags):
    width = flags.shape[1]
    centre = window[:, 1, 1:width + 1, :]
    places = centre[0:3]
    moving = places - damping * centre[3:6]
    own_sq = jnp.sum(places * places, axis=0)
    total = jnp.zeros(places.shape, jnp.float32)
    for row_step in range(3):
        for col_step in range(3):
            other = window[:, row_step, col_step:col_step + width, :]
            offset = jnp.array([col_step - 1.0, 0.0, row_step - 1.0], jnp.float32)[:, None, None]
            other_places = other[0:3] + offset
            cross = jnp.einsum("cip,ciq->ipq", places, other_places, precision=highest)
            other_sq = jnp.sum(other_places * other_places, axis=0)
            dist_sq = own_sq[:, :, None] + other_sq[:, None, :] - 2.0 * cross
            active = flags[row_step * 3 + col_step].astype(jnp.float32)
            weight = spring * jnp.maximum(1.0 - dist_sq / cutoff_sq, 0.0) * active[:, None, None]
            pulled = jnp.einsum("ipq,ciq->cip", weight, other_places - damping * other[3:6], precision=highest)
            total = total + moving * jnp.sum(weight, axis=2)[None] - pulled
    return total


def tile_forces(extended, flags):
    count = flags.shape[1]

    def one_row(index):
        window = lax.dynamic_slice_in_dim(extended, index, 3, 1)
        row_flags = lax.dynamic_slice_in_dim(flags, index, 1, 1)[:, 0]
        return row_forces(window, row_flags)

    stacked = lax.map(one_row, jnp.arange(count, dtype=jnp.int32))
    return jnp.transpose(stacked, (1, 0, 2, 3))


def advance(state, forces):
    upward = jnp.array([0.0, 0.0, 1.0], jnp.float32)[:, None, None, None]
    speeds = state[3:6] + step_dt * forces - step_dt * gravity * upward
    places = state[0:3] + step_dt * speeds
    return jnp.concatenate([places, speeds], axis=0)


def migrate(state, exit_flags, inlet_slots):
    chans, tile_rows, tile_cols, parts = state.shape
    slabs = tile_rows // TH
    groups = tile_cols // TC
    tiles = state.reshape(chans, slabs, TH, groups, TC, parts).transpose(0, 1, 3, 2, 4, 5)
    tiles = tiles.reshape(chans, slabs, groups, TH * TC, parts)
    leaving = exit_flags.reshape(slabs, TH, groups, TC).transpose(0, 2, 1, 3).reshape(slabs, groups, TH * TC)
    ranks = (jnp.cumsum(leaving, axis=2) - 1).astype(jnp.int32)
    buffer_ids = jnp.arange(TC, dtype=jnp.int32)
    picker = ((ranks[:, :, None, :] == buffer_ids[None, None, :, None]) & (leaving[:, :, None, :] > 0)).astype(jnp.float32)
    outgoing = jnp.einsum("sgkt,csgtp->csgkp", picker, tiles, precision=highest)
    kept = tiles * (1 - leaving).astype(jnp.float32)[None, :, :, :, None]
    arrived = jnp.roll(outgoing, 1, axis=1)
    targets = inlet_slots.reshape(slabs, groups, TC)
    placing = (targets[:, :, None, :] == buffer_ids[None, None, :, None]).astype(jnp.float32)
    bottom = jnp.einsum("sgjk,csgkp->csgjp", placing, arrived, precision=highest)
    tiles = jnp.concatenate([bottom, kept[:, :, :, TC:, :]], axis=3)
    tiles = tiles.reshape(chans, slabs, groups, TH, TC, parts).transpose(0, 1, 3, 2, 4, 5)
    return tiles.reshape(chans, tile_rows, tile_cols, parts)


def deposit(state, cell_blocks, cell_slots):
    chans, tile_rows, tile_cols, parts = state.shape
    slabs = tile_rows // TH
    groups = tile_cols // TC
    lifting = deposit_gain * state[5]
    blocks = GH * GX * GY // parts

    def one_slab(index):
        lifted = lax.dynamic_slice_in_dim(lifting, index * TH, TH, 0)
        slots = lax.dynamic_slice_in_dim(cell_slots, index * TH, TH, 0)
        owners = lax.dynamic_slice_in_dim(cell_blocks, index * TH, TH, 0)
        lifted = lifted.reshape(TH, groups, TC, parts).transpose(1, 0, 2, 3).reshape(groups, TH * TC, parts)
        slots = slots.reshape(TH, groups, TC, parts).transpose(1, 0, 2, 3).reshape(groups, TH * TC, parts)
        owners = owners.reshape(TH, groups, TC).transpose(1, 0, 2).reshape(groups, TH * TC)
        table = (slots[:, :, :, None] == jnp.arange(parts, dtype=jnp.int32)[None, None, None, :]).astype(jnp.float32)
        per_tile = jnp.einsum("gtp,gtpc->gtc", lifted, table, precision=highest)
        owner_table = (jnp.arange(blocks, dtype=jnp.int32)[None, :, None] == owners[:, None, :]).astype(jnp.float32)
        grid = jnp.einsum("gbt,gtc->gbc", owner_table, per_tile, precision=highest)
        return grid.reshape(groups, GH, GX, GY).transpose(1, 0, 2, 3).reshape(GH, groups * GX, GY)

    stacked = lax.map(one_slab, jnp.arange(slabs, dtype=jnp.int32))
    return stacked.reshape(slabs * GH, groups * GX, GY)


def operate(field, diagonal):
    padded = jnp.pad(field, 1)
    beside_all = padded[2:, 1:-1, 1:-1] + padded[:-2, 1:-1, 1:-1]
    beside_all = beside_all + padded[1:-1, 2:, 1:-1] + padded[1:-1, :-2, 1:-1]
    beside_all = beside_all + padded[1:-1, 1:-1, 2:] + padded[1:-1, 1:-1, :-2]
    return (6.0 + diagonal) * field - beside_all


def solve(right_side, diagonal):
    scaling = 1.0 / (6.0 + diagonal)
    solution = jnp.zeros_like(right_side)
    residual = right_side
    precond = residual * scaling
    weighted = jnp.sum(residual * precond)
    direction = precond
    for step in range(ITERS):
        image = operate(direction, diagonal)
        alpha = weighted / jnp.sum(direction * image)
        solution = solution + alpha * direction
        residual = residual - alpha * image
        if step + 1 < ITERS:
            precond = residual * scaling
            renewed = jnp.sum(residual * precond)
            direction = precond + (renewed / weighted) * direction
            weighted = renewed
    return solution, residual


def reference(positions, velocities, contacts, exit_flags, inlet_slots, cell_blocks, cell_slots, gas_source, diagonal):
    state = jnp.concatenate([positions, velocities], axis=0)
    for repeat in range(2):
        extended = jnp.pad(state, ((0, 0), (1, 1), (1, 1), (0, 0)))
        state = advance(state, tile_forces(extended, contacts))
    settled = state
    state = migrate(settled, exit_flags, inlet_slots)
    right_side = gas_source - deposit(settled, cell_blocks, cell_slots)
    solution, residual = solve(right_side, diagonal)
    return state[0:3], state[3:6], solution, residual
```

```python
import functools
import jax
import jax.numpy as jnp
from jax import lax
from jax.experimental import pallas as pl
from jax.experimental.pallas import tpu as pltpu
from jax.sharding import PartitionSpec as P

f32, bf16, i32 = jnp.float32, jnp.bfloat16, jnp.int32
spring = 0.05
cutoff_sq = 1.44
damping = 0.5
step_dt = 0.05
gravity = 1.0
deposit_gain = 2.0
LANES = 128
COMPS = 8
DEPTH = 2
ROWS_OUT = 24


def rounded(value):
    return value.astype(bf16).astype(f32)


def rounded_pair(value):
    high = rounded(value)
    return high, rounded(value - high)


def split(value):
    high = rounded(value)
    mid = rounded(value - high)
    return high, mid, value - high - mid


def centred(tile, r, c, rows, wide):
    row = lax.broadcasted_iota(i32, (COMPS, LANES), 0)
    side = jnp.float32(c - wide // 2)
    up = (r - rows // 2).astype(f32)
    return tile + jnp.where(row == 0, side, jnp.where(row == 2, up, 0.0))


def place_parts(tile, r, c, rows, wide):
    row = lax.broadcasted_iota(i32, (COMPS, LANES), 0)
    place = jnp.where(row < 3, centred(tile, r, c, rows, wide), 0.0)
    high, mid = rounded_pair(place)
    place = high + mid
    return high, mid, -jnp.sum(place * place, axis=0, keepdims=True)


def source_features(tile, r, c, rows, wide):
    row = lax.broadcasted_iota(i32, (COMPS, LANES), 0)
    row32 = lax.broadcasted_iota(i32, (32, LANES), 0)
    high, mid, size = place_parts(tile, r, c, rows, wide)
    size_high, size_mid, size_low = split(size)
    first = jnp.where(row < 3, high, 1.0)
    first = jnp.where(row == 3, size_high, jnp.where(row == 4, size_mid, jnp.where(row == 5, size_low, first)))
    second = jnp.where(row < 3, high, jnp.where(row == 3, 1.0, 0.0))
    kind = lax.rem(r, 3) * 4 + c % 4
    kind = kind + jnp.where(kind < 4, 12, jnp.where(kind < 9, 15, 18))
    near = jnp.concatenate([first, second, mid, mid], axis=0) + jnp.where(row32 == kind, 1.0, 0.0)
    high, mid, low = split(centred(tile, r, c, rows, wide) - damping * pltpu.roll(tile, 5, 0))
    first = jnp.where(row < 3, high, jnp.where(row == 3, 1.0, 0.0))
    second = jnp.where(row < 3, mid, jnp.where(row < 4, 0.0, pltpu.roll(low, 4, 0)))
    return near, jnp.concatenate([first, second], axis=0).astype(bf16)


def target_features(tile, r, c, rows, wide):
    row = lax.broadcasted_iota(i32, (COMPS, LANES), 0)
    row32 = lax.broadcasted_iota(i32, (32, LANES), 0)
    lane32 = lax.broadcasted_iota(i32, (32, LANES), 1)
    high, mid, size = place_parts(tile, r, c, rows, wide)
    own_high, own_mid, own_low = split(cutoff_sq + size)
    first = jnp.where(row < 3, 2.0 * high, jnp.where(row < 6, 1.0, jnp.where(row == 6, own_high, own_mid)))
    second = jnp.where(row < 3, 2.0 * mid, jnp.where(row == 3, own_low, 0.0))
    third = jnp.where(row < 3, 2.0 * high, 0.0)
    fourth = jnp.where(row < 3, 2.0 * mid, 0.0)
    kind = jnp.where(row32 < 16, row32 - 12, jnp.where(row32 < 24, row32 - 15, row32 - 18))
    is_kind = ((row32 >= 12) & (row32 < 16)) | ((row32 >= 19) & (row32 < 24)) | ((row32 >= 27) & (row32 < 30))
    kind_row = jnp.where(kind < 4, 0, jnp.where(kind < 8, 1, 2))
    up = kind_row + lax.rem(4 - lax.rem(r, 3), 3)
    up = jnp.where(up > 2, up - 3, up)
    side = kind - 4 * kind_row + (5 - c % 4) % 4
    side = jnp.where(side > 3, side - 4, side)
    wanted = jnp.where(side < 3, 3 * up + side, LANES)
    flags = jnp.sum(jnp.where(lane32 == wanted, tile[6:7, :], 0.0), axis=1, keepdims=True)
    barred = jnp.where(is_kind, -1024.0 * (1.0 - flags), 0.0)
    return jnp.concatenate([first, second, third, fourth], axis=0) + barred


def forces_on(tiles, r, c, rows, wide, turned, pulled):
    features = [target_features(tile, r, c + k, rows, wide) for k, tile in enumerate(tiles)]
    target = jnp.concatenate(features, axis=1).astype(bf16)
    weights = []
    for k in range(4):
        spread = [jnp.zeros((32, 2 * LANES), bf16)] * 4
        spread[k] = target
        weights.append(jnp.concatenate(spread, axis=0))
    total = jnp.zeros((16, 2 * LANES), f32)
    for i in range(3):
        for half in range(2):
            parts = []
            pulls = []
            for j in (2 * half, 2 * half + 1):
                s = c - 1 + j
                near = jnp.dot(turned[r + i - 1, s // 4], weights[s % 4], preferred_element_type=f32)
                parts.append(jnp.maximum(near, 0.0))
                pulls.append(pulled[r + i - 1, s])
            pulls = jnp.concatenate(pulls, axis=1)
            weight = jnp.concatenate(parts, axis=0)
            high = weight.astype(bf16)
            total = total + jnp.dot(pulls, high, preferred_element_type=f32)
            low = (weight - high.astype(f32)).astype(bf16)
            total = total + jnp.dot(pulls, low, preferred_element_type=f32)
    forces = []
    for k, tile in enumerate(tiles):
        first, second = total[0:8, k * LANES : (k + 1) * LANES], total[8:16, k * LANES : (k + 1) * LANES]
        moving = centred(tile, r, c + k, rows, wide) - damping * pltpu.roll(tile, 5, 0)
        forces.append((spring / cutoff_sq) * (moving * first[3:4, :] - first - second - pltpu.roll(second, 4, 0)))
    return forces


def stepped(tile, force):
    row = lax.broadcasted_iota(i32, (COMPS, LANES), 0)
    change = step_dt * force - jnp.where(row == 2, step_dt * gravity, 0.0)
    speeds = tile + pltpu.roll(change, 3, 0)
    places = tile + step_dt * pltpu.roll(speeds, 5, 0)
    return jnp.where(row < 3, places, jnp.where(row < 6, speeds, tile))


def particles_kernel(
    where_ref, exits_ref, owners_ref, own_ref, first_ref, second_ref, slots_ref,
    sums_ref, settled_ref, leaving_ref, state, turned, pulled, begun,
    *, rows, cols,
):
    wide = cols + 2 * DEPTH
    high = rows + 2 * DEPTH
    left, right = where_ref[0], where_ref[1]
    even, below, above = where_ref[2], where_ref[3], where_ref[4]
    for r in range(rows):
        for c in range(wide):
            one, two = first_ref[r, c], second_ref[r, c]
            low = jnp.where(even > 0, two, one)
            top = jnp.where(even > 0, one, two)
            state[r, c] = jnp.where(below > 0, low, 0.0)
            state[rows + DEPTH + r, c] = jnp.where(above > 0, top, 0.0)
            state[DEPTH + r, c] = own_ref[r, c]

    def fill(source, first, last):
        def one_row(r, carry):
            for block in range(wide // 4):
                near = []
                for c in range(4 * block, 4 * block + 4):
                    places, moving = source_features(source[r, c], r, c, high, wide)
                    near.append(places)
                    pulled[r, c] = moving
                turned[r, block] = jnp.concatenate(near, axis=0).T.astype(bf16)
            return carry

        lax.fori_loop(first, last, one_row, 0)

    fill(state, 0, high)

    def first_step(r, carry):
        begun[r, 0] = jnp.zeros((COMPS, LANES), f32)
        begun[r, wide - 1] = jnp.zeros((COMPS, LANES), f32)
        for c in range(1, wide - 1, 2):
            tiles = [state[r, c], state[r, c + 1]]
            forces = forces_on(tiles, r, c, high, wide, turned, pulled)
            for k in range(2):
                inside = ((r >= DEPTH) | (below > 0)) & ((r < rows + DEPTH) | (above > 0))
                if c + k < DEPTH:
                    inside = inside & (left > 0)
                if c + k >= cols + DEPTH:
                    inside = inside & (right > 0)
                begun[r, c + k] = jnp.where(inside, stepped(tiles[k], forces[k]), 0.0)
        return carry

    lax.fori_loop(1, high - 1, first_step, 0)
    fill(begun, 1, high - 1)

    def second_step(r, carry):
        for c in range(DEPTH, DEPTH + cols, 2):
            tiles = [begun[r, c], begun[r, c + 1]]
            forces = forces_on(tiles, r, c, high, wide, turned, pulled)
            for k in range(2):
                done = stepped(tiles[k], forces[k])
                settled_ref[r - DEPTH, c + k - DEPTH] = done
                lift = deposit_gain * done[5:6, :]
                lift_high, lift_mid, lift_low = split(lift)
                row = lax.broadcasted_iota(i32, (16, LANES), 0)
                parts = jnp.where(
                    row == 0, lift_high, jnp.where(row == 1, lift_mid, jnp.where(row == 2, lift_low, 0.0))
                ).astype(bf16)
                cell = lax.broadcasted_iota(i32, (LANES, LANES), 0)
                slots = slots_ref[r - DEPTH, c + k - DEPTH : c + k - DEPTH + 1, :]
                table = jnp.where(cell == slots, 1.0, 0.0).astype(bf16)
                gathered = lax.dot_general(parts, table, (((1,), (1,)), ((), ())), preferred_element_type=f32)
                sums_ref[pl.ds((r - DEPTH) * cols + c + k - DEPTH, 1), :] = jnp.sum(gathered, axis=0, keepdims=True)
        return carry

    lax.fori_loop(DEPTH, DEPTH + rows, second_step, 0)

    lane = lax.broadcasted_iota(i32, (1, LANES), 1)
    owner_row = jnp.zeros((1, LANES), i32)
    for t in range(rows * cols):
        owner_row = jnp.where(lax.rem(lane, rows * cols) == t, owners_ref[t // cols, t % cols], owner_row)
    row = lax.broadcasted_iota(i32, (ROWS_OUT - rows * cols, LANES), 0)
    sums_ref[rows * cols :, :] = jnp.where(row == 0, owner_row.astype(f32), 0.0)

    leaving_ref[...] = jnp.zeros_like(leaving_ref)
    count = jnp.int32(0)
    for t in range(rows * cols):
        flag = exits_ref[t // cols, t % cols]

        @pl.when((flag > 0) & (count < cols))
        def _(t=t, count=count):
            leaving_ref[count] = settled_ref[t // cols, t % cols]

        count = count + flag


def particles(where, exits, owners, own, first, second, slots):
    rows, cols = slots.shape[:2]
    wide, high = cols + 2 * DEPTH, rows + 2 * DEPTH
    smem = pl.BlockSpec(memory_space=pltpu.SMEM)
    vmem = pl.BlockSpec(memory_space=pltpu.VMEM)
    return pl.pallas_call(
        functools.partial(particles_kernel, rows=rows, cols=cols),
        out_shape=(
            jax.ShapeDtypeStruct((ROWS_OUT, LANES), f32),
            jax.ShapeDtypeStruct((rows, cols, COMPS, LANES), f32),
            jax.ShapeDtypeStruct((cols, COMPS, LANES), f32),
        ),
        in_specs=[smem, smem, smem, vmem, vmem, vmem, vmem],
        out_specs=(vmem, vmem, vmem),
        scratch_shapes=[
            pltpu.VMEM((high, wide, COMPS, LANES), f32),
            pltpu.VMEM((high, wide // 4, LANES, LANES), bf16),
            pltpu.VMEM((high, wide, 16, LANES), bf16),
            pltpu.VMEM((high, wide, COMPS, LANES), f32),
        ],
        compiler_params=pltpu.CompilerParams(vmem_limit_bytes=40 * 1024 * 1024),
        name="particles",
    )(where, exits, owners, own, first, second, slots)


def matching(heights, groups, axis, odd, wrap):
    size = heights if axis == "height" else groups
    pairs = []
    for h in range(heights):
        for c in range(groups):
            i = h if axis == "height" else c
            j = i ^ 1 if not odd else (i + 1 if i % 2 else i - 1)
            if 0 <= j < size or wrap:
                j = j % size
                target = (j, c) if axis == "height" else (h, j)
            else:
                target = (h, c ^ 1) if axis == "height" else (h ^ 1, c)
            pairs.append((h * groups + c, target[0] * groups + target[1]))
    return pairs


def exchanged(value, axis, wrap):
    heights, groups = lax.axis_size("height"), lax.axis_size("cols")
    return [
        lax.ppermute(value, ("height", "cols"), matching(heights, groups, axis, odd, wrap)) for odd in (False, True)
    ]


def right_side_kernel(
    where_ref, sums_ref, side_a, side_b, height_a, height_b, gas_ref, diagonal_ref, line_a, line_b,
    corner_a, corner_b, gas_a, gas_b, rhs_ref, near_ref, far_ref, dots_ref, scaling, rhs, first, second,
    *, cols,
):
    levels, across, along = gas_ref.shape
    edge = 8
    wide = across + 2 * edge
    quarters = along // LANES
    left, right, even_c = where_ref[0], where_ref[1], where_ref[5]
    even, below, above = where_ref[2], where_ref[3], where_ref[4]

    def low_of(is_even, one, two):
        return jnp.where(is_even > 0, two, one)

    def high_of(is_even, one, two):
        return jnp.where(is_even > 0, one, two)

    for ref in (scaling, rhs):
        ref[:, 0:edge, :] = jnp.zeros((3 * levels, edge, along), f32)
        ref[:, edge + across :, :] = jnp.zeros((3 * levels, edge, along), f32)
    scaling[levels : 2 * levels, edge : edge + across] = 1.0 / (6.0 + diagonal_ref[...])
    rhs[levels : 2 * levels, edge : edge + across] = gas_ref[...]
    for level, choose, present in ((0, low_of, below), (2 * levels, high_of, above)):
        for z in range(levels):
            rhs[level + z, edge : edge + across] = choose(even, gas_a[0, z], gas_b[0, z])
            m = 1.0 / (6.0 + choose(even, gas_a[1, z], gas_b[1, z]))
            scaling[level + z, edge : edge + across] = jnp.where(present > 0, m, 0.0)

    def put_line(z, x, lines, present):
        m = jnp.where(present, 1.0 / (6.0 + lines), 0.0)
        for k in range(quarters):
            rhs[z, x : x + 1, k * LANES : (k + 1) * LANES] = lines[k : k + 1]
            scaling[z, x : x + 1, k * LANES : (k + 1) * LANES] = m[quarters + k : quarters + k + 1]

    for z in range(levels):
        for x in range(2):
            put_line(levels + z, edge - 2 + x, low_of(even_c, line_a[z, x, 8:16], line_b[z, x, 8:16]), left > 0)
            put_line(levels + z, edge + across + x, high_of(even_c, line_a[z, x, 8:16], line_b[z, x, 8:16]), right > 0)
        for level, choose, present in ((0, low_of, below), (2 * levels, high_of, above)):
            lines = [choose(even, corner_a[z, cols + 4 + x], corner_b[z, cols + 4 + x]) for x in range(2)]
            put_line(level + z, edge - 1, lines[0], (present > 0) & (left > 0))
            put_line(level + z, edge + across, lines[1], (present > 0) & (right > 0))

    lane = lax.broadcasted_iota(i32, (1, LANES), 1)
    tiles = 16
    shift_q, shift_x = quarters.bit_length() - 1, across.bit_length() - 1
    groups = []
    for name, choose, present in (("below", low_of, below), ("own", None, None), ("above", high_of, above)):
        if choose is None:
            parts = [low_of(even_c, side_a[...], side_b[...]), sums_ref[...], high_of(even_c, side_a[...], side_b[...])]
        else:
            block = [choose(even, height_a[k * ROWS_OUT : (k + 1) * ROWS_OUT], height_b[k * ROWS_OUT : (k + 1) * ROWS_OUT]) for k in range(3)]
            parts = [low_of(even_c, block[1], block[2]), block[0], high_of(even_c, block[1], block[2])]
        level = 0 if name == "below" else levels if name == "own" else 2 * levels
        code = jnp.full((1, LANES), -1, i32)
        for n, part in enumerate(parts):
            owner = part[tiles : tiles + 1].astype(i32)
            x = ((owner >> shift_q) & (across - 1)) + (edge + (n - 1) * across)
            z = owner >> (shift_q + shift_x)
            here = ((lane >> 4) == n) | ((lane >> 4) == n + 3)
            here = here & (x >= edge - 2) & (x < edge + across + 2)
            if n == 0:
                here = here & (left > 0)
            if n == 2:
                here = here & (right > 0)
            if present is not None:
                here = here & (present > 0)
            code = jnp.where(here, (z * wide + x) * quarters + (owner & (quarters - 1)), code)
        values = jnp.concatenate([part[0:tiles] for part in parts], axis=0)
        high = values.astype(bf16)
        low = (values - high.astype(f32)).astype(bf16)
        values = jnp.concatenate([high, low, jnp.zeros((LANES - 6 * tiles, LANES), bf16)], axis=0)
        spot = lax.broadcasted_iota(i32, (levels * wide, LANES), 0) * quarters
        for k in range(quarters):
            table = jnp.where(code == spot + k, 1.0, 0.0).astype(bf16)
            added = jnp.dot(table, values, preferred_element_type=f32)
            for z in range(levels):
                rhs[level + z, :, k * LANES : (k + 1) * LANES] -= added[z * wide : (z + 1) * wide]

    for z in range(3 * levels):
        first[z] = scaling[z] * rhs[z]
    place = lax.broadcasted_iota(i32, (wide, along), 1)

    def beside(ref, z):
        mid = ref[z]
        total = ref[z - 1] + ref[z + 1] + pltpu.roll(mid, 1, 0) + pltpu.roll(mid, wide - 1, 0)
        total = total + jnp.where(place > 0, pltpu.roll(mid, 1, 1), 0.0)
        return total + jnp.where(place < along - 1, pltpu.roll(mid, along - 1, 1), 0.0)

    dots = [jnp.zeros((8, LANES), f32)] * 4

    def folded(value):
        value = jnp.sum(value.reshape(across // 8, 8, along), axis=0)
        return sum(value[:, k * LANES : (k + 1) * LANES] for k in range(quarters))

    inner = slice(edge, edge + across)
    for z in range(levels - 1, 2 * levels + 1):
        near = beside(first, z)
        second[z] = scaling[z] * near
        if levels <= z < 2 * levels:
            near = near[inner]
            near_ref[z - levels] = near
            rhs_ref[z - levels] = rhs[z, inner]
            z0 = first[z, inner]
            dots[0] = dots[0] + folded(z0 * rhs[z, inner])
            dots[1] = dots[1] + folded(z0 * near)
            dots[2] = dots[2] + folded(second[z, inner] * near)
    for z in range(levels, 2 * levels):
        far = beside(second, z)[inner]
        far_ref[z - levels] = far
        dots[3] = dots[3] + folded(second[z, inner] * far)
    row = lax.broadcasted_iota(i32, (8, LANES), 0)
    lane8 = lax.broadcasted_iota(i32, (8, LANES), 1)
    line = jnp.zeros((1, LANES), f32)
    for k in range(4):
        total = jnp.sum(jnp.sum(dots[k], axis=0, keepdims=True), axis=1, keepdims=True)
        line = jnp.where(lane == k, total, line)
    dots_ref[...] = jnp.broadcast_to(line, dots_ref.shape)


def right_side_of(where, sums, side, height, gas, diagonal, lines, corners, gases, devices, cols):
    levels, across, along = gas.shape
    smem = pl.BlockSpec(memory_space=pltpu.SMEM)
    vmem = pl.BlockSpec(memory_space=pltpu.VMEM)
    whole = pltpu.VMEM((3 * levels, across + 16, along), f32)
    return pl.pallas_call(
        functools.partial(right_side_kernel, cols=cols),
        out_shape=(jax.ShapeDtypeStruct(gas.shape, f32),) * 3 + (jax.ShapeDtypeStruct((devices, LANES), f32),),
        in_specs=[smem] + [vmem] * 13,
        out_specs=(vmem,) * 4,
        scratch_shapes=[whole] * 4,
        compiler_params=pltpu.CompilerParams(vmem_limit_bytes=40 * 1024 * 1024),
        name="right_side",
    )(where, sums, *side, *height, gas, diagonal, *lines, *corners, *gases)


def results_kernel(
    where_ref, exits_ref, inlets_ref, dots_ref, rhs_ref, near_ref, far_ref, diagonal_ref, settled_ref,
    height_a, height_b, positions_ref, velocities_ref, pressure_ref, residual_ref,
):
    rows, cols = settled_ref.shape[:2]
    even = where_ref[2]
    totals = jnp.sum(dots_ref[...], axis=0, keepdims=True)
    g00, g01, g11, g12 = [totals[:, k : k + 1] for k in range(4)]
    ratio = g01 / g00
    alpha = g00 / (g00 - g01)
    square = alpha * alpha
    renewed = square * (g11 - ratio * g01)
    beta = renewed / g00
    crossed = square * (ratio * ratio * g01 - 2.0 * ratio * g11 + g12)
    curvature = renewed - crossed - beta * renewed / alpha
    later = renewed / curvature
    one = alpha + later * (1.0 - alpha + beta)
    two = later * alpha
    for z in range(rhs_ref.shape[0]):
        m = 1.0 / (6.0 + diagonal_ref[z])
        rhs, near = rhs_ref[z], near_ref[z]
        pressure_ref[z] = m * (one * rhs + two * near)
        residual_ref[z] = (1.0 - one) * rhs + (one - two) * near + two * far_ref[z]
    for r in range(rows):
        for c in range(cols):
            kept = jnp.where(exits_ref[r, c] > 0, 0.0, settled_ref[r, c])
            if r > 0:
                for d in range(3):
                    positions_ref[d, r, c : c + 1] = kept[d : d + 1]
                    velocities_ref[d, r, c : c + 1] = kept[d + 3 : d + 4]
    start = 3 * ROWS_OUT
    for k in range(cols):
        slot = slice(start + k * COMPS, start + (k + 1) * COMPS)
        tile = jnp.where(even > 0, height_b[slot], height_a[slot])
        c = inlets_ref[0, k]
        for d in range(3):
            positions_ref[d, 0, pl.ds(c, 1)] = tile[d : d + 1]
            velocities_ref[d, 0, pl.ds(c, 1)] = tile[d + 3 : d + 4]


def results_of(where, exits, inlets, dots, rhs, near, far, diagonal, settled, height):
    rows, cols = settled.shape[:2]
    smem = pl.BlockSpec(memory_space=pltpu.SMEM)
    vmem = pl.BlockSpec(memory_space=pltpu.VMEM)
    particle = jax.ShapeDtypeStruct((3, rows, cols, LANES), f32)
    cells = jax.ShapeDtypeStruct(rhs.shape, f32)
    return pl.pallas_call(
        results_kernel,
        out_shape=(particle, particle, cells, cells),
        in_specs=[smem] * 3 + [vmem] * 8,
        out_specs=(vmem,) * 4,
        compiler_params=pltpu.CompilerParams(vmem_limit_bytes=40 * 1024 * 1024),
        name="results",
    )(where, exits, inlets, dots, rhs, near, far, diagonal, settled, *height)


def on_device(
    positions, velocities, contacts, exit_flags, inlet_slots, cell_blocks, cell_slots, gas_source, diagonal
):
    heights, groups = lax.axis_size("height"), lax.axis_size("cols")
    h, c = lax.axis_index("height"), lax.axis_index("cols")
    rows, cols = positions.shape[1:3]
    levels, across, along = gas_source.shape
    where = jnp.stack([c > 0, c < groups - 1, h % 2 == 0, h > 0, h < heights - 1, c % 2 == 0, c < 0, c < 0])
    where = where.astype(jnp.int32)
    flags = jnp.pad(contacts.astype(f32).transpose(1, 2, 0), ((0, 0), (0, 0), (0, LANES - contacts.shape[0])))
    tiles = jnp.concatenate(
        [
            positions.transpose(1, 2, 0, 3),
            velocities.transpose(1, 2, 0, 3),
            flags[:, :, None, :],
            jnp.zeros((rows, cols, 1, LANES), f32),
        ],
        axis=2,
    )

    def edge_lines(lines):
        return lines.reshape(levels, 2, along // LANES, LANES)

    def side(first, last):
        cells = slice(0, 2) if first else slice(across - 2, across)
        return jnp.concatenate(
            [
                tiles[:, :DEPTH] if first else tiles[:, cols - DEPTH :],
                edge_lines(gas_source[:, cells]),
                edge_lines(diagonal[:, cells]),
            ],
            axis=2,
        )

    at_left, at_right = side(True, False), side(False, True)
    even = c % 2 == 0
    shared = [jnp.where(even, at_right, at_left), jnp.where(even, at_left, at_right)]
    lines = [
        lax.ppermute(value, ("height", "cols"), matching(heights, groups, "cols", odd, True))
        for value, odd in zip(shared, (False, True))
    ]
    low = jnp.where(c > 0, jnp.where(even, lines[1], lines[0]), 0.0)
    high = jnp.where(c < groups - 1, jnp.where(even, lines[0], lines[1]), 0.0)
    window = jnp.concatenate(
        [low[:, :, :COMPS], tiles, high[:, :, :COMPS], low[:, 1:2, COMPS:], high[:, 0:1, COMPS:]], axis=1
    )
    beside = exchanged(window, "height", False)
    gases = exchanged(jnp.stack([gas_source, diagonal]), "height", False)
    sums, settled, leaving = particles(where, exit_flags, cell_blocks, window, *beside, cell_slots)
    sides = exchanged(sums, "cols", True)
    parcel = jnp.concatenate([sums, *sides, leaving.reshape(cols * COMPS, LANES)], axis=0)
    parcels = exchanged(parcel, "height", True)
    rhs, near, far, dots = right_side_of(
        where, sums, sides, parcels, gas_source, diagonal, lines, beside, gases, heights * groups, cols
    )
    dots = lax.all_to_all(dots, ("height", "cols"), 0, 0, tiled=True)
    return results_of(where, exit_flags, inlet_slots, dots, rhs, near, far, diagonal, settled, parcels)


def solution(mesh):
    in_specs = (
        P(None, "height", "cols", None),
        P(None, "height", "cols", None),
        P(None, "height", "cols"),
        P("height", "cols"),
        P("height", "cols"),
        P("height", "cols"),
        P("height", "cols", None),
        P("height", "cols", None),
        P("height", "cols", None),
    )
    out_specs = (
        P(None, "height", "cols", None),
        P(None, "height", "cols", None),
        P("height", "cols", None),
        P("height", "cols", None),
    )
    return jax.shard_map(
        on_device, mesh=mesh, in_specs=in_specs, out_specs=out_specs, check_vma=False
    )
```

```python
import functools
import jax
import jax.numpy as jnp
from jax import lax
from jax.experimental import pallas as pl
from jax.experimental.pallas import tpu as pltpu
from jax.sharding import PartitionSpec as P

f32, bf16, i32 = jnp.float32, jnp.bfloat16, jnp.int32
spring = 0.05
cutoff_sq = 1.44
damping = 0.5
step_dt = 0.05
gravity = 1.0
deposit_gain = 2.0
LANES = 128
COMPS = 8
DEPTH = 2
ROWS_OUT = 24


def rounded(value):
    return value.astype(bf16).astype(f32)


def rounded_pair(value):
    high = rounded(value)
    return high, rounded(value - high)


def split(value):
    high = rounded(value)
    mid = rounded(value - high)
    return high, mid, value - high - mid


def centred(tile, r, c, rows, wide):
    row = lax.broadcasted_iota(i32, (COMPS, LANES), 0)
    side = jnp.float32(c - wide // 2)
    up = (r - rows // 2).astype(f32)
    return tile + jnp.where(row == 0, side, jnp.where(row == 2, up, 0.0))


def place_parts(tile, r, c, rows, wide):
    row = lax.broadcasted_iota(i32, (COMPS, LANES), 0)
    place = jnp.where(row < 3, centred(tile, r, c, rows, wide), 0.0)
    high, mid = rounded_pair(place)
    place = high + mid
    return high, mid, -jnp.sum(place * place, axis=0, keepdims=True)


def source_features(tile, r, c, rows, wide):
    row = lax.broadcasted_iota(i32, (COMPS, LANES), 0)
    row32 = lax.broadcasted_iota(i32, (32, LANES), 0)
    high, mid, size = place_parts(tile, r, c, rows, wide)
    size_high, size_mid, size_low = split(size)
    first = jnp.where(row < 3, high, 1.0)
    first = jnp.where(row == 3, size_high, jnp.where(row == 4, size_mid, jnp.where(row == 5, size_low, first)))
    second = jnp.where(row < 3, high, jnp.where(row == 3, 1.0, 0.0))
    kind = lax.rem(r, 3) * 4 + c % 4
    kind = kind + jnp.where(kind < 4, 12, jnp.where(kind < 9, 15, 18))
    near = jnp.concatenate([first, second, mid, mid], axis=0) + jnp.where(row32 == kind, 1.0, 0.0)
    high, mid, low = split(centred(tile, r, c, rows, wide) - damping * pltpu.roll(tile, 5, 0))
    first = jnp.where(row < 3, high, jnp.where(row == 3, 1.0, 0.0))
    second = jnp.where(row < 3, mid, jnp.where(row < 4, 0.0, pltpu.roll(low, 4, 0)))
    return near, jnp.concatenate([first, second], axis=0).astype(bf16)


def target_features(tile, r, c, rows, wide):
    row = lax.broadcasted_iota(i32, (COMPS, LANES), 0)
    row32 = lax.broadcasted_iota(i32, (32, LANES), 0)
    lane32 = lax.broadcasted_iota(i32, (32, LANES), 1)
    high, mid, size = place_parts(tile, r, c, rows, wide)
    own_high, own_mid, own_low = split(cutoff_sq + size)
    first = jnp.where(row < 3, 2.0 * high, jnp.where(row < 6, 1.0, jnp.where(row == 6, own_high, own_mid)))
    second = jnp.where(row < 3, 2.0 * mid, jnp.where(row == 3, own_low, 0.0))
    third = jnp.where(row < 3, 2.0 * high, 0.0)
    fourth = jnp.where(row < 3, 2.0 * mid, 0.0)
    kind = jnp.where(row32 < 16, row32 - 12, jnp.where(row32 < 24, row32 - 15, row32 - 18))
    is_kind = ((row32 >= 12) & (row32 < 16)) | ((row32 >= 19) & (row32 < 24)) | ((row32 >= 27) & (row32 < 30))
    kind_row = jnp.where(kind < 4, 0, jnp.where(kind < 8, 1, 2))
    up = kind_row + lax.rem(4 - lax.rem(r, 3), 3)
    up = jnp.where(up > 2, up - 3, up)
    side = kind - 4 * kind_row + (5 - c % 4) % 4
    side = jnp.where(side > 3, side - 4, side)
    wanted = jnp.where(side < 3, 3 * up + side, LANES)
    flags = jnp.sum(jnp.where(lane32 == wanted, tile[6:7, :], 0.0), axis=1, keepdims=True)
    barred = jnp.where(is_kind, -1024.0 * (1.0 - flags), 0.0)
    return jnp.concatenate([first, second, third, fourth], axis=0) + barred


def forces_on(tiles, r, c, rows, wide, turned, pulled):
    features = [target_features(tile, r, c + k, rows, wide) for k, tile in enumerate(tiles)]
    target = jnp.concatenate(features, axis=1).astype(bf16)
    weights = []
    for k in range(4):
        spread = [jnp.zeros((32, 2 * LANES), bf16)] * 4
        spread[k] = target
        weights.append(jnp.concatenate(spread, axis=0))
    total = jnp.zeros((16, 2 * LANES), f32)
    for i in range(3):
        for j in range(4):
            s = c - 1 + j
            near = jnp.dot(turned[r + i - 1, s // 4], weights[s % 4], preferred_element_type=f32)
            weight = jnp.maximum(near, 0.0)
            pulls = pulled[r + i - 1, s]
            high = weight.astype(bf16)
            total = total + jnp.dot(pulls, high, preferred_element_type=f32)
            low = (weight - high.astype(f32)).astype(bf16)
            total = total + jnp.dot(pulls, low, preferred_element_type=f32)
    forces = []
    for k, tile in enumerate(tiles):
        first, second = total[0:8, k * LANES : (k + 1) * LANES], total[8:16, k * LANES : (k + 1) * LANES]
        moving = centred(tile, r, c + k, rows, wide) - damping * pltpu.roll(tile, 5, 0)
        forces.append((spring / cutoff_sq) * (moving * first[3:4, :] - first - second - pltpu.roll(second, 4, 0)))
    return forces


def stepped(tile, force):
    row = lax.broadcasted_iota(i32, (COMPS, LANES), 0)
    change = step_dt * force - jnp.where(row == 2, step_dt * gravity, 0.0)
    speeds = tile + pltpu.roll(change, 3, 0)
    places = tile + step_dt * pltpu.roll(speeds, 5, 0)
    return jnp.where(row < 3, places, jnp.where(row < 6, speeds, tile))


def particles_kernel(
    where_ref, exits_ref, owners_ref, own_ref, first_ref, second_ref, slots_ref,
    sums_ref, settled_ref, leaving_ref, state, turned, pulled, begun,
    *, rows, cols,
):
    wide = cols + 2 * DEPTH
    high = rows + 2 * DEPTH
    left, right = where_ref[0], where_ref[1]
    even, below, above = where_ref[2], where_ref[3], where_ref[4]
    for r in range(rows):
        for c in range(wide):
            one, two = first_ref[r, c], second_ref[r, c]
            low = jnp.where(even > 0, two, one)
            top = jnp.where(even > 0, one, two)
            state[r, c] = jnp.where(below > 0, low, 0.0)
            state[rows + DEPTH + r, c] = jnp.where(above > 0, top, 0.0)
            state[DEPTH + r, c] = own_ref[r, c]

    def fill(source, first, last):
        def one_row(r, carry):
            for block in range(wide // 4):
                near = []
                for c in range(4 * block, 4 * block + 4):
                    places, moving = source_features(source[r, c], r, c, high, wide)
                    near.append(places)
                    pulled[r, c] = moving
                turned[r, block] = jnp.concatenate(near, axis=0).T.astype(bf16)
            return carry

        lax.fori_loop(first, last, one_row, 0)

    fill(state, 0, high)

    def first_step(r, carry):
        begun[r, 0] = jnp.zeros((COMPS, LANES), f32)
        begun[r, wide - 1] = jnp.zeros((COMPS, LANES), f32)
        for c in range(1, wide - 1, 2):
            tiles = [state[r, c], state[r, c + 1]]
            forces = forces_on(tiles, r, c, high, wide, turned, pulled)
            for k in range(2):
                inside = ((r >= DEPTH) | (below > 0)) & ((r < rows + DEPTH) | (above > 0))
                if c + k < DEPTH:
                    inside = inside & (left > 0)
                if c + k >= cols + DEPTH:
                    inside = inside & (right > 0)
                begun[r, c + k] = jnp.where(inside, stepped(tiles[k], forces[k]), 0.0)
        return carry

    lax.fori_loop(1, high - 1, first_step, 0)
    fill(begun, 1, high - 1)

    def second_step(r, carry):
        for c in range(DEPTH, DEPTH + cols, 2):
            tiles = [begun[r, c], begun[r, c + 1]]
            forces = forces_on(tiles, r, c, high, wide, turned, pulled)
            for k in range(2):
                done = stepped(tiles[k], forces[k])
                settled_ref[r - DEPTH, c + k - DEPTH] = done
        return carry

    lax.fori_loop(DEPTH, DEPTH + rows, second_step, 0)

    def deposit(r, carry):
        row = lax.broadcasted_iota(i32, (16, LANES), 0)
        cell = lax.broadcasted_iota(i32, (LANES, LANES), 0)
        for c in range(cols):
            lift_high, lift_mid, lift_low = split(deposit_gain * settled_ref[r, c, 5:6, :])
            parts = jnp.where(row == 0, lift_high, jnp.where(row == 1, lift_mid, jnp.where(row == 2, lift_low, 0.0)))
            table = jnp.where(cell == slots_ref[r, c : c + 1, :], 1.0, 0.0).astype(bf16)
            gathered = lax.dot_general(
                parts.astype(bf16), table, (((1,), (1,)), ((), ())), preferred_element_type=f32
            )
            sums_ref[pl.ds(r * cols + c, 1), :] = jnp.sum(gathered, axis=0, keepdims=True)
        return carry

    lax.fori_loop(0, rows, deposit, 0)

    lane = lax.broadcasted_iota(i32, (1, LANES), 1)
    owner_row = jnp.zeros((1, LANES), i32)
    for t in range(rows * cols):
        owner_row = jnp.where(lax.rem(lane, rows * cols) == t, owners_ref[t // cols, t % cols], owner_row)
    row = lax.broadcasted_iota(i32, (ROWS_OUT - rows * cols, LANES), 0)
    sums_ref[rows * cols :, :] = jnp.where(row == 0, owner_row.astype(f32), 0.0)

    leaving_ref[...] = jnp.zeros_like(leaving_ref)
    count = jnp.int32(0)
    for t in range(rows * cols):
        flag = exits_ref[t // cols, t % cols]

        @pl.when((flag > 0) & (count < cols))
        def _(t=t, count=count):
            leaving_ref[count] = settled_ref[t // cols, t % cols]

        count = count + flag


def particles(where, exits, owners, own, first, second, slots):
    rows, cols = slots.shape[:2]
    wide, high = cols + 2 * DEPTH, rows + 2 * DEPTH
    smem = pl.BlockSpec(memory_space=pltpu.SMEM)
    vmem = pl.BlockSpec(memory_space=pltpu.VMEM)
    return pl.pallas_call(
        functools.partial(particles_kernel, rows=rows, cols=cols),
        out_shape=(
            jax.ShapeDtypeStruct((ROWS_OUT, LANES), f32),
            jax.ShapeDtypeStruct((rows, cols, COMPS, LANES), f32),
            jax.ShapeDtypeStruct((cols, COMPS, LANES), f32),
        ),
        in_specs=[smem, smem, smem, vmem, vmem, vmem, vmem],
        out_specs=(vmem, vmem, vmem),
        scratch_shapes=[
            pltpu.VMEM((high, wide, COMPS, LANES), f32),
            pltpu.VMEM((high, wide // 4, LANES, LANES), bf16),
            pltpu.VMEM((high, wide, 16, LANES), bf16),
            pltpu.VMEM((high, wide, COMPS, LANES), f32),
        ],
        compiler_params=pltpu.CompilerParams(vmem_limit_bytes=40 * 1024 * 1024),
        name="particles",
    )(where, exits, owners, own, first, second, slots)


def matching(heights, groups, axis, odd, wrap):
    size = heights if axis == "height" else groups
    pairs = []
    for h in range(heights):
        for c in range(groups):
            i = h if axis == "height" else c
            j = i ^ 1 if not odd else (i + 1 if i % 2 else i - 1)
            if 0 <= j < size or wrap:
                j = j % size
                target = (j, c) if axis == "height" else (h, j)
            else:
                target = (h, c ^ 1) if axis == "height" else (h ^ 1, c)
            pairs.append((h * groups + c, target[0] * groups + target[1]))
    return pairs


def exchanged(value, axis, wrap):
    heights, groups = lax.axis_size("height"), lax.axis_size("cols")
    return [
        lax.ppermute(value, ("height", "cols"), matching(heights, groups, axis, odd, wrap)) for odd in (False, True)
    ]


def right_side_kernel(
    where_ref, sums_ref, side_a, side_b, height_a, height_b, gas_ref, diagonal_ref, line_a, line_b,
    corner_a, corner_b, gas_a, gas_b, rhs_ref, near_ref, far_ref, dots_ref, scaling, rhs, first, second,
    *, cols,
):
    levels, across, along = gas_ref.shape
    edge = 8
    wide = across + 2 * edge
    quarters = along // LANES
    left, right, even_c = where_ref[0], where_ref[1], where_ref[5]
    even, below, above = where_ref[2], where_ref[3], where_ref[4]

    def low_of(is_even, one, two):
        return jnp.where(is_even > 0, two, one)

    def high_of(is_even, one, two):
        return jnp.where(is_even > 0, one, two)

    for ref in (scaling, rhs):
        ref[:, 0:edge, :] = jnp.zeros((3 * levels, edge, along), f32)
        ref[:, edge + across :, :] = jnp.zeros((3 * levels, edge, along), f32)
    scaling[levels : 2 * levels, edge : edge + across] = 1.0 / (6.0 + diagonal_ref[...])
    rhs[levels : 2 * levels, edge : edge + across] = gas_ref[...]
    for level, choose, present in ((0, low_of, below), (2 * levels, high_of, above)):
        for z in range(levels):
            rhs[level + z, edge : edge + across] = choose(even, gas_a[0, z], gas_b[0, z])
            m = 1.0 / (6.0 + choose(even, gas_a[1, z], gas_b[1, z]))
            scaling[level + z, edge : edge + across] = jnp.where(present > 0, m, 0.0)

    def put_line(z, x, lines, present):
        m = jnp.where(present, 1.0 / (6.0 + lines), 0.0)
        for k in range(quarters):
            rhs[z, x : x + 1, k * LANES : (k + 1) * LANES] = lines[k : k + 1]
            scaling[z, x : x + 1, k * LANES : (k + 1) * LANES] = m[quarters + k : quarters + k + 1]

    for z in range(levels):
        for x in range(2):
            put_line(levels + z, edge - 2 + x, low_of(even_c, line_a[z, x, 8:16], line_b[z, x, 8:16]), left > 0)
            put_line(levels + z, edge + across + x, high_of(even_c, line_a[z, x, 8:16], line_b[z, x, 8:16]), right > 0)
        for level, choose, present in ((0, low_of, below), (2 * levels, high_of, above)):
            lines = [choose(even, corner_a[z, cols + 4 + x], corner_b[z, cols + 4 + x]) for x in range(2)]
            put_line(level + z, edge - 1, lines[0], (present > 0) & (left > 0))
            put_line(level + z, edge + across, lines[1], (present > 0) & (right > 0))

    lane = lax.broadcasted_iota(i32, (1, LANES), 1)
    tiles = 16
    shift_q, shift_x = quarters.bit_length() - 1, across.bit_length() - 1
    groups = []
    for name, choose, present in (("below", low_of, below), ("own", None, None), ("above", high_of, above)):
        if choose is None:
            parts = [low_of(even_c, side_a[...], side_b[...]), sums_ref[...], high_of(even_c, side_a[...], side_b[...])]
        else:
            block = [choose(even, height_a[k * ROWS_OUT : (k + 1) * ROWS_OUT], height_b[k * ROWS_OUT : (k + 1) * ROWS_OUT]) for k in range(3)]
            parts = [low_of(even_c, block[1], block[2]), block[0], high_of(even_c, block[1], block[2])]
        level = 0 if name == "below" else levels if name == "own" else 2 * levels
        code = jnp.full((1, LANES), -1, i32)
        for n, part in enumerate(parts):
            owner = part[tiles : tiles + 1].astype(i32)
            x = ((owner >> shift_q) & (across - 1)) + (edge + (n - 1) * across)
            z = owner >> (shift_q + shift_x)
            here = ((lane >> 4) == n) | ((lane >> 4) == n + 3)
            here = here & (x >= edge - 2) & (x < edge + across + 2)
            if n == 0:
                here = here & (left > 0)
            if n == 2:
                here = here & (right > 0)
            if present is not None:
                here = here & (present > 0)
            code = jnp.where(here, (z * wide + x) * quarters + (owner & (quarters - 1)), code)
        values = jnp.concatenate([part[0:tiles] for part in parts], axis=0)
        high = values.astype(bf16)
        low = (values - high.astype(f32)).astype(bf16)
        values = jnp.concatenate([high, low, jnp.zeros((LANES - 6 * tiles, LANES), bf16)], axis=0)
        spot = lax.broadcasted_iota(i32, (levels * wide, LANES), 0) * quarters
        for k in range(quarters):
            table = jnp.where(code == spot + k, 1.0, 0.0).astype(bf16)
            added = jnp.dot(table, values, preferred_element_type=f32)
            for z in range(levels):
                rhs[level + z, :, k * LANES : (k + 1) * LANES] -= added[z * wide : (z + 1) * wide]

    for z in range(3 * levels):
        first[z] = scaling[z] * rhs[z]
    place = lax.broadcasted_iota(i32, (wide, along), 1)

    def beside(ref, z):
        mid = ref[z]
        total = ref[z - 1] + ref[z + 1] + pltpu.roll(mid, 1, 0) + pltpu.roll(mid, wide - 1, 0)
        total = total + jnp.where(place > 0, pltpu.roll(mid, 1, 1), 0.0)
        return total + jnp.where(place < along - 1, pltpu.roll(mid, along - 1, 1), 0.0)

    dots = [jnp.zeros((8, LANES), f32)] * 4

    def folded(value):
        value = jnp.sum(value.reshape(across // 8, 8, along), axis=0)
        return sum(value[:, k * LANES : (k + 1) * LANES] for k in range(quarters))

    inner = slice(edge, edge + across)
    for z in range(levels - 1, 2 * levels + 1):
        near = beside(first, z)
        second[z] = scaling[z] * near
        if levels <= z < 2 * levels:
            near = near[inner]
            near_ref[z - levels] = near
            rhs_ref[z - levels] = rhs[z, inner]
            z0 = first[z, inner]
            dots[0] = dots[0] + folded(z0 * rhs[z, inner])
            dots[1] = dots[1] + folded(z0 * near)
            dots[2] = dots[2] + folded(second[z, inner] * near)
    for z in range(levels, 2 * levels):
        far = beside(second, z)[inner]
        far_ref[z - levels] = far
        dots[3] = dots[3] + folded(second[z, inner] * far)
    row = lax.broadcasted_iota(i32, (8, LANES), 0)
    lane8 = lax.broadcasted_iota(i32, (8, LANES), 1)
    line = jnp.zeros((1, LANES), f32)
    for k in range(4):
        total = jnp.sum(jnp.sum(dots[k], axis=0, keepdims=True), axis=1, keepdims=True)
        line = jnp.where(lane == k, total, line)
    dots_ref[...] = jnp.broadcast_to(line, dots_ref.shape)


def right_side_of(where, sums, side, height, gas, diagonal, lines, corners, gases, devices, cols):
    levels, across, along = gas.shape
    smem = pl.BlockSpec(memory_space=pltpu.SMEM)
    vmem = pl.BlockSpec(memory_space=pltpu.VMEM)
    whole = pltpu.VMEM((3 * levels, across + 16, along), f32)
    return pl.pallas_call(
        functools.partial(right_side_kernel, cols=cols),
        out_shape=(jax.ShapeDtypeStruct(gas.shape, f32),) * 3 + (jax.ShapeDtypeStruct((devices, LANES), f32),),
        in_specs=[smem] + [vmem] * 13,
        out_specs=(vmem,) * 4,
        scratch_shapes=[whole] * 4,
        compiler_params=pltpu.CompilerParams(vmem_limit_bytes=40 * 1024 * 1024),
        name="right_side",
    )(where, sums, *side, *height, gas, diagonal, *lines, *corners, *gases)


def results_kernel(
    where_ref, exits_ref, inlets_ref, dots_ref, rhs_ref, near_ref, far_ref, diagonal_ref, settled_ref,
    height_a, height_b, positions_ref, velocities_ref, pressure_ref, residual_ref,
):
    rows, cols = settled_ref.shape[:2]
    even = where_ref[2]
    totals = jnp.sum(dots_ref[...], axis=0, keepdims=True)
    g00, g01, g11, g12 = [totals[:, k : k + 1] for k in range(4)]
    ratio = g01 / g00
    alpha = g00 / (g00 - g01)
    square = alpha * alpha
    renewed = square * (g11 - ratio * g01)
    beta = renewed / g00
    crossed = square * (ratio * ratio * g01 - 2.0 * ratio * g11 + g12)
    curvature = renewed - crossed - beta * renewed / alpha
    later = renewed / curvature
    one = alpha + later * (1.0 - alpha + beta)
    two = later * alpha
    for z in range(rhs_ref.shape[0]):
        m = 1.0 / (6.0 + diagonal_ref[z])
        rhs, near = rhs_ref[z], near_ref[z]
        pressure_ref[z] = m * (one * rhs + two * near)
        residual_ref[z] = (1.0 - one) * rhs + (one - two) * near + two * far_ref[z]
    for r in range(rows):
        for c in range(cols):
            kept = jnp.where(exits_ref[r, c] > 0, 0.0, settled_ref[r, c])
            if r > 0:
                for d in range(3):
                    positions_ref[d, r, c : c + 1] = kept[d : d + 1]
                    velocities_ref[d, r, c : c + 1] = kept[d + 3 : d + 4]
    start = 3 * ROWS_OUT
    for k in range(cols):
        slot = slice(start + k * COMPS, start + (k + 1) * COMPS)
        tile = jnp.where(even > 0, height_b[slot], height_a[slot])
        c = inlets_ref[0, k]
        for d in range(3):
            positions_ref[d, 0, pl.ds(c, 1)] = tile[d : d + 1]
            velocities_ref[d, 0, pl.ds(c, 1)] = tile[d + 3 : d + 4]


def results_of(where, exits, inlets, dots, rhs, near, far, diagonal, settled, height):
    rows, cols = settled.shape[:2]
    smem = pl.BlockSpec(memory_space=pltpu.SMEM)
    vmem = pl.BlockSpec(memory_space=pltpu.VMEM)
    particle = jax.ShapeDtypeStruct((3, rows, cols, LANES), f32)
    cells = jax.ShapeDtypeStruct(rhs.shape, f32)
    return pl.pallas_call(
        results_kernel,
        out_shape=(particle, particle, cells, cells),
        in_specs=[smem] * 3 + [vmem] * 8,
        out_specs=(vmem,) * 4,
        compiler_params=pltpu.CompilerParams(vmem_limit_bytes=40 * 1024 * 1024),
        name="results",
    )(where, exits, inlets, dots, rhs, near, far, diagonal, settled, *height)


def on_device(
    positions, velocities, contacts, exit_flags, inlet_slots, cell_blocks, cell_slots, gas_source, diagonal
):
    heights, groups = lax.axis_size("height"), lax.axis_size("cols")
    h, c = lax.axis_index("height"), lax.axis_index("cols")
    rows, cols = positions.shape[1:3]
    levels, across, along = gas_source.shape
    where = jnp.stack([c > 0, c < groups - 1, h % 2 == 0, h > 0, h < heights - 1, c % 2 == 0, c < 0, c < 0])
    where = where.astype(jnp.int32)
    flags = jnp.pad(contacts.astype(f32).transpose(1, 2, 0), ((0, 0), (0, 0), (0, LANES - contacts.shape[0])))
    tiles = jnp.concatenate(
        [
            positions.transpose(1, 2, 0, 3),
            velocities.transpose(1, 2, 0, 3),
            flags[:, :, None, :],
            jnp.zeros((rows, cols, 1, LANES), f32),
        ],
        axis=2,
    )

    def edge_lines(lines):
        return lines.reshape(levels, 2, along // LANES, LANES)

    def side(first, last):
        cells = slice(0, 2) if first else slice(across - 2, across)
        return jnp.concatenate(
            [
                tiles[:, :DEPTH] if first else tiles[:, cols - DEPTH :],
                edge_lines(gas_source[:, cells]),
                edge_lines(diagonal[:, cells]),
            ],
            axis=2,
        )

    at_left, at_right = side(True, False), side(False, True)
    even = c % 2 == 0
    shared = [jnp.where(even, at_right, at_left), jnp.where(even, at_left, at_right)]
    lines = [
        lax.ppermute(value, ("height", "cols"), matching(heights, groups, "cols", odd, True))
        for value, odd in zip(shared, (False, True))
    ]
    low = jnp.where(c > 0, jnp.where(even, lines[1], lines[0]), 0.0)
    high = jnp.where(c < groups - 1, jnp.where(even, lines[0], lines[1]), 0.0)
    window = jnp.concatenate(
        [low[:, :, :COMPS], tiles, high[:, :, :COMPS], low[:, 1:2, COMPS:], high[:, 0:1, COMPS:]], axis=1
    )
    beside = exchanged(window, "height", False)
    cells, beside = lax.optimization_barrier((jnp.stack([gas_source, diagonal]), beside))
    gases = exchanged(cells, "height", False)
    sums, settled, leaving = particles(where, exit_flags, cell_blocks, window, *beside, cell_slots)
    sides = exchanged(sums, "cols", True)
    parcel = jnp.concatenate([sums, *sides, leaving.reshape(cols * COMPS, LANES)], axis=0)
    parcels = exchanged(parcel, "height", True)
    rhs, near, far, dots = right_side_of(
        where, sums, sides, parcels, gas_source, diagonal, lines, beside, gases, heights * groups, cols
    )
    dots = lax.all_to_all(dots, ("height", "cols"), 0, 0, tiled=True)
    return results_of(where, exit_flags, inlet_slots, dots, rhs, near, far, diagonal, settled, parcels)


def solution(mesh):
    in_specs = (
        P(None, "height", "cols", None),
        P(None, "height", "cols", None),
        P(None, "height", "cols"),
        P("height", "cols"),
        P("height", "cols"),
        P("height", "cols"),
        P("height", "cols", None),
        P("height", "cols", None),
        P("height", "cols", None),
    )
    out_specs = (
        P(None, "height", "cols", None),
        P(None, "height", "cols", None),
        P("height", "cols", None),
        P("height", "cols", None),
    )
    return jax.shard_map(
        on_device, mesh=mesh, in_specs=in_specs, out_specs=out_specs, check_vma=False
    )
```

```python
import functools
import jax
import jax.numpy as jnp
from jax import lax
from jax.experimental import pallas as pl
from jax.experimental.pallas import tpu as pltpu
from jax.sharding import PartitionSpec as P

f32, bf16, i32 = jnp.float32, jnp.bfloat16, jnp.int32
spring = 0.05
cutoff_sq = 1.44
damping = 0.5
step_dt = 0.05
gravity = 1.0
deposit_gain = 2.0
LANES = 128
COMPS = 8
DEPTH = 2
ROWS_OUT = 24
FLAG_LANES = 16
MIB = 1024 * 1024
EXITS, OWNERS, INLETS = 0, 16, 32


def rounded(value):
    return value.astype(bf16).astype(f32)


def rounded_pair(value):
    high = rounded(value)
    return high, rounded(value - high)


def split(value):
    high = rounded(value)
    mid = rounded(value - high)
    return high, mid, value - high - mid


def centred(tile, r, c, rows, wide):
    row = lax.broadcasted_iota(i32, (COMPS, LANES), 0)
    side = jnp.float32(c - wide // 2)
    up = (r - rows // 2).astype(f32)
    return tile + jnp.where(row == 0, side, jnp.where(row == 2, up, 0.0))


def place_parts(tile, r, c, rows, wide):
    row = lax.broadcasted_iota(i32, (COMPS, LANES), 0)
    place = jnp.where(row < 3, centred(tile, r, c, rows, wide), 0.0)
    high, mid = rounded_pair(place)
    place = high + mid
    return high, mid, -jnp.sum(place * place, axis=0, keepdims=True)


def source_features(tile, r, c, rows, wide):
    row = lax.broadcasted_iota(i32, (COMPS, LANES), 0)
    row32 = lax.broadcasted_iota(i32, (32, LANES), 0)
    high, mid, size = place_parts(tile, r, c, rows, wide)
    size_high, size_mid, size_low = split(size)
    first = jnp.where(row < 3, high, 1.0)
    first = jnp.where(row == 3, size_high, jnp.where(row == 4, size_mid, jnp.where(row == 5, size_low, first)))
    second = jnp.where(row < 3, high, jnp.where(row == 3, 1.0, 0.0))
    kind = lax.rem(r, 3) * 4 + c % 4
    kind = kind + jnp.where(kind < 4, 12, jnp.where(kind < 9, 15, 18))
    near = jnp.concatenate([first, second, mid, mid], axis=0) + jnp.where(row32 == kind, 1.0, 0.0)
    high, mid, low = split(centred(tile, r, c, rows, wide) - damping * pltpu.roll(tile, 5, 0))
    first = jnp.where(row < 3, high, jnp.where(row == 3, 1.0, 0.0))
    second = jnp.where(row < 3, mid, jnp.where(row < 4, 0.0, pltpu.roll(low, 4, 0)))
    return near, jnp.concatenate([first, second], axis=0).astype(bf16)


def target_features(tile, r, c, rows, wide):
    row = lax.broadcasted_iota(i32, (COMPS, LANES), 0)
    row32 = lax.broadcasted_iota(i32, (32, LANES), 0)
    lane32 = lax.broadcasted_iota(i32, (32, LANES), 1)
    high, mid, size = place_parts(tile, r, c, rows, wide)
    own_high, own_mid, own_low = split(cutoff_sq + size)
    first = jnp.where(row < 3, 2.0 * high, jnp.where(row < 6, 1.0, jnp.where(row == 6, own_high, own_mid)))
    second = jnp.where(row < 3, 2.0 * mid, jnp.where(row == 3, own_low, 0.0))
    third = jnp.where(row < 3, 2.0 * high, 0.0)
    fourth = jnp.where(row < 3, 2.0 * mid, 0.0)
    kind = jnp.where(row32 < 16, row32 - 12, jnp.where(row32 < 24, row32 - 15, row32 - 18))
    is_kind = ((row32 >= 12) & (row32 < 16)) | ((row32 >= 19) & (row32 < 24)) | ((row32 >= 27) & (row32 < 30))
    kind_row = jnp.where(kind < 4, 0, jnp.where(kind < 8, 1, 2))
    up = kind_row + lax.rem(4 - lax.rem(r, 3), 3)
    up = jnp.where(up > 2, up - 3, up)
    side = kind - 4 * kind_row + (5 - c % 4) % 4
    side = jnp.where(side > 3, side - 4, side)
    if DEPTH <= c < wide - DEPTH:
        start = (c - DEPTH) * FLAG_LANES
    else:
        start = (lax.rem(r, DEPTH) * DEPTH + c % 2) * FLAG_LANES
    wanted = jnp.where(side < 3, 3 * up + side + start, LANES)
    flags = jnp.sum(jnp.where(lane32 == wanted, tile[6:7, :], 0.0), axis=1, keepdims=True)
    barred = jnp.where(is_kind, -1024.0 * (1.0 - flags), 0.0)
    return jnp.concatenate([first, second, third, fourth], axis=0) + barred


def forces_on(tiles, r, c, rows, wide, turned, pulled):
    features = [target_features(tile, r, c + k, rows, wide) for k, tile in enumerate(tiles)]
    target = jnp.concatenate(features, axis=1).astype(bf16)
    weights = []
    for k in range(4):
        spread = [jnp.zeros((32, 2 * LANES), bf16)] * 4
        spread[k] = target
        weights.append(jnp.concatenate(spread, axis=0))
    total = jnp.zeros((16, 2 * LANES), f32)
    for i in range(3):
        for j in range(4):
            s = c - 1 + j
            near = jnp.dot(turned[r + i - 1, s // 4], weights[s % 4], preferred_element_type=f32)
            weight = jnp.maximum(near, 0.0)
            pulls = pulled[r + i - 1, s]
            high = weight.astype(bf16)
            total = total + jnp.dot(pulls, high, preferred_element_type=f32)
            low = (weight - high.astype(f32)).astype(bf16)
            total = total + jnp.dot(pulls, low, preferred_element_type=f32)
    forces = []
    for k, tile in enumerate(tiles):
        first, second = total[0:8, k * LANES : (k + 1) * LANES], total[8:16, k * LANES : (k + 1) * LANES]
        moving = centred(tile, r, c + k, rows, wide) - damping * pltpu.roll(tile, 5, 0)
        forces.append((spring / cutoff_sq) * (moving * first[3:4, :] - first - second - pltpu.roll(second, 4, 0)))
    return forces


def stepped(tile, force):
    row = lax.broadcasted_iota(i32, (COMPS, LANES), 0)
    change = step_dt * force - jnp.where(row == 2, step_dt * gravity, 0.0)
    speeds = tile + pltpu.roll(change, 3, 0)
    places = tile + step_dt * pltpu.roll(speeds, 5, 0)
    return jnp.where(row < 3, places, jnp.where(row < 6, speeds, tile))


def position():
    heights, groups = lax.axis_size("height"), lax.axis_size("cols")
    h, c = lax.axis_index("height"), lax.axis_index("cols")
    return c > 0, c < groups - 1, h > 0, h < heights - 1, lax.rem(h, 2) == 0, lax.rem(c, 2) == 0


def halo_rows(rows, cols, d, r, c):
    wide = cols + 2 * DEPTH
    start = d * rows * wide
    if c < DEPTH:
        return start + rows * cols + r * DEPTH + c
    if c >= cols + DEPTH:
        return start + rows * (cols + DEPTH) + r * DEPTH + c - cols - DEPTH
    return start + r * cols + c - DEPTH


def particles_kernel(
    ints_ref, own_ref, first_ref, second_ref, slots_ref,
    sums_ref, settled_ref, leaving_ref, state, turned, pulled, begun, blocks,
    *, rows, cols,
):
    wide = cols + 2 * DEPTH
    high = rows + 2 * DEPTH
    left, right, below, above, even, _ = position()
    one, two = first_ref[...], second_ref[...]
    blocks[0] = jnp.where(below, jnp.where(even, two, one), 0.0)
    blocks[1] = own_ref[...]
    blocks[2] = jnp.where(above, jnp.where(even, one, two), 0.0)
    flag_row = 6 * rows * wide
    for block in range(3):
        for r in range(rows):
            for c in range(wide):
                for d in range(6):
                    row = halo_rows(rows, cols, d, r, c)
                    state[block * rows + r, c, d : d + 1] = blocks[block, row : row + 1]
                row = flag_row + (rows if c < DEPTH else rows + 1 if c >= cols + DEPTH else r)
                state[block * rows + r, c, 6:7] = blocks[block, row : row + 1]
                state[block * rows + r, c, 7:8] = jnp.zeros((1, LANES), f32)

    def fill(source, first, last):
        def one_row(r, carry):
            for block in range(wide // 4):
                near = []
                for c in range(4 * block, 4 * block + 4):
                    places, moving = source_features(source[r, c], r, c, high, wide)
                    near.append(places)
                    pulled[r, c] = moving
                turned[r, block] = jnp.concatenate(near, axis=0).T.astype(bf16)
            return carry

        lax.fori_loop(first, last, one_row, 0)

    fill(state, 0, high)

    def first_step(r, carry):
        begun[r, 0] = jnp.zeros((COMPS, LANES), f32)
        begun[r, wide - 1] = jnp.zeros((COMPS, LANES), f32)
        for c in range(1, wide - 1, 2):
            tiles = [state[r, c], state[r, c + 1]]
            forces = forces_on(tiles, r, c, high, wide, turned, pulled)
            for k in range(2):
                inside = ((r >= DEPTH) | below) & ((r < rows + DEPTH) | above)
                if c + k < DEPTH:
                    inside = inside & left
                if c + k >= cols + DEPTH:
                    inside = inside & right
                begun[r, c + k] = jnp.where(inside, stepped(tiles[k], forces[k]), 0.0)
        return carry

    lax.fori_loop(1, high - 1, first_step, 0)
    fill(begun, 1, high - 1)

    def second_step(r, carry):
        for c in range(DEPTH, DEPTH + cols, 2):
            tiles = [begun[r, c], begun[r, c + 1]]
            forces = forces_on(tiles, r, c, high, wide, turned, pulled)
            for k in range(2):
                done = stepped(tiles[k], forces[k])
                settled_ref[r - DEPTH, c + k - DEPTH] = done
        return carry

    lax.fori_loop(DEPTH, DEPTH + rows, second_step, 0)

    def deposit(r, carry):
        row = lax.broadcasted_iota(i32, (16, LANES), 0)
        cell = lax.broadcasted_iota(i32, (LANES, LANES), 0)
        for c in range(cols):
            lift_high, lift_mid, lift_low = split(deposit_gain * settled_ref[r, c, 5:6, :])
            parts = jnp.where(row == 0, lift_high, jnp.where(row == 1, lift_mid, jnp.where(row == 2, lift_low, 0.0)))
            table = jnp.where(cell == slots_ref[r, c : c + 1, :], 1.0, 0.0).astype(bf16)
            gathered = lax.dot_general(
                parts.astype(bf16), table, (((1,), (1,)), ((), ())), preferred_element_type=f32
            )
            sums_ref[pl.ds(r * cols + c, 1), :] = jnp.sum(gathered, axis=0, keepdims=True)
        return carry

    lax.fori_loop(0, rows, deposit, 0)

    lane = lax.broadcasted_iota(i32, (1, LANES), 1)
    owner_row = jnp.zeros((1, LANES), i32)
    for t in range(rows * cols):
        owner_row = jnp.where(lax.rem(lane, rows * cols) == t, ints_ref[0, OWNERS + t], owner_row)
    row = lax.broadcasted_iota(i32, (ROWS_OUT - rows * cols, LANES), 0)
    sums_ref[rows * cols :, :] = jnp.where(row == 0, owner_row.astype(f32), 0.0)

    leaving_ref[...] = jnp.zeros_like(leaving_ref)
    count = jnp.int32(0)
    for t in range(rows * cols):
        flag = ints_ref[0, EXITS + t]

        @pl.when((flag > 0) & (count < cols))
        def _(t=t, count=count):
            for d in range(6):
                leaving_ref[d, pl.ds(count, 1)] = settled_ref[t // cols, t % cols, d : d + 1]

        count = count + flag


def particles(ints, own, first, second, slots):
    rows, cols = slots.shape[:2]
    wide, high = cols + 2 * DEPTH, rows + 2 * DEPTH
    smem = pl.BlockSpec(memory_space=pltpu.SMEM)
    vmem = pl.BlockSpec(memory_space=pltpu.VMEM)
    return pl.pallas_call(
        functools.partial(particles_kernel, rows=rows, cols=cols),
        out_shape=(
            jax.ShapeDtypeStruct((ROWS_OUT, LANES), f32),
            jax.ShapeDtypeStruct((rows, cols, COMPS, LANES), f32),
            jax.ShapeDtypeStruct((6, cols, LANES), f32),
        ),
        in_specs=[smem, vmem, vmem, vmem, vmem],
        out_specs=(vmem, vmem, vmem),
        scratch_shapes=[
            pltpu.VMEM((high, wide, COMPS, LANES), f32),
            pltpu.VMEM((high, wide // 4, LANES, LANES), bf16),
            pltpu.VMEM((high, wide, 16, LANES), bf16),
            pltpu.VMEM((high, wide, COMPS, LANES), f32),
            pltpu.VMEM((3, *own.shape), f32),
        ],
        compiler_params=pltpu.CompilerParams(vmem_limit_bytes=12 * MIB),
        name="particles",
    )(ints, own, first, second, slots)


def matching(heights, groups, axis, odd, wrap):
    size = heights if axis == "height" else groups
    pairs = []
    for h in range(heights):
        for c in range(groups):
            i = h if axis == "height" else c
            j = i ^ 1 if not odd else (i + 1 if i % 2 else i - 1)
            if 0 <= j < size or wrap:
                j = j % size
                target = (j, c) if axis == "height" else (h, j)
            else:
                target = (h, c ^ 1) if axis == "height" else (h ^ 1, c)
            pairs.append((h * groups + c, target[0] * groups + target[1]))
    return pairs


def around_pairs(heights, groups):
    pairs = []
    for h in range(heights):
        for c in range(groups):
            target = (heights - 1 - h, c) if h in (0, heights - 1) else (h, c ^ 1)
            pairs.append((h * groups + c, target[0] * groups + target[1]))
    return pairs


def exchanged(value, axis, wrap):
    heights, groups = lax.axis_size("height"), lax.axis_size("cols")
    return [
        lax.ppermute(value, ("height", "cols"), matching(heights, groups, axis, odd, wrap)) for odd in (False, True)
    ]


LINES = 32


def begin_kernel(zeros_ref):
    zeros_ref[...] = jnp.zeros_like(zeros_ref)


def begun_zeros():
    return pl.pallas_call(
        begin_kernel,
        out_shape=jax.ShapeDtypeStruct((8, LANES), f32),
        out_specs=pl.BlockSpec(memory_space=pltpu.VMEM),
        cost_estimate=pl.CostEstimate(flops=10**10, bytes_accessed=4096, transcendentals=0),
        compiler_params=pltpu.CompilerParams(vmem_limit_bytes=MIB),
        name="begin",
    )()


def pack_kernel(
    zeros_ref, exits_hbm, owners_hbm, inlets_hbm, positions_hbm, velocities_hbm, contacts_hbm, slots_hbm, gas_hbm, diagonal_hbm,
    first_ref, second_ref, flags_ref, ints_ref, slots_ref, state_ref, cells_ref,
    sides, wide_flags, contacts_ref, exits_ref, owners_ref, inlets_ref, arrived,
):
    rows, cols = state_ref.shape[1:3]
    _, levels, across, along = cells_ref.shape
    across = across - 8
    pairs = (
        (positions_hbm, state_ref.at[0:3]),
        (velocities_hbm, state_ref.at[3:6]),
        (gas_hbm, cells_ref.at[0, :, 0:across]),
        (diagonal_hbm, cells_ref.at[1, :, 0:across]),
        (contacts_hbm, contacts_ref),
        (exits_hbm, exits_ref),
        (owners_hbm, owners_ref),
        (inlets_hbm, inlets_ref),
        (slots_hbm, slots_ref),
    )
    copies = [pltpu.make_async_copy(source, target, arrived.at[n]) for n, (source, target) in enumerate(pairs)]
    for copy in copies:
        copy.start()
    sides[...] = jnp.zeros_like(sides) + zeros_ref[0:1]
    wide_flags[...] = jnp.zeros_like(wide_flags)
    cells_ref[:, :, across:] = jnp.zeros((2, levels, 8, along), f32)
    for copy in copies:
        copy.wait()
    lane = lax.broadcasted_iota(i32, (1, LANES), 1)
    ints = jnp.zeros((1, LANES), i32)
    for r in range(rows):
        for c in range(cols):
            ints = jnp.where(lane == EXITS + r * cols + c, exits_ref[r, c], ints)
            ints = jnp.where(lane == OWNERS + r * cols + c, owners_ref[r, c], ints)
    for c in range(cols):
        ints = jnp.where(lane == INLETS + c, inlets_ref[0, c], ints)
    ints_ref[...] = ints
    wide_flags[:, :, 0 : contacts_ref.shape[2]] = contacts_ref[...].astype(f32)
    flags = []
    for r in range(rows):
        spread = pltpu.roll(wide_flags[r], 0, 1, stride=FLAG_LANES, stride_axis=0)
        flags.append(jnp.sum(spread, axis=0, keepdims=True))
        flags_ref[r : r + 1] = flags[r]
    for side in range(2):
        shown = jnp.zeros((1, LANES), f32)
        for r in range(rows):
            for k in range(DEPTH):
                c = k if side == 0 else cols - DEPTH + k
                for d in range(6):
                    row = d * rows * DEPTH + r * DEPTH + k
                    sides[side, row : row + 1] = state_ref[d, r, c : c + 1]
            turn = (r * DEPTH - (0 if side == 0 else cols - DEPTH)) * FLAG_LANES
            part = pltpu.roll(flags[r], turn % LANES, 1)
            shown = jnp.where(lane // (DEPTH * FLAG_LANES) == r, part, shown)
        sides[side, 6 * rows * DEPTH : 6 * rows * DEPTH + 1] = shown
        for z in range(levels):
            for k in range(2):
                x = k if side == 0 else across - 2 + k
                for kind in range(2):
                    for q in range(along // LANES):
                        row = LINES + ((z * 2 + k) * 2 + kind) * (along // LANES) + q
                        sides[side, row : row + 1] = cells_ref[kind, z, x : x + 1, q * LANES : (q + 1) * LANES]
    even = position()[5]
    first_ref[...] = jnp.where(even, sides[1], sides[0])
    second_ref[...] = jnp.where(even, sides[0], sides[1])


def packed(exits, owners, inlets, positions, velocities, contacts, slots, gas, diagonal):
    levels, across, along = gas.shape
    rows, cols = positions.shape[1:3]
    side = jax.ShapeDtypeStruct((LINES + levels * 4 * (along // LANES), LANES), f32)
    vmem = pl.BlockSpec(memory_space=pltpu.VMEM)
    return pl.pallas_call(
        pack_kernel,
        out_shape=(
            side,
            side,
            jax.ShapeDtypeStruct((rows, LANES), f32),
            jax.ShapeDtypeStruct((1, LANES), i32),
            jax.ShapeDtypeStruct(slots.shape, i32),
            jax.ShapeDtypeStruct((6, rows, cols, LANES), f32),
            jax.ShapeDtypeStruct((2, levels, across + 8, along), f32),
        ),
        in_specs=[vmem] + [pl.BlockSpec(memory_space=pl.ANY)] * 9,
        out_specs=(vmem,) * 7,
        scratch_shapes=[
            pltpu.VMEM((2, *side.shape), f32),
            pltpu.VMEM((rows, cols, LANES), f32),
            pltpu.VMEM(contacts.shape, i32),
            pltpu.SMEM(exits.shape, i32),
            pltpu.SMEM(owners.shape, i32),
            pltpu.SMEM(inlets.shape, i32),
            pltpu.SemaphoreType.DMA((9,)),
        ],
        compiler_params=pltpu.CompilerParams(vmem_limit_bytes=8 * MIB),
        name="pack",
    )(begun_zeros(), exits, owners, inlets, positions, velocities, contacts, slots, gas, diagonal)


def merge_kernel(state_ref, flags_ref, line_a, line_b, window_ref):
    rows, cols = state_ref.shape[1:3]
    each = rows * (cols + 2 * DEPTH)
    count = 6 * rows * DEPTH
    left, right, _, _, _, even = position()
    one, two = line_a[0 : count + 8], line_b[0 : count + 8]
    low = jnp.where(left, jnp.where(even, two, one), 0.0)
    top = jnp.where(right, jnp.where(even, one, two), 0.0)
    for d in range(6):
        for r in range(rows):
            window_ref[d * each + r * cols : d * each + (r + 1) * cols] = state_ref[d, r]
        at = d * each + rows * cols
        piece = slice(d * rows * DEPTH, (d + 1) * rows * DEPTH)
        window_ref[at : at + rows * DEPTH] = low[piece]
        window_ref[at + rows * DEPTH : at + 2 * rows * DEPTH] = top[piece]
    window_ref[6 * each : 6 * each + 8] = jnp.concatenate(
        [flags_ref[...], low[count : count + 1], top[count : count + 1], jnp.zeros((6 - rows, LANES), f32)], axis=0
    )


def merged(state, flags, lines):
    rows, cols = state.shape[1:3]
    vmem = pl.BlockSpec(memory_space=pltpu.VMEM)
    return pl.pallas_call(
        merge_kernel,
        out_shape=jax.ShapeDtypeStruct((6 * rows * (cols + 2 * DEPTH) + 8, LANES), f32),
        in_specs=[vmem] * 4,
        out_specs=vmem,
        compiler_params=pltpu.CompilerParams(vmem_limit_bytes=4 * MIB),
        name="merge",
    )(state, flags, *lines)


def line_at(lines, z, k, kind, q, quarters):
    row = LINES + ((z * 2 + k) * 2 + kind) * quarters + q
    return lines[row : row + 1]


def cells_kernel(cells_in, line_a, line_b, cells_ref):
    kinds, levels, rows, along = cells_ref.shape
    quarters = along // LANES
    even = position()[5]
    cells_ref[...] = cells_in[...]
    for kind in range(kinds):
        for z in range(levels):
            for q in range(quarters):
                low = [line_at(lines, z, 1, kind, q, quarters) for lines in (line_a, line_b)]
                top = [line_at(lines, z, 0, kind, q, quarters) for lines in (line_a, line_b)]
                cells_ref[kind, z, rows - 8 : rows, q * LANES : (q + 1) * LANES] = jnp.concatenate(
                    [
                        jnp.where(even, low[1], low[0]),
                        jnp.where(even, top[0], top[1]),
                        jnp.zeros((6, LANES), f32),
                    ],
                    axis=0,
                )


def cells_of(cells, lines):
    vmem = pl.BlockSpec(memory_space=pltpu.VMEM)
    return pl.pallas_call(
        cells_kernel,
        out_shape=jax.ShapeDtypeStruct(cells.shape, f32),
        in_specs=[pl.BlockSpec(memory_space=pltpu.VMEM)] * 3,
        out_specs=vmem,
        compiler_params=pltpu.CompilerParams(vmem_limit_bytes=4 * MIB),
        name="cells",
    )(cells, *lines)


def right_side_kernel(
    sums_ref, side_a, side_b, height_a, height_b, cells_ref, line_a, line_b, gas_a, gas_b, rhs_ref, near_ref, far_ref, dots_ref, scaling, rhs, first, second,
):
    _, levels, across, along = cells_ref.shape
    across = across - 8
    edge = 8
    wide = across + 2 * edge
    quarters = along // LANES
    left, right, below, above, even, even_c = position()

    def low_of(is_even, one, two):
        return jnp.where(is_even, two, one)

    def high_of(is_even, one, two):
        return jnp.where(is_even, one, two)

    for ref in (scaling, rhs):
        ref[:, 0:edge, :] = jnp.zeros((3 * levels, edge, along), f32)
        ref[:, edge + across :, :] = jnp.zeros((3 * levels, edge, along), f32)
    scaling[levels : 2 * levels, edge : edge + across] = 1.0 / (6.0 + cells_ref[1, :, 0:across])
    rhs[levels : 2 * levels, edge : edge + across] = cells_ref[0, :, 0:across]
    for level, choose, present in ((0, low_of, below), (2 * levels, high_of, above)):
        for z in range(levels):
            rhs[level + z, edge : edge + across] = choose(even, gas_a[0, z, 0:across], gas_b[0, z, 0:across])
            m = 1.0 / (6.0 + choose(even, gas_a[1, z, 0:across], gas_b[1, z, 0:across]))
            scaling[level + z, edge : edge + across] = jnp.where(present, m, 0.0)
            for row, x, beside_it in ((across, edge - 1, left), (across + 1, edge + across, right)):
                line = slice(row, row + 1)
                rhs[level + z, x : x + 1] = choose(even, gas_a[0, z, line], gas_b[0, z, line])
                m = 1.0 / (6.0 + choose(even, gas_a[1, z, line], gas_b[1, z, line]))
                scaling[level + z, x : x + 1] = jnp.where(present & beside_it, m, 0.0)
    for choose, start, present in ((low_of, edge - 2, left), (high_of, edge + across, right)):
        for z in range(levels):
            for k in range(2):
                for q in range(quarters):
                    part = slice(q * LANES, (q + 1) * LANES)
                    x = slice(start + k, start + k + 1)
                    kinds = [
                        choose(even_c, *[line_at(lines, z, k, kind, q, quarters) for lines in (line_a, line_b)])
                        for kind in range(2)
                    ]
                    rhs[levels + z, x, part] = kinds[0]
                    scaling[levels + z, x, part] = jnp.where(present, 1.0 / (6.0 + kinds[1]), 0.0)

    lane = lax.broadcasted_iota(i32, (1, LANES), 1)
    tiles = 16
    shift_q, shift_x = quarters.bit_length() - 1, across.bit_length() - 1
    groups = []
    for name, choose, present in (("below", low_of, below), ("own", None, None), ("above", high_of, above)):
        if choose is None:
            parts = [low_of(even_c, side_a[...], side_b[...]), sums_ref[...], high_of(even_c, side_a[...], side_b[...])]
        else:
            block = [choose(even, height_a[k * ROWS_OUT : (k + 1) * ROWS_OUT], height_b[k * ROWS_OUT : (k + 1) * ROWS_OUT]) for k in range(3)]
            parts = [low_of(even_c, block[1], block[2]), block[0], high_of(even_c, block[1], block[2])]
        level = 0 if name == "below" else levels if name == "own" else 2 * levels
        code = jnp.full((1, LANES), -1, i32)
        for n, part in enumerate(parts):
            owner = part[tiles : tiles + 1].astype(i32)
            x = ((owner >> shift_q) & (across - 1)) + (edge + (n - 1) * across)
            z = owner >> (shift_q + shift_x)
            here = ((lane >> 4) == n) | ((lane >> 4) == n + 3)
            here = here & (x >= edge - 2) & (x < edge + across + 2)
            if n == 0:
                here = here & left
            if n == 2:
                here = here & right
            if present is not None:
                here = here & present
            code = jnp.where(here, (z * wide + x) * quarters + (owner & (quarters - 1)), code)
        values = jnp.concatenate([part[0:tiles] for part in parts], axis=0)
        high = values.astype(bf16)
        low = (values - high.astype(f32)).astype(bf16)
        values = jnp.concatenate([high, low, jnp.zeros((LANES - 6 * tiles, LANES), bf16)], axis=0)
        spot = lax.broadcasted_iota(i32, (levels * wide, LANES), 0) * quarters
        for k in range(quarters):
            table = jnp.where(code == spot + k, 1.0, 0.0).astype(bf16)
            added = jnp.dot(table, values, preferred_element_type=f32)
            for z in range(levels):
                rhs[level + z, :, k * LANES : (k + 1) * LANES] -= added[z * wide : (z + 1) * wide]

    for z in range(3 * levels):
        first[z] = scaling[z] * rhs[z]
    place = lax.broadcasted_iota(i32, (wide, along), 1)

    def beside(ref, z):
        mid = ref[z]
        total = ref[z - 1] + ref[z + 1] + pltpu.roll(mid, 1, 0) + pltpu.roll(mid, wide - 1, 0)
        total = total + jnp.where(place > 0, pltpu.roll(mid, 1, 1), 0.0)
        return total + jnp.where(place < along - 1, pltpu.roll(mid, along - 1, 1), 0.0)

    dots = [jnp.zeros((8, LANES), f32)] * 4

    def folded(value):
        value = jnp.sum(value.reshape(across // 8, 8, along), axis=0)
        return sum(value[:, k * LANES : (k + 1) * LANES] for k in range(quarters))

    inner = slice(edge, edge + across)
    for z in range(levels - 1, 2 * levels + 1):
        near = beside(first, z)
        second[z] = scaling[z] * near
        if levels <= z < 2 * levels:
            near = near[inner]
            near_ref[z - levels] = near
            rhs_ref[z - levels] = rhs[z, inner]
            z0 = first[z, inner]
            dots[0] = dots[0] + folded(z0 * rhs[z, inner])
            dots[1] = dots[1] + folded(z0 * near)
            dots[2] = dots[2] + folded(second[z, inner] * near)
    for z in range(levels, 2 * levels):
        far = beside(second, z)[inner]
        far_ref[z - levels] = far
        dots[3] = dots[3] + folded(second[z, inner] * far)
    row = lax.broadcasted_iota(i32, (8, LANES), 0)
    lane8 = lax.broadcasted_iota(i32, (8, LANES), 1)
    line = jnp.zeros((1, LANES), f32)
    for k in range(4):
        total = jnp.sum(jnp.sum(dots[k], axis=0, keepdims=True), axis=1, keepdims=True)
        line = jnp.where(lane == k, total, line)
    dots_ref[...] = jnp.broadcast_to(line, dots_ref.shape)


def right_side_of(sums, side, height, cells, lines, gases, devices):
    _, levels, across, along = cells.shape
    across = across - 8
    vmem = pl.BlockSpec(memory_space=pltpu.VMEM)
    whole = pltpu.VMEM((3 * levels, across + 16, along), f32)
    return pl.pallas_call(
        right_side_kernel,
        out_shape=(jax.ShapeDtypeStruct((levels, across, along), f32),) * 3 + (jax.ShapeDtypeStruct((devices, LANES), f32),),
        in_specs=[vmem] * 10,
        out_specs=(vmem,) * 4,
        scratch_shapes=[whole] * 4,
        compiler_params=pltpu.CompilerParams(vmem_limit_bytes=16 * MIB),
        name="right_side",
    )(sums, *side, *height, cells, *lines, *gases)


def results_kernel(
    ints_ref, dots_ref, rhs_ref, near_ref, far_ref, cells_ref, settled_ref,
    height_a, height_b, around_ref, positions_ref, velocities_ref, pressure_ref, residual_ref,
):
    rows, cols = settled_ref.shape[:2]
    _, _, below, _, even, _ = position()
    totals = jnp.sum(dots_ref[...], axis=0, keepdims=True)
    g00, g01, g11, g12 = [totals[:, k : k + 1] for k in range(4)]
    ratio = g01 / g00
    alpha = g00 / (g00 - g01)
    square = alpha * alpha
    renewed = square * (g11 - ratio * g01)
    beta = renewed / g00
    crossed = square * (ratio * ratio * g01 - 2.0 * ratio * g11 + g12)
    curvature = renewed - crossed - beta * renewed / alpha
    later = renewed / curvature
    one = alpha + later * (1.0 - alpha + beta)
    two = later * alpha
    for z in range(rhs_ref.shape[0]):
        m = 1.0 / (6.0 + cells_ref[1, z, 0 : rhs_ref.shape[1]])
        rhs, near = rhs_ref[z], near_ref[z]
        pressure_ref[z] = m * (one * rhs + two * near)
        residual_ref[z] = (1.0 - one) * rhs + (one - two) * near + two * far_ref[z]
    for r in range(1, rows):
        for c in range(cols):
            kept = jnp.where(ints_ref[0, EXITS + r * cols + c] > 0, 0.0, settled_ref[r, c])
            for d in range(3):
                positions_ref[d, r, c : c + 1] = kept[d : d + 1]
                velocities_ref[d, r, c : c + 1] = kept[d + 3 : d + 4]
    start = 3 * ROWS_OUT
    for d in range(6):
        block = slice(start + d * cols, start + (d + 1) * cols)
        tiles = jnp.where(even, height_b[block], height_a[block])
        target = positions_ref if d < 3 else velocities_ref
        for k in range(cols):
            target[d % 3, 0, pl.ds(ints_ref[0, INLETS + k], 1)] = tiles[k : k + 1]


def results_of(ints, dots, rhs, near, far, cells, settled, height, around):
    rows, cols = settled.shape[:2]
    smem = pl.BlockSpec(memory_space=pltpu.SMEM)
    vmem = pl.BlockSpec(memory_space=pltpu.VMEM)
    particle = jax.ShapeDtypeStruct((3, rows, cols, LANES), f32)
    field = jax.ShapeDtypeStruct(rhs.shape, f32)
    return pl.pallas_call(
        results_kernel,
        out_shape=(particle, particle, field, field),
        in_specs=[smem] + [vmem] * 9,
        out_specs=(vmem,) * 4,
        compiler_params=pltpu.CompilerParams(vmem_limit_bytes=8 * MIB),
        name="results",
    )(ints, dots, rhs, near, far, cells, settled, *height, around)


def on_device(
    positions, velocities, contacts, exit_flags, inlet_slots, cell_blocks, cell_slots, gas_source, diagonal
):
    heights, groups = lax.axis_size("height"), lax.axis_size("cols")
    h, c = lax.axis_index("height"), lax.axis_index("cols")
    *sides, flags, ints, slots, state, cells = packed(
        exit_flags, cell_blocks, inlet_slots, positions, velocities, contacts.transpose(1, 2, 0), cell_slots,
        gas_source, diagonal,
    )
    lines = [
        lax.ppermute(value, ("height", "cols"), matching(heights, groups, "cols", odd, True))
        for value, odd in zip(sides, (False, True))
    ]
    window = merged(state, flags, lines)
    beside = exchanged(window, "height", False)
    cells = cells_of(cells, lines)
    sent, beside = lax.optimization_barrier((cells, beside))
    gases = exchanged(sent, "height", False)
    sums, settled, leaving = particles(ints, window, *beside, slots)
    near = exchanged(sums, "cols", True)
    parcel = jnp.concatenate([sums, *near, leaving.reshape(-1, LANES)], axis=0)
    parcels = exchanged(parcel, "height", True)
    rhs, first, second, dots = right_side_of(sums, near, parcels, cells, lines, gases, heights * groups)
    dots = lax.all_to_all(dots, ("height", "cols"), 0, 0, tiled=True)
    return results_of(ints, dots, rhs, first, second, cells, settled, parcels, leaving)


def solution(mesh):
    in_specs = (
        P(None, "height", "cols", None),
        P(None, "height", "cols", None),
        P(None, "height", "cols"),
        P("height", "cols"),
        P("height", "cols"),
        P("height", "cols"),
        P("height", "cols", None),
        P("height", "cols", None),
        P("height", "cols", None),
    )
    out_specs = (
        P(None, "height", "cols", None),
        P(None, "height", "cols", None),
        P("height", "cols", None),
        P("height", "cols", None),
    )
    return jax.shard_map(
        on_device, mesh=mesh, in_specs=in_specs, out_specs=out_specs, check_vma=False
    )
```

```python
import functools
import jax
import jax.numpy as jnp
from jax import lax
from jax.experimental import pallas as pl
from jax.experimental.pallas import tpu as pltpu
from jax.sharding import PartitionSpec as P

f32, bf16, i32 = jnp.float32, jnp.bfloat16, jnp.int32
spring = 0.05
cutoff_sq = 1.44
damping = 0.5
step_dt = 0.05
gravity = 1.0
deposit_gain = 2.0
LANES = 128
COMPS = 8
DEPTH = 2
ROWS_OUT = 24
FLAG_LANES = 16
MIB = 1024 * 1024
NEARS = 6
EXITS, OWNERS, INLETS = 0, 16, 32


def rounded(value):
    return value.astype(bf16).astype(f32)


def rounded_pair(value):
    high = rounded(value)
    return high, rounded(value - high)


def split(value):
    high = rounded(value)
    mid = rounded(value - high)
    return high, mid, value - high - mid


def centred(tile, r, c, rows, wide):
    row = lax.broadcasted_iota(i32, (COMPS, LANES), 0)
    side = jnp.float32(c - wide // 2)
    up = (r - rows // 2).astype(f32)
    return tile + jnp.where(row == 0, side, jnp.where(row == 2, up, 0.0))


def place_parts(tile, r, c, rows, wide):
    row = lax.broadcasted_iota(i32, (COMPS, LANES), 0)
    place = jnp.where(row < 3, centred(tile, r, c, rows, wide), 0.0)
    high, mid = rounded_pair(place)
    place = high + mid
    return high, mid, -jnp.sum(place * place, axis=0, keepdims=True)


def source_features(tile, r, c, rows, wide):
    row = lax.broadcasted_iota(i32, (COMPS, LANES), 0)
    row32 = lax.broadcasted_iota(i32, (32, LANES), 0)
    high, mid, size = place_parts(tile, r, c, rows, wide)
    size_high, size_mid, size_low = split(size)
    first = jnp.where(row < 3, high, 1.0)
    first = jnp.where(row == 3, size_high, jnp.where(row == 4, size_mid, jnp.where(row == 5, size_low, first)))
    second = jnp.where(row < 3, high, jnp.where(row == 3, 1.0, 0.0))
    kind = lax.rem(r, 3) * 4 + c % 4
    kind = kind + jnp.where(kind < 4, 12, jnp.where(kind < 9, 15, 18))
    near = jnp.concatenate([first, second, mid, mid], axis=0) + jnp.where(row32 == kind, 1.0, 0.0)
    high, mid, low = split(centred(tile, r, c, rows, wide) - damping * pltpu.roll(tile, 5, 0))
    first = jnp.where(row < 3, high, jnp.where(row == 3, 1.0, 0.0))
    second = jnp.where(row < 3, mid, jnp.where(row < 4, 0.0, pltpu.roll(low, 4, 0)))
    return near, jnp.concatenate([first, second], axis=0).astype(bf16)


def target_features(tile, r, c, rows, wide):
    row = lax.broadcasted_iota(i32, (COMPS, LANES), 0)
    row32 = lax.broadcasted_iota(i32, (32, LANES), 0)
    lane32 = lax.broadcasted_iota(i32, (32, LANES), 1)
    high, mid, size = place_parts(tile, r, c, rows, wide)
    own_high, own_mid, own_low = split(cutoff_sq + size)
    first = jnp.where(row < 3, 2.0 * high, jnp.where(row < 6, 1.0, jnp.where(row == 6, own_high, own_mid)))
    second = jnp.where(row < 3, 2.0 * mid, jnp.where(row == 3, own_low, 0.0))
    third = jnp.where(row < 3, 2.0 * high, 0.0)
    fourth = jnp.where(row < 3, 2.0 * mid, 0.0)
    kind = jnp.where(row32 < 16, row32 - 12, jnp.where(row32 < 24, row32 - 15, row32 - 18))
    is_kind = ((row32 >= 12) & (row32 < 16)) | ((row32 >= 19) & (row32 < 24)) | ((row32 >= 27) & (row32 < 30))
    kind_row = jnp.where(kind < 4, 0, jnp.where(kind < 8, 1, 2))
    up = kind_row + lax.rem(4 - lax.rem(r, 3), 3)
    up = jnp.where(up > 2, up - 3, up)
    side = kind - 4 * kind_row + (5 - c % 4) % 4
    side = jnp.where(side > 3, side - 4, side)
    if DEPTH <= c < wide - DEPTH:
        start = (c - DEPTH) * FLAG_LANES
    else:
        start = (lax.rem(r, DEPTH) * DEPTH + c % 2) * FLAG_LANES
    wanted = jnp.where(side < 3, 3 * up + side + start, LANES)
    flags = jnp.sum(jnp.where(lane32 == wanted, tile[6:7, :], 0.0), axis=1, keepdims=True)
    barred = jnp.where(is_kind, -1024.0 * (1.0 - flags), 0.0)
    return jnp.concatenate([first, second, third, fourth], axis=0) + barred


def unit_operands(tiles, r, c, rows, wide):
    features = [target_features(tile, r, c + k, rows, wide) for k, tile in enumerate(tiles)]
    features = jnp.concatenate(features, axis=1).astype(bf16)
    start = (c - 1) // 4
    ends = (c - 1, c + 2)

    def spread(part, s):
        at = 4 * (s // 4 - start) + s % 4
        return jnp.concatenate([part if k == at else jnp.zeros_like(part) for k in range(8)], axis=0)

    halves = [spread(features[:, k * LANES : (k + 1) * LANES], s) for k, s in enumerate(ends)]
    return [spread(features, c), spread(features, c + 1), jnp.concatenate(halves, axis=1)]


def forces_row(tiles, r, columns, rows, wide, turned, pulled, nears, founds):
    ahead = len(nears) - 1
    units = [(pair, kind, i) for pair in range(len(columns)) for kind in range(3) for i in range(3)]
    blocks = wide // 4
    operands = [None] * len(columns)

    def begin(n):
        pair, kind, i = units[n]
        c = columns[pair]
        staged = (3 * pair + kind) % 2
        if i == 0:
            if kind == 0:
                operands[pair] = unit_operands(tiles[pair], r, c, rows, wide)
            pltpu.matmul_push_rhs(operands[pair][kind], staged, 0)
        start = (c - 1) // 4
        after = start + 1 if start + 1 < blocks else 0
        sources = jnp.concatenate([turned[r + i - 1, start], turned[r + i - 1, after]], axis=1)
        pltpu.matmul_acc_lhs(nears[n % len(nears)], sources, load_staged_rhs=staged if i == 0 else None)

    def finish(n):
        pair, kind, i = units[n]
        c = columns[pair]
        weight = jnp.maximum(pltpu.matmul_pop(nears[n % len(nears)]), 0.0)
        high = weight.astype(bf16)
        low = (weight - high.astype(f32)).astype(bf16)
        pltpu.matmul_push_rhs(jnp.concatenate([high, low], axis=0), n % 2, 1)
        row = r + i - 1
        if kind < 2:
            pulls = pulled[row, c + kind]
        else:
            pulls = jnp.concatenate([pulled[row, c - 1], pulled[row, c + 2]], axis=0)
        pulls = jnp.concatenate([pulls, pulls], axis=1)
        pltpu.matmul_acc_lhs(founds[2 * pair + (kind == 2)], pulls, load_staged_rhs=n % 2)

    for n in range(len(units) + ahead):
        if n < len(units):
            begin(n)
        if n >= ahead:
            finish(n - ahead)
    forces = []
    for pair, c in enumerate(columns):
        inner, outer = pltpu.matmul_pop(founds[2 * pair]), pltpu.matmul_pop(founds[2 * pair + 1])
        for k, tile in enumerate(tiles[pair]):
            part = slice(k * LANES, (k + 1) * LANES)
            total = inner[:, part] + outer[16 * k : 16 * k + 16, part]
            first, second = total[0:8], total[8:16]
            moving = centred(tile, r, c + k, rows, wide) - damping * pltpu.roll(tile, 5, 0)
            forces.append((spring / cutoff_sq) * (moving * first[3:4, :] - first - second - pltpu.roll(second, 4, 0)))
    return forces


def stepped(tile, force):
    row = lax.broadcasted_iota(i32, (COMPS, LANES), 0)
    change = step_dt * force - jnp.where(row == 2, step_dt * gravity, 0.0)
    speeds = tile + pltpu.roll(change, 3, 0)
    places = tile + step_dt * pltpu.roll(speeds, 5, 0)
    return jnp.where(row < 3, places, jnp.where(row < 6, speeds, tile))


def position():
    heights, groups = lax.axis_size("height"), lax.axis_size("cols")
    h, c = lax.axis_index("height"), lax.axis_index("cols")
    return c > 0, c < groups - 1, h > 0, h < heights - 1, lax.rem(h, 2) == 0, lax.rem(c, 2) == 0


def halo_rows(rows, cols, d, r, c):
    wide = cols + 2 * DEPTH
    start = d * rows * wide
    if c < DEPTH:
        return start + rows * cols + r * DEPTH + c
    if c >= cols + DEPTH:
        return start + rows * (cols + DEPTH) + r * DEPTH + c - cols - DEPTH
    return start + r * cols + c - DEPTH


def particles_kernel(
    ints_ref, own_ref, first_ref, second_ref,
    settled_ref, leaving_ref, state, turned, pulled, begun, blocks,
    *, rows, cols,
):
    wide = cols + 2 * DEPTH
    high = rows + 2 * DEPTH
    left, right, below, above, even, _ = position()
    one, two = first_ref[...], second_ref[...]
    blocks[0] = jnp.where(below, jnp.where(even, two, one), 0.0)
    blocks[1] = own_ref[...]
    blocks[2] = jnp.where(above, jnp.where(even, one, two), 0.0)
    flag_row = 6 * rows * wide
    for block in range(3):
        for r in range(rows):
            for c in range(wide):
                for d in range(6):
                    row = halo_rows(rows, cols, d, r, c)
                    state[block * rows + r, c, d : d + 1] = blocks[block, row : row + 1]
                row = flag_row + (rows if c < DEPTH else rows + 1 if c >= cols + DEPTH else r)
                state[block * rows + r, c, 6:7] = blocks[block, row : row + 1]
                state[block * rows + r, c, 7:8] = jnp.zeros((1, LANES), f32)

    def fill(source, first, last):
        def one_row(r, carry):
            for block in range(wide // 4):
                near = []
                for c in range(4 * block, 4 * block + 4):
                    places, moving = source_features(source[r, c], r, c, high, wide)
                    near.append(places)
                    pulled[r, c] = moving
                turned[r, block] = jnp.concatenate(near, axis=0).T.astype(bf16)
            return carry

        lax.fori_loop(first, last, one_row, 0)

    def substeps(*accumulators):
        nears, founds = accumulators[:NEARS], accumulators[NEARS:]
        for accumulator in accumulators:
            pltpu.matmul_pop(accumulator)
        fill(state, 0, high)

        def first_step(r, carry):
            begun[r, 0] = jnp.zeros((COMPS, LANES), f32)
            begun[r, wide - 1] = jnp.zeros((COMPS, LANES), f32)
            columns = list(range(1, wide - 1, 2))
            tiles = [[state[r, c], state[r, c + 1]] for c in columns]
            forces = forces_row(tiles, r, columns, high, wide, turned, pulled, nears, founds)
            for c in range(1, wide - 1):
                inside = ((r >= DEPTH) | below) & ((r < rows + DEPTH) | above)
                if c < DEPTH:
                    inside = inside & left
                if c >= cols + DEPTH:
                    inside = inside & right
                begun[r, c] = jnp.where(inside, stepped(tiles[(c - 1) // 2][(c - 1) % 2], forces[c - 1]), 0.0)
            return carry

        lax.fori_loop(1, high - 1, first_step, 0)
        fill(begun, 1, high - 1)

        def second_step(r, carry):
            columns = list(range(DEPTH, DEPTH + cols, 2))
            tiles = [[begun[r, c], begun[r, c + 1]] for c in columns]
            forces = forces_row(tiles, r, columns, high, wide, turned, pulled, nears, founds)
            for c in range(cols):
                settled_ref[r - DEPTH, c] = stepped(tiles[c // 2][c % 2], forces[c])
            return carry

        lax.fori_loop(DEPTH, DEPTH + rows, second_step, 0)

    pl.run_scoped(
        substeps,
        *[pltpu.ACC(0)((LANES, 2 * LANES), f32)] * NEARS,
        *[pltpu.ACC(1)((held, 2 * LANES), f32) for _ in range(wide // 2 - 1) for held in (16, 32)],
    )

    leaving_ref[...] = jnp.zeros_like(leaving_ref)
    count = jnp.int32(0)
    for t in range(rows * cols):
        flag = ints_ref[0, EXITS + t]

        @pl.when((flag > 0) & (count < cols))
        def _(t=t, count=count):
            for d in range(6):
                leaving_ref[d, pl.ds(count, 1)] = settled_ref[t // cols, t % cols, d : d + 1]

        count = count + flag


def particles(ints, own, first, second, rows, cols):
    wide, high = cols + 2 * DEPTH, rows + 2 * DEPTH
    smem = pl.BlockSpec(memory_space=pltpu.SMEM)
    vmem = pl.BlockSpec(memory_space=pltpu.VMEM)
    return pl.pallas_call(
        functools.partial(particles_kernel, rows=rows, cols=cols),
        out_shape=(
            jax.ShapeDtypeStruct((rows, cols, COMPS, LANES), f32),
            jax.ShapeDtypeStruct((6, cols, LANES), f32),
        ),
        in_specs=[smem, vmem, vmem, vmem],
        out_specs=(vmem, vmem),
        scratch_shapes=[
            pltpu.VMEM((high, wide, COMPS, LANES), f32),
            pltpu.VMEM((high, wide // 4, LANES, LANES), bf16),
            pltpu.VMEM((high, wide, 16, LANES), bf16),
            pltpu.VMEM((high, wide, COMPS, LANES), f32),
            pltpu.VMEM((3, *own.shape), f32),
        ],
        compiler_params=pltpu.CompilerParams(vmem_limit_bytes=12 * MIB),
        name="particles",
    )(ints, own, first, second)


def deposit_kernel(ints_ref, settled_ref, slots_ref, blocks_ref, own_ref, shared_ref):
    rows, cols = settled_ref.shape[:2]
    quarters = blocks_ref.shape[0]
    row = lax.broadcasted_iota(i32, (16, LANES), 0)
    cell = lax.broadcasted_iota(i32, (LANES, LANES), 0)
    lane = lax.broadcasted_iota(i32, (1, LANES), 1)
    owner_row = jnp.zeros((1, LANES), i32)
    for t in range(rows * cols):
        r, c = t // cols, t % cols
        owner = ints_ref[0, OWNERS + t]
        owner_row = jnp.where(lax.rem(lane, rows * cols) == t, owner, owner_row)
        lift_high, lift_mid, lift_low = split(deposit_gain * settled_ref[r, c, 5:6, :])
        parts = jnp.where(row == 0, lift_high, jnp.where(row == 1, lift_mid, jnp.where(row == 2, lift_low, 0.0)))
        table = jnp.where(cell == slots_ref[r, c : c + 1, :], 1.0, 0.0).astype(bf16)
        gathered = lax.dot_general(parts.astype(bf16), table, (((1,), (1,)), ((), ())), preferred_element_type=f32)
        sums = jnp.sum(gathered, axis=0, keepdims=True)
        own_ref[t : t + 1, :] = sums
        shared_ref[t : t + 1, :] = blocks_ref[owner % quarters, pl.ds(owner // quarters, 1), :] * sums
    row = lax.broadcasted_iota(i32, (ROWS_OUT - rows * cols, LANES), 0)
    shared_ref[rows * cols :, :] = jnp.where(row == 0, owner_row.astype(f32), 0.0)


def deposits(ints, settled, slots, blocks):
    rows, cols = settled.shape[:2]
    smem = pl.BlockSpec(memory_space=pltpu.SMEM)
    vmem = pl.BlockSpec(memory_space=pltpu.VMEM)
    return pl.pallas_call(
        deposit_kernel,
        out_shape=(
            jax.ShapeDtypeStruct((rows * cols, LANES), f32),
            jax.ShapeDtypeStruct((ROWS_OUT, LANES), f32),
        ),
        in_specs=[smem, vmem, vmem, vmem],
        out_specs=(vmem, vmem),
        compiler_params=pltpu.CompilerParams(vmem_limit_bytes=4 * MIB),
        name="deposits",
    )(ints, settled, slots, blocks)


def matching(heights, groups, axis, odd, wrap):
    size = heights if axis == "height" else groups
    pairs = []
    for h in range(heights):
        for c in range(groups):
            i = h if axis == "height" else c
            j = i ^ 1 if not odd else (i + 1 if i % 2 else i - 1)
            if 0 <= j < size or wrap:
                j = j % size
                target = (j, c) if axis == "height" else (h, j)
            else:
                target = (h, c ^ 1) if axis == "height" else (h ^ 1, c)
            pairs.append((h * groups + c, target[0] * groups + target[1]))
    return pairs


def around_pairs(heights, groups):
    pairs = []
    for h in range(heights):
        for c in range(groups):
            target = (heights - 1 - h, c) if h in (0, heights - 1) else (h, c ^ 1)
            pairs.append((h * groups + c, target[0] * groups + target[1]))
    return pairs


def exchanged(value, axis, wrap):
    heights, groups = lax.axis_size("height"), lax.axis_size("cols")
    return [
        lax.ppermute(value, ("height", "cols"), matching(heights, groups, axis, odd, wrap)) for odd in (False, True)
    ]


LINES = 32


def begin_kernel(zeros_ref):
    zeros_ref[...] = jnp.zeros_like(zeros_ref)


def begun_zeros():
    return pl.pallas_call(
        begin_kernel,
        out_shape=jax.ShapeDtypeStruct((8, LANES), f32),
        out_specs=pl.BlockSpec(memory_space=pltpu.VMEM),
        cost_estimate=pl.CostEstimate(flops=10**10, bytes_accessed=4096, transcendentals=0),
        compiler_params=pltpu.CompilerParams(vmem_limit_bytes=MIB),
        name="begin",
    )()


def pack_kernel(
    zeros_ref, exits_hbm, owners_hbm, inlets_hbm, positions_hbm, velocities_hbm, contacts_hbm, slots_hbm, gas_hbm, diagonal_hbm,
    first_ref, second_ref, flags_ref, ints_ref, slots_ref, state_ref, cells_ref,
    sides, wide_flags, contacts_ref, exits_ref, owners_ref, inlets_ref, arrived,
):
    rows, cols = state_ref.shape[1:3]
    _, levels, across, along = cells_ref.shape
    pairs = (
        (positions_hbm, state_ref.at[0:3]),
        (velocities_hbm, state_ref.at[3:6]),
        (gas_hbm, cells_ref.at[0]),
        (diagonal_hbm, cells_ref.at[1]),
        (contacts_hbm, contacts_ref),
        (exits_hbm, exits_ref),
        (owners_hbm, owners_ref),
        (inlets_hbm, inlets_ref),
        (slots_hbm, slots_ref),
    )
    copies = [pltpu.make_async_copy(source, target, arrived.at[n]) for n, (source, target) in enumerate(pairs)]
    for copy in copies:
        copy.start()
    sides[...] = jnp.zeros_like(sides) + zeros_ref[0:1]
    wide_flags[...] = jnp.zeros_like(wide_flags)
    for copy in copies:
        copy.wait()
    lane = lax.broadcasted_iota(i32, (1, LANES), 1)
    ints = jnp.zeros((1, LANES), i32)
    for r in range(rows):
        for c in range(cols):
            ints = jnp.where(lane == EXITS + r * cols + c, exits_ref[r, c], ints)
            ints = jnp.where(lane == OWNERS + r * cols + c, owners_ref[r, c], ints)
    for c in range(cols):
        ints = jnp.where(lane == INLETS + c, inlets_ref[0, c], ints)
    ints_ref[...] = ints
    wide_flags[:, :, 0 : contacts_ref.shape[2]] = contacts_ref[...].astype(f32)
    flags = []
    for r in range(rows):
        spread = pltpu.roll(wide_flags[r], 0, 1, stride=FLAG_LANES, stride_axis=0)
        flags.append(jnp.sum(spread, axis=0, keepdims=True))
        flags_ref[r : r + 1] = flags[r]
    for side in range(2):
        shown = jnp.zeros((1, LANES), f32)
        for r in range(rows):
            for k in range(DEPTH):
                c = k if side == 0 else cols - DEPTH + k
                for d in range(6):
                    row = d * rows * DEPTH + r * DEPTH + k
                    sides[side, row : row + 1] = state_ref[d, r, c : c + 1]
            turn = (r * DEPTH - (0 if side == 0 else cols - DEPTH)) * FLAG_LANES
            part = pltpu.roll(flags[r], turn % LANES, 1)
            shown = jnp.where(lane // (DEPTH * FLAG_LANES) == r, part, shown)
        sides[side, 6 * rows * DEPTH : 6 * rows * DEPTH + 1] = shown
        for z in range(levels):
            for k in range(2):
                x = k if side == 0 else across - 2 + k
                for kind in range(2):
                    for q in range(along // LANES):
                        row = LINES + ((z * 2 + k) * 2 + kind) * (along // LANES) + q
                        sides[side, row : row + 1] = cells_ref[kind, z, x : x + 1, q * LANES : (q + 1) * LANES]
    even = position()[5]
    first_ref[...] = jnp.where(even, sides[1], sides[0])
    second_ref[...] = jnp.where(even, sides[0], sides[1])


def packed(exits, owners, inlets, positions, velocities, contacts, slots, gas, diagonal):
    levels, across, along = gas.shape
    rows, cols = positions.shape[1:3]
    side = jax.ShapeDtypeStruct((LINES + levels * 4 * (along // LANES), LANES), f32)
    vmem = pl.BlockSpec(memory_space=pltpu.VMEM)
    return pl.pallas_call(
        pack_kernel,
        out_shape=(
            side,
            side,
            jax.ShapeDtypeStruct((rows, LANES), f32),
            jax.ShapeDtypeStruct((1, LANES), i32),
            jax.ShapeDtypeStruct(slots.shape, i32),
            jax.ShapeDtypeStruct((6, rows, cols, LANES), f32),
            jax.ShapeDtypeStruct((2, levels, across, along), f32),
        ),
        in_specs=[vmem] + [pl.BlockSpec(memory_space=pl.ANY)] * 9,
        out_specs=(vmem,) * 7,
        scratch_shapes=[
            pltpu.VMEM((2, *side.shape), f32),
            pltpu.VMEM((rows, cols, LANES), f32),
            pltpu.VMEM(contacts.shape, i32),
            pltpu.SMEM(exits.shape, i32),
            pltpu.SMEM(owners.shape, i32),
            pltpu.SMEM(inlets.shape, i32),
            pltpu.SemaphoreType.DMA((9,)),
        ],
        compiler_params=pltpu.CompilerParams(vmem_limit_bytes=8 * MIB),
        name="pack",
    )(begun_zeros(), exits, owners, inlets, positions, velocities, contacts, slots, gas, diagonal)


def merge_kernel(state_ref, flags_ref, line_a, line_b, window_ref):
    rows, cols = state_ref.shape[1:3]
    each = rows * (cols + 2 * DEPTH)
    count = 6 * rows * DEPTH
    left, right, _, _, _, even = position()
    one, two = line_a[0 : count + 8], line_b[0 : count + 8]
    low = jnp.where(left, jnp.where(even, two, one), 0.0)
    top = jnp.where(right, jnp.where(even, one, two), 0.0)
    for d in range(6):
        for r in range(rows):
            window_ref[d * each + r * cols : d * each + (r + 1) * cols] = state_ref[d, r]
        at = d * each + rows * cols
        piece = slice(d * rows * DEPTH, (d + 1) * rows * DEPTH)
        window_ref[at : at + rows * DEPTH] = low[piece]
        window_ref[at + rows * DEPTH : at + 2 * rows * DEPTH] = top[piece]
    window_ref[6 * each : 6 * each + 8] = jnp.concatenate(
        [flags_ref[...], low[count : count + 1], top[count : count + 1], jnp.zeros((6 - rows, LANES), f32)], axis=0
    )


def merged(state, flags, lines):
    rows, cols = state.shape[1:3]
    vmem = pl.BlockSpec(memory_space=pltpu.VMEM)
    return pl.pallas_call(
        merge_kernel,
        out_shape=jax.ShapeDtypeStruct((6 * rows * (cols + 2 * DEPTH) + 8, LANES), f32),
        in_specs=[vmem] * 4,
        out_specs=vmem,
        compiler_params=pltpu.CompilerParams(vmem_limit_bytes=4 * MIB),
        name="merge",
    )(state, flags, *lines)


def line_at(lines, z, k, kind, q, quarters):
    row = LINES + ((z * 2 + k) * 2 + kind) * quarters + q
    return lines[row : row + 1]


def faces_kernel(cells_ref, line_a, line_b, scaling_ref, blocks_ref, first_ref, second_ref):
    _, levels, across, along = cells_ref.shape
    quarters = along // LANES
    left, right, _, _, even, even_c = position()
    row = lax.broadcasted_iota(i32, (across, along), 0)
    place = lax.broadcasted_iota(i32, (across, along), 1)
    scaled = []
    for z in range(levels):
        scaling_ref[z] = 1.0 / (6.0 + cells_ref[1, z])
        scaled.append(scaling_ref[z] * cells_ref[0, z])
        for q in range(quarters):
            blocks_ref[q, z * across : (z + 1) * across] = scaling_ref[z, :, q * LANES : (q + 1) * LANES]
    faces = []
    for z in range(levels):
        ends = []
        for k, present, flip in ((1, left, False), (0, right, True)):
            parts = []
            for q in range(quarters):
                kinds = []
                for kind in range(2):
                    one, two = (line_at(lines, z, k, kind, q, quarters) for lines in (line_a, line_b))
                    kinds.append(jnp.where(even_c, one, two) if flip else jnp.where(even_c, two, one))
                parts.append(jnp.where(present, kinds[0] / (6.0 + kinds[1]), 0.0))
            ends.append(jnp.concatenate(parts, axis=1))
        mid = scaled[z]
        total = scaled[levels - 1 - z]
        total = total + jnp.where(row > 0, pltpu.roll(mid, 1, 0), ends[0])
        total = total + jnp.where(row < across - 1, pltpu.roll(mid, across - 1, 0), ends[1])
        total = total + jnp.where(place > 0, pltpu.roll(mid, 1, 1), 0.0)
        total = total + jnp.where(place < along - 1, pltpu.roll(mid, along - 1, 1), 0.0)
        outer = jnp.concatenate([*ends, jnp.zeros((6, along), f32)], axis=0)
        faces.append((scaling_ref[z], mid, total, outer))
    for n in range(4):
        bottom, top = faces[0][n], faces[levels - 1][n]
        at = slice(n * across, n * across + bottom.shape[0])
        first_ref[at] = jnp.where(even, top, bottom)
        second_ref[at] = jnp.where(even, bottom, top)


def faces_of(cells, lines):
    _, levels, across, along = cells.shape
    vmem = pl.BlockSpec(memory_space=pltpu.VMEM)
    face = jax.ShapeDtypeStruct((3 * across + 8, along), f32)
    return pl.pallas_call(
        faces_kernel,
        out_shape=(
            jax.ShapeDtypeStruct((levels, across, along), f32),
            jax.ShapeDtypeStruct((along // LANES, levels * across, LANES), f32),
            face,
            face,
        ),
        in_specs=[vmem] * 3,
        out_specs=(vmem,) * 4,
        compiler_params=pltpu.CompilerParams(vmem_limit_bytes=8 * MIB),
        name="faces",
    )(cells, *lines)


def right_side_kernel(
    own_ref, shared_ref, side_a, side_b, height_a, height_b, cells_ref, scaling_ref, line_a, line_b, face_a, face_b,
    rhs_ref, near_ref, far_ref, dots_ref, first, second,
):
    levels, across, along = scaling_ref.shape
    edge = 8
    wide = across + 2 * edge
    inner = slice(edge, edge + across)
    quarters = along // LANES
    left, right, below, above, even, even_c = position()

    def low_of(is_even, one, two):
        return jnp.where(is_even, two, one)

    def high_of(is_even, one, two):
        return jnp.where(is_even, one, two)

    lane = lax.broadcasted_iota(i32, (1, LANES), 1)
    tiles = 16
    shift_q, shift_x = quarters.bit_length() - 1, across.bit_length() - 1
    for level, choose, present in ((0, low_of, below), (levels, None, None), (2 * levels, high_of, above)):
        if choose is None:
            parts = [low_of(even_c, side_a[...], side_b[...]), shared_ref[...], high_of(even_c, side_a[...], side_b[...])]
            values = [parts[0][0:tiles], own_ref[...], parts[2][0:tiles]]
        else:
            block = [
                choose(even, height_a[k * ROWS_OUT : (k + 1) * ROWS_OUT], height_b[k * ROWS_OUT : (k + 1) * ROWS_OUT])
                for k in range(3)
            ]
            parts = [low_of(even_c, block[1], block[2]), block[0], high_of(even_c, block[1], block[2])]
            values = [part[0:tiles] for part in parts]
        code = jnp.full((1, LANES), -1, i32)
        for n, part in enumerate(parts):
            owner = part[tiles : tiles + 1].astype(i32)
            x = ((owner >> shift_q) & (across - 1)) + (edge + (n - 1) * across)
            z = owner >> (shift_q + shift_x)
            here = ((lane >> 4) == n) | ((lane >> 4) == n + 3)
            here = here & (x >= edge - 2) & (x < edge + across + 2)
            if n == 0:
                here = here & left
            if n == 2:
                here = here & right
            if present is not None:
                here = here & present
            code = jnp.where(here, (z * wide + x) * quarters + (owner & (quarters - 1)), code)
        values = jnp.concatenate(values, axis=0)
        high = values.astype(bf16)
        low = (values - high.astype(f32)).astype(bf16)
        values = jnp.concatenate([high, low, jnp.zeros((LANES - 6 * tiles, LANES), bf16)], axis=0)
        spot = lax.broadcasted_iota(i32, (levels * wide, LANES), 0) * quarters
        for k in range(quarters):
            table = jnp.where(code == spot + k, 1.0, 0.0).astype(bf16)
            added = jnp.dot(table, values, preferred_element_type=f32)
            for z in range(levels):
                first[level + z, :, k * LANES : (k + 1) * LANES] = -added[z * wide : (z + 1) * wide]

    second[:, 0:edge, :] = jnp.zeros((3 * levels, edge, along), f32)
    second[:, edge + across :, :] = jnp.zeros((3 * levels, edge, along), f32)
    for z in range(levels):
        rhs = cells_ref[0, z] + first[levels + z, inner]
        rhs_ref[z] = rhs
        first[levels + z, inner] = scaling_ref[z] * rhs
        for choose, start, present, beside_at in ((low_of, edge - 2, left, 1), (high_of, edge + across, right, 0)):
            for k in range(2):
                x = slice(start + k, start + k + 1)
                for q in range(quarters):
                    part = slice(q * LANES, (q + 1) * LANES)
                    kinds = [
                        choose(even_c, *[line_at(lines, z, k, kind, q, quarters) for lines in (line_a, line_b)])
                        for kind in range(2)
                    ]
                    m = jnp.where(present, 1.0 / (6.0 + kinds[1]), 0.0)
                    first[levels + z, x, part] += m * kinds[0]
                    if k == beside_at:
                        second[levels + z, x, part] = m
    place = lax.broadcasted_iota(i32, (wide, along), 1)

    def beside(ref, z):
        mid = ref[z]
        total = ref[z - 1] + ref[z + 1] + pltpu.roll(mid, 1, 0) + pltpu.roll(mid, wide - 1, 0)
        total = total + jnp.where(place > 0, pltpu.roll(mid, 1, 1), 0.0)
        return total + jnp.where(place < along - 1, pltpu.roll(mid, along - 1, 1), 0.0)

    for z, choose, present in ((levels - 1, low_of, below), (2 * levels, high_of, above)):
        part = [slice(n * across, (n + 1) * across) for n in range(3)]
        near = beside(first, z)[inner] + choose(even, face_a[part[2]], face_b[part[2]])
        second[z, inner] = jnp.where(present, choose(even, face_a[part[0]], face_b[part[0]]) * near, 0.0)
        first[z, inner] += jnp.where(present, choose(even, face_a[part[1]], face_b[part[1]]), 0.0)
        for n, x in enumerate((edge - 1, edge + across)):
            line = slice(3 * across + n, 3 * across + n + 1)
            first[z, x : x + 1] += jnp.where(present, choose(even, face_a[line], face_b[line]), 0.0)

    dots = [jnp.zeros((8, LANES), f32)] * 4

    def folded(value):
        value = jnp.sum(value.reshape(across // 8, 8, along), axis=0)
        return sum(value[:, k * LANES : (k + 1) * LANES] for k in range(quarters))

    ends = (slice(0, edge), slice(edge + across, wide))
    for z in range(levels, 2 * levels):
        near = beside(first, z)
        for end in ends:
            second[z, end] = second[z, end] * near[end]
        near = near[inner]
        scaled = scaling_ref[z - levels] * near
        second[z, inner] = scaled
        near_ref[z - levels] = near
        start = first[z, inner]
        dots[0] = dots[0] + folded(start * rhs_ref[z - levels])
        dots[1] = dots[1] + folded(start * near)
        dots[2] = dots[2] + folded(scaled * near)
    for z in range(levels, 2 * levels):
        far = beside(second, z)[inner]
        far_ref[z - levels] = far
        dots[3] = dots[3] + folded(second[z, inner] * far)
    line = jnp.zeros((1, LANES), f32)
    for k in range(4):
        total = jnp.sum(jnp.sum(dots[k], axis=0, keepdims=True), axis=1, keepdims=True)
        line = jnp.where(lane == k, total, line)
    dots_ref[...] = jnp.broadcast_to(line, dots_ref.shape)


def right_side_of(own, shared, side, height, cells, scaling, lines, faces, devices):
    levels, across, along = scaling.shape
    vmem = pl.BlockSpec(memory_space=pltpu.VMEM)
    whole = pltpu.VMEM((3 * levels, across + 16, along), f32)
    return pl.pallas_call(
        right_side_kernel,
        out_shape=(jax.ShapeDtypeStruct(scaling.shape, f32),) * 3 + (jax.ShapeDtypeStruct((devices, LANES), f32),),
        in_specs=[vmem] * 12,
        out_specs=(vmem,) * 4,
        scratch_shapes=[whole] * 2,
        compiler_params=pltpu.CompilerParams(vmem_limit_bytes=16 * MIB),
        name="right_side",
    )(own, shared, *side, *height, cells, scaling, *lines, *faces)


def results_kernel(
    ints_ref, dots_ref, rhs_ref, near_ref, far_ref, scaling_ref, settled_ref,
    height_a, height_b, around_ref, positions_ref, velocities_ref, pressure_ref, residual_ref,
):
    rows, cols = settled_ref.shape[:2]
    _, _, below, _, even, _ = position()
    totals = jnp.sum(dots_ref[...], axis=0, keepdims=True)
    g00, g01, g11, g12 = [totals[:, k : k + 1] for k in range(4)]
    ratio = g01 / g00
    alpha = g00 / (g00 - g01)
    square = alpha * alpha
    renewed = square * (g11 - ratio * g01)
    beta = renewed / g00
    crossed = square * (ratio * ratio * g01 - 2.0 * ratio * g11 + g12)
    curvature = renewed - crossed - beta * renewed / alpha
    later = renewed / curvature
    one = alpha + later * (1.0 - alpha + beta)
    two = later * alpha
    for z in range(rhs_ref.shape[0]):
        m = scaling_ref[z]
        rhs, near = rhs_ref[z], near_ref[z]
        pressure_ref[z] = m * (one * rhs + two * near)
        residual_ref[z] = (1.0 - one) * rhs + (one - two) * near + two * far_ref[z]
    for r in range(1, rows):
        for c in range(cols):
            kept = jnp.where(ints_ref[0, EXITS + r * cols + c] > 0, 0.0, settled_ref[r, c])
            for d in range(3):
                positions_ref[d, r, c : c + 1] = kept[d : d + 1]
                velocities_ref[d, r, c : c + 1] = kept[d + 3 : d + 4]
    start = 3 * ROWS_OUT
    for d in range(6):
        block = slice(start + d * cols, start + (d + 1) * cols)
        tiles = jnp.where(even, height_b[block], height_a[block])
        target = positions_ref if d < 3 else velocities_ref
        for k in range(cols):
            target[d % 3, 0, pl.ds(ints_ref[0, INLETS + k], 1)] = tiles[k : k + 1]


def results_of(ints, dots, rhs, near, far, scaling, settled, height, around):
    rows, cols = settled.shape[:2]
    smem = pl.BlockSpec(memory_space=pltpu.SMEM)
    vmem = pl.BlockSpec(memory_space=pltpu.VMEM)
    particle = jax.ShapeDtypeStruct((3, rows, cols, LANES), f32)
    field = jax.ShapeDtypeStruct(rhs.shape, f32)
    return pl.pallas_call(
        results_kernel,
        out_shape=(particle, particle, field, field),
        in_specs=[smem] + [vmem] * 9,
        out_specs=(vmem,) * 4,
        compiler_params=pltpu.CompilerParams(vmem_limit_bytes=8 * MIB),
        name="results",
    )(ints, dots, rhs, near, far, scaling, settled, *height, around)


def on_device(
    positions, velocities, contacts, exit_flags, inlet_slots, cell_blocks, cell_slots, gas_source, diagonal
):
    heights, groups = lax.axis_size("height"), lax.axis_size("cols")
    h, c = lax.axis_index("height"), lax.axis_index("cols")
    *sides, flags, ints, slots, state, cells = packed(
        exit_flags, cell_blocks, inlet_slots, positions, velocities, contacts.transpose(1, 2, 0), cell_slots,
        gas_source, diagonal,
    )
    lines = [
        lax.ppermute(value, ("height", "cols"), matching(heights, groups, "cols", odd, True))
        for value, odd in zip(sides, (False, True))
    ]
    window = merged(state, flags, lines)
    beside = exchanged(window, "height", False)
    scaling, blocks, *faces = faces_of(cells, lines)
    faces, beside = lax.optimization_barrier((faces, beside))
    faces = [
        lax.ppermute(value, ("height", "cols"), matching(heights, groups, "height", odd, False))
        for value, odd in zip(faces, (False, True))
    ]
    settled, leaving = particles(ints, window, *beside, *state.shape[1:3])
    own, shared = deposits(ints, settled, slots, blocks)
    near = exchanged(shared, "cols", True)
    parcel = jnp.concatenate([shared, *near, leaving.reshape(-1, LANES)], axis=0)
    parcels = exchanged(parcel, "height", True)
    rhs, first, second, dots = right_side_of(
        own, shared, near, parcels, cells, scaling, lines, faces, heights * groups
    )
    dots = lax.all_to_all(dots, ("height", "cols"), 0, 0, tiled=True)
    return results_of(ints, dots, rhs, first, second, scaling, settled, parcels, leaving)


def solution(mesh):
    in_specs = (
        P(None, "height", "cols", None),
        P(None, "height", "cols", None),
        P(None, "height", "cols"),
        P("height", "cols"),
        P("height", "cols"),
        P("height", "cols"),
        P("height", "cols", None),
        P("height", "cols", None),
        P("height", "cols", None),
    )
    out_specs = (
        P(None, "height", "cols", None),
        P(None, "height", "cols", None),
        P("height", "cols", None),
        P("height", "cols", None),
    )
    return jax.shard_map(
        on_device, mesh=mesh, in_specs=in_specs, out_specs=out_specs, check_vma=False
    )
```

```python
import functools
import jax
import jax.numpy as jnp
from jax import lax
from jax.experimental import pallas as pl
from jax.experimental.pallas import tpu as pltpu
from jax.sharding import PartitionSpec as P

f32, bf16, i32 = jnp.float32, jnp.bfloat16, jnp.int32
spring = 0.05
cutoff_sq = 1.44
damping = 0.5
step_dt = 0.05
gravity = 1.0
deposit_gain = 2.0
LANES = 128
COMPS = 8
DEPTH = 2
ROWS_OUT = 24
FLAG_LANES = 16
MIB = 1024 * 1024
NEARS = 6
EXITS, OWNERS, INLETS = 0, 16, 32


def rounded(value):
    return value.astype(bf16).astype(f32)


def rounded_pair(value):
    high = rounded(value)
    return high, rounded(value - high)


def split(value):
    high = rounded(value)
    mid = rounded(value - high)
    return high, mid, value - high - mid


def centred(tile, r, c, rows, wide):
    row = lax.broadcasted_iota(i32, (COMPS, LANES), 0)
    side = jnp.float32(c - wide // 2)
    up = (r - rows // 2).astype(f32)
    return tile + jnp.where(row == 0, side, jnp.where(row == 2, up, 0.0))


def place_parts(tile, r, c, rows, wide):
    row = lax.broadcasted_iota(i32, (COMPS, LANES), 0)
    place = jnp.where(row < 3, centred(tile, r, c, rows, wide), 0.0)
    high, mid = rounded_pair(place)
    place = high + mid
    return high, mid, -jnp.sum(place * place, axis=0, keepdims=True)


def source_features(tile, r, c, rows, wide):
    row = lax.broadcasted_iota(i32, (COMPS, LANES), 0)
    row32 = lax.broadcasted_iota(i32, (32, LANES), 0)
    high, mid, size = place_parts(tile, r, c, rows, wide)
    size_high, size_mid, size_low = split(size)
    first = jnp.where(row < 3, high, 1.0)
    first = jnp.where(row == 3, size_high, jnp.where(row == 4, size_mid, jnp.where(row == 5, size_low, first)))
    second = jnp.where(row < 3, high, jnp.where(row == 3, 1.0, 0.0))
    kind = lax.rem(r, 3) * 4 + c % 4
    kind = kind + jnp.where(kind < 4, 12, jnp.where(kind < 9, 15, 18))
    near = jnp.concatenate([first, second, mid, mid], axis=0) + jnp.where(row32 == kind, 1.0, 0.0)
    high, mid, low = split(centred(tile, r, c, rows, wide) - damping * pltpu.roll(tile, 5, 0))
    first = jnp.where(row < 3, high, jnp.where(row == 3, 1.0, 0.0))
    second = jnp.where(row < 3, mid, jnp.where(row < 4, 0.0, pltpu.roll(low, 4, 0)))
    return near, jnp.concatenate([first, second], axis=0).astype(bf16)


def target_features(tile, r, c, rows, wide):
    row = lax.broadcasted_iota(i32, (COMPS, LANES), 0)
    row32 = lax.broadcasted_iota(i32, (32, LANES), 0)
    lane32 = lax.broadcasted_iota(i32, (32, LANES), 1)
    high, mid, size = place_parts(tile, r, c, rows, wide)
    own_high, own_mid, own_low = split(cutoff_sq + size)
    first = jnp.where(row < 3, 2.0 * high, jnp.where(row < 6, 1.0, jnp.where(row == 6, own_high, own_mid)))
    second = jnp.where(row < 3, 2.0 * mid, jnp.where(row == 3, own_low, 0.0))
    third = jnp.where(row < 3, 2.0 * high, 0.0)
    fourth = jnp.where(row < 3, 2.0 * mid, 0.0)
    kind = jnp.where(row32 < 16, row32 - 12, jnp.where(row32 < 24, row32 - 15, row32 - 18))
    is_kind = ((row32 >= 12) & (row32 < 16)) | ((row32 >= 19) & (row32 < 24)) | ((row32 >= 27) & (row32 < 30))
    kind_row = jnp.where(kind < 4, 0, jnp.where(kind < 8, 1, 2))
    up = kind_row + lax.rem(4 - lax.rem(r, 3), 3)
    up = jnp.where(up > 2, up - 3, up)
    side = kind - 4 * kind_row + (5 - c % 4) % 4
    side = jnp.where(side > 3, side - 4, side)
    if DEPTH <= c < wide - DEPTH:
        start = (c - DEPTH) * FLAG_LANES
    else:
        start = (lax.rem(r, DEPTH) * DEPTH + c % 2) * FLAG_LANES
    wanted = jnp.where(side < 3, 3 * up + side + start, LANES)
    flags = jnp.sum(jnp.where(lane32 == wanted, tile[6:7, :], 0.0), axis=1, keepdims=True)
    barred = jnp.where(is_kind, -1024.0 * (1.0 - flags), 0.0)
    return jnp.concatenate([first, second, third, fourth], axis=0) + barred


def unit_operands(tiles, r, c, rows, wide):
    features = [target_features(tile, r, c + k, rows, wide) for k, tile in enumerate(tiles)]
    features = jnp.concatenate(features, axis=1).astype(bf16)
    start = (c - 1) // 4
    ends = (c - 1, c + 2)

    def spread(part, s):
        at = 4 * (s // 4 - start) + s % 4
        return jnp.concatenate([part if k == at else jnp.zeros_like(part) for k in range(8)], axis=0)

    halves = [spread(features[:, k * LANES : (k + 1) * LANES], s) for k, s in enumerate(ends)]
    return [spread(features, c), spread(features, c + 1), jnp.concatenate(halves, axis=1)]


def pulls_row(tiles, r, columns, source_rows, rows, wide, turned, pulled, nears, founds):
    ahead = len(nears) - 1
    count = len(source_rows)
    units = [(pair, kind, i) for pair in range(len(columns)) for kind in range(3) for i in range(count)]
    blocks = wide // 4
    operands = [None] * len(columns)

    def begin(n):
        pair, kind, i = units[n]
        c = columns[pair]
        staged = (3 * pair + kind) % 2
        if i == 0:
            if kind == 0:
                operands[pair] = unit_operands(tiles[pair], r, c, rows, wide)
            pltpu.matmul_push_rhs(operands[pair][kind], staged, 0)
        start = (c - 1) // 4
        after = start + 1 if start + 1 < blocks else 0
        row = source_rows[i]
        sources = jnp.concatenate([turned(row)[start], turned(row)[after]], axis=1)
        pltpu.matmul_acc_lhs(nears[n % len(nears)], sources, load_staged_rhs=staged if i == 0 else None)

    def finish(n):
        pair, kind, i = units[n]
        c = columns[pair]
        weight = jnp.maximum(pltpu.matmul_pop(nears[n % len(nears)]), 0.0)
        high = weight.astype(bf16)
        low = (weight - high.astype(f32)).astype(bf16)
        pltpu.matmul_push_rhs(jnp.concatenate([high, low], axis=0), n % 2, 1)
        of_row = pulled(source_rows[i])
        if kind < 2:
            pulls = of_row[c + kind]
        else:
            pulls = jnp.concatenate([of_row[c - 1], of_row[c + 2]], axis=0)
        pulls = jnp.concatenate([pulls, pulls], axis=1)
        pltpu.matmul_acc_lhs(founds[2 * pair + (kind == 2)], pulls, load_staged_rhs=n % 2)

    for n in range(len(units) + ahead):
        if n < len(units):
            begin(n)
        if n >= ahead:
            finish(n - ahead)
    totals = []
    for pair in range(len(columns)):
        inner, outer = pltpu.matmul_pop(founds[2 * pair]), pltpu.matmul_pop(founds[2 * pair + 1])
        totals.append(inner + jnp.concatenate([outer[0:16, 0:LANES], outer[16:32, LANES:]], axis=1))
    return totals


def forces_of(totals, tiles, r, columns, rows, wide):
    forces = []
    for pair, c in enumerate(columns):
        for k, tile in enumerate(tiles[pair]):
            total = totals[pair][:, k * LANES : (k + 1) * LANES]
            first, second = total[0:8], total[8:16]
            moving = centred(tile, r, c + k, rows, wide) - damping * pltpu.roll(tile, 5, 0)
            forces.append((spring / cutoff_sq) * (moving * first[3:4, :] - first - second - pltpu.roll(second, 4, 0)))
    return forces


def stepped(tile, force):
    row = lax.broadcasted_iota(i32, (COMPS, LANES), 0)
    change = step_dt * force - jnp.where(row == 2, step_dt * gravity, 0.0)
    speeds = tile + pltpu.roll(change, 3, 0)
    places = tile + step_dt * pltpu.roll(speeds, 5, 0)
    return jnp.where(row < 3, places, jnp.where(row < 6, speeds, tile))


def position():
    heights, groups = lax.axis_size("height"), lax.axis_size("cols")
    h, c = lax.axis_index("height"), lax.axis_index("cols")
    return c > 0, c < groups - 1, h > 0, h < heights - 1, lax.rem(h, 2) == 0, lax.rem(c, 2) == 0


def halo_rows(rows, cols, d, r, c):
    wide = cols + 2 * DEPTH
    start = d * rows * wide
    if c < DEPTH:
        return start + rows * cols + r * DEPTH + c
    if c >= cols + DEPTH:
        return start + rows * (cols + DEPTH) + r * DEPTH + c - cols - DEPTH
    return start + r * cols + c - DEPTH


def tiles_of_block(block, place, rows, cols):
    wide = cols + 2 * DEPTH
    flag_row = 6 * rows * wide
    for r in range(rows):
        for c in range(wide):
            for d in range(6):
                row = halo_rows(rows, cols, d, r, c)
                place(r, c, d, block[row : row + 1])
            row = flag_row + (rows if c < DEPTH else rows + 1 if c >= cols + DEPTH else r)
            place(r, c, 6, block[row : row + 1])
            place(r, c, 7, jnp.zeros((1, LANES), f32))


def fill_row(tile_at, r, high, wide, turned_row, pulled_row):
    for block in range(wide // 4):
        near = []
        for c in range(4 * block, 4 * block + 4):
            places, moving = source_features(tile_at(c), r, c, high, wide)
            near.append(places)
            pulled_row[c] = moving
        turned_row[block] = jnp.concatenate(near, axis=0).T.astype(bf16)


def accumulators(wide):
    return (
        *[pltpu.ACC(0)((LANES, 2 * LANES), f32)] * NEARS,
        *[pltpu.ACC(1)((held, 2 * LANES), f32) for _ in range(wide // 2 - 1) for held in (16, 32)],
    )


def emptied(refs):
    for ref in refs:
        pltpu.matmul_pop(ref)
    return refs[:NEARS], refs[NEARS:]


def own_kernel(own_ref, state_ref, turned_ref, pulled_ref, partial_ref, *, rows, cols):
    wide = cols + 2 * DEPTH
    high = rows + 2 * DEPTH
    columns = list(range(1, wide - 1, 2))

    def place(r, c, d, value):
        state_ref[r, c, d : d + 1] = value

    tiles_of_block(own_ref, place, rows, cols)

    def one_row(r, carry):
        fill_row(lambda c: state_ref[r, c], r + DEPTH, high, wide, turned_ref.at[r], pulled_ref.at[r])
        return carry

    lax.fori_loop(0, rows, one_row, 0)

    def sums(*refs):
        nears, founds = emptied(refs)

        def one_sum(r, carry):
            tiles = [[state_ref[r, c], state_ref[r, c + 1]] for c in columns]
            totals = pulls_row(
                tiles, r + DEPTH, columns, list(range(rows)), high, wide,
                lambda row: turned_ref.at[row], lambda row: pulled_ref.at[row], nears, founds,
            )
            for pair, total in enumerate(totals):
                partial_ref[r, pair] = total
            return carry

        lax.fori_loop(0, rows, one_sum, 0)

    pl.run_scoped(sums, *accumulators(wide))


def own_sums(own, rows, cols):
    wide = cols + 2 * DEPTH
    vmem = pl.BlockSpec(memory_space=pltpu.VMEM)
    return pl.pallas_call(
        functools.partial(own_kernel, rows=rows, cols=cols),
        out_shape=(
            jax.ShapeDtypeStruct((rows, wide, COMPS, LANES), f32),
            jax.ShapeDtypeStruct((rows, wide // 4, LANES, LANES), bf16),
            jax.ShapeDtypeStruct((rows, wide, 16, LANES), bf16),
            jax.ShapeDtypeStruct((rows, wide // 2 - 1, 16, 2 * LANES), f32),
        ),
        in_specs=[vmem],
        out_specs=(vmem,) * 4,
        cost_estimate=pl.CostEstimate(flops=4 * 10**9, bytes_accessed=4096, transcendentals=0),
        compiler_params=pltpu.CompilerParams(vmem_limit_bytes=8 * MIB),
        name="own_sums",
    )(own)


def particles_kernel(
    ints_ref, first_ref, second_ref, own_ref, own_turned, own_pulled, partial_ref,
    settled_ref, leaving_ref, state, turned, pulled, begun, blocks,
    *, rows, cols,
):
    wide = cols + 2 * DEPTH
    high = rows + 2 * DEPTH
    left, right, below, above, even, _ = position()
    one, two = first_ref[...], second_ref[...]
    blocks[0] = jnp.where(below, jnp.where(even, two, one), 0.0)
    blocks[1] = jnp.where(above, jnp.where(even, one, two), 0.0)
    for half, start in ((0, 0), (1, rows + DEPTH)):

        def place(r, c, d, value, start=start):
            state[start + r, c, d : d + 1] = value

        tiles_of_block(blocks.at[half], place, rows, cols)

    def far_row(n, carry):
        r = n + jnp.where(n >= DEPTH, rows, 0)
        fill_row(lambda c: state[r, c], r, high, wide, turned.at[r], pulled.at[r])
        return carry

    lax.fori_loop(0, 2 * DEPTH, far_row, 0)
    for r in range(rows):
        state[DEPTH + r] = own_ref[r]
        turned[DEPTH + r] = own_turned[r]
        pulled[DEPTH + r] = own_pulled[r]

    def substeps(*refs):
        nears, founds = emptied(refs)
        sources = dict(turned=lambda row: turned.at[row], pulled=lambda row: pulled.at[row], nears=nears, founds=founds)
        columns = list(range(1, wide - 1, 2))

        def begin_row(r, totals):
            tiles = [[state[r, c], state[r, c + 1]] for c in columns]
            forces = forces_of(totals, tiles, r, columns, high, wide)
            begun[r, 0] = jnp.zeros((COMPS, LANES), f32)
            begun[r, wide - 1] = jnp.zeros((COMPS, LANES), f32)
            for c in range(1, wide - 1):
                inside = ((r >= DEPTH) | below) & ((r < rows + DEPTH) | above)
                if c < DEPTH:
                    inside = inside & left
                if c >= cols + DEPTH:
                    inside = inside & right
                begun[r, c] = jnp.where(inside, stepped(tiles[(c - 1) // 2][(c - 1) % 2], forces[c - 1]), 0.0)

        def outer_step(n, carry):
            r = 1 + n * (rows + 1)
            tiles = [[state[r, c], state[r, c + 1]] for c in columns]
            begin_row(r, pulls_row(tiles, r, columns, [r - 1, r, r + 1], high, wide, **sources))
            return carry

        def inner_step(n, carry):
            r = DEPTH + n * (rows - 1)
            tiles = [[state[r, c], state[r, c + 1]] for c in columns]
            totals = pulls_row(tiles, r, columns, [1 + n * (rows + 1)], high, wide, **sources)
            begin_row(r, [total + partial_ref[n * (rows - 1), pair] for pair, total in enumerate(totals)])
            return carry

        lax.fori_loop(0, 2, inner_step, 0)
        lax.fori_loop(0, 2, outer_step, 0)

        def begun_row(r, carry):
            fill_row(lambda c: begun[r, c], r, high, wide, turned.at[r], pulled.at[r])
            return carry

        lax.fori_loop(1, high - 1, begun_row, 0)

        def second_step(r, carry):
            columns = list(range(DEPTH, DEPTH + cols, 2))
            tiles = [[begun[r, c], begun[r, c + 1]] for c in columns]
            totals = pulls_row(tiles, r, columns, [r - 1, r, r + 1], high, wide, **sources)
            forces = forces_of(totals, tiles, r, columns, high, wide)
            for c in range(cols):
                settled_ref[r - DEPTH, c] = stepped(tiles[c // 2][c % 2], forces[c])
            return carry

        lax.fori_loop(DEPTH, DEPTH + rows, second_step, 0)

    pl.run_scoped(substeps, *accumulators(wide))

    leaving_ref[...] = jnp.zeros_like(leaving_ref)
    count = jnp.int32(0)
    for t in range(rows * cols):
        flag = ints_ref[0, EXITS + t]

        @pl.when((flag > 0) & (count < cols))
        def _(t=t, count=count):
            for d in range(6):
                leaving_ref[d, pl.ds(count, 1)] = settled_ref[t // cols, t % cols, d : d + 1]

        count = count + flag


def particles(ints, first, second, own):
    rows, wide = own[0].shape[:2]
    cols, high = wide - 2 * DEPTH, rows + 2 * DEPTH
    smem = pl.BlockSpec(memory_space=pltpu.SMEM)
    vmem = pl.BlockSpec(memory_space=pltpu.VMEM)
    return pl.pallas_call(
        functools.partial(particles_kernel, rows=rows, cols=cols),
        out_shape=(
            jax.ShapeDtypeStruct((rows, cols, COMPS, LANES), f32),
            jax.ShapeDtypeStruct((6, cols, LANES), f32),
        ),
        in_specs=[smem] + [vmem] * 6,
        out_specs=(vmem, vmem),
        scratch_shapes=[
            pltpu.VMEM((high, wide, COMPS, LANES), f32),
            pltpu.VMEM((high, wide // 4, LANES, LANES), bf16),
            pltpu.VMEM((high, wide, 16, LANES), bf16),
            pltpu.VMEM((high, wide, COMPS, LANES), f32),
            pltpu.VMEM((2, *first.shape), f32),
        ],
        cost_estimate=pl.CostEstimate(flops=10**10, bytes_accessed=4096, transcendentals=0),
        compiler_params=pltpu.CompilerParams(vmem_limit_bytes=12 * MIB),
        name="particles",
    )(ints, first, second, *own)


def deposit_kernel(ints_ref, settled_ref, slots_ref, blocks_ref, own_ref, shared_ref):
    rows, cols = settled_ref.shape[:2]
    quarters = blocks_ref.shape[0]
    row = lax.broadcasted_iota(i32, (16, LANES), 0)
    cell = lax.broadcasted_iota(i32, (LANES, LANES), 0)
    lane = lax.broadcasted_iota(i32, (1, LANES), 1)
    owner_row = jnp.zeros((1, LANES), i32)
    for t in range(rows * cols):
        r, c = t // cols, t % cols
        owner = ints_ref[0, OWNERS + t]
        owner_row = jnp.where(lax.rem(lane, rows * cols) == t, owner, owner_row)
        lift_high, lift_mid, lift_low = split(deposit_gain * settled_ref[r, c, 5:6, :])
        parts = jnp.where(row == 0, lift_high, jnp.where(row == 1, lift_mid, jnp.where(row == 2, lift_low, 0.0)))
        table = jnp.where(cell == slots_ref[r, c : c + 1, :], 1.0, 0.0).astype(bf16)
        gathered = lax.dot_general(parts.astype(bf16), table, (((1,), (1,)), ((), ())), preferred_element_type=f32)
        sums = jnp.sum(gathered, axis=0, keepdims=True)
        own_ref[t : t + 1, :] = sums
        shared_ref[t : t + 1, :] = blocks_ref[owner % quarters, pl.ds(owner // quarters, 1), :] * sums
    row = lax.broadcasted_iota(i32, (ROWS_OUT - rows * cols, LANES), 0)
    shared_ref[rows * cols :, :] = jnp.where(row == 0, owner_row.astype(f32), 0.0)


def deposits(ints, settled, slots, blocks):
    rows, cols = settled.shape[:2]
    smem = pl.BlockSpec(memory_space=pltpu.SMEM)
    vmem = pl.BlockSpec(memory_space=pltpu.VMEM)
    return pl.pallas_call(
        deposit_kernel,
        out_shape=(
            jax.ShapeDtypeStruct((rows * cols, LANES), f32),
            jax.ShapeDtypeStruct((ROWS_OUT, LANES), f32),
        ),
        in_specs=[smem, vmem, vmem, vmem],
        out_specs=(vmem, vmem),
        compiler_params=pltpu.CompilerParams(vmem_limit_bytes=4 * MIB),
        name="deposits",
    )(ints, settled, slots, blocks)


def matching(heights, groups, axis, odd, wrap):
    size = heights if axis == "height" else groups
    pairs = []
    for h in range(heights):
        for c in range(groups):
            i = h if axis == "height" else c
            j = i ^ 1 if not odd else (i + 1 if i % 2 else i - 1)
            if 0 <= j < size or wrap:
                j = j % size
                target = (j, c) if axis == "height" else (h, j)
            else:
                target = (h, c ^ 1) if axis == "height" else (h ^ 1, c)
            pairs.append((h * groups + c, target[0] * groups + target[1]))
    return pairs


def around_pairs(heights, groups):
    pairs = []
    for h in range(heights):
        for c in range(groups):
            target = (heights - 1 - h, c) if h in (0, heights - 1) else (h, c ^ 1)
            pairs.append((h * groups + c, target[0] * groups + target[1]))
    return pairs


def exchanged(value, axis, wrap):
    heights, groups = lax.axis_size("height"), lax.axis_size("cols")
    return [
        lax.ppermute(value, ("height", "cols"), matching(heights, groups, axis, odd, wrap)) for odd in (False, True)
    ]


LINES = 32


def begin_kernel(zeros_ref):
    zeros_ref[...] = jnp.zeros_like(zeros_ref)


def begun_zeros():
    return pl.pallas_call(
        begin_kernel,
        out_shape=jax.ShapeDtypeStruct((8, LANES), f32),
        out_specs=pl.BlockSpec(memory_space=pltpu.VMEM),
        cost_estimate=pl.CostEstimate(flops=10**10, bytes_accessed=4096, transcendentals=0),
        compiler_params=pltpu.CompilerParams(vmem_limit_bytes=MIB),
        name="begin",
    )()


def pack_kernel(
    zeros_ref, exits_ref, owners_ref, inlets_ref, positions_ref, velocities_ref, contacts_ref, slots_in, gas_ref,
    diagonal_ref, first_ref, second_ref, flags_ref, ints_ref, slots_ref, state_ref, cells_ref, sides, wide_flags, small,
):
    rows, cols = state_ref.shape[1:3]
    _, levels, across, along = cells_ref.shape
    lane = lax.broadcasted_iota(i32, (1, LANES), 1)
    sides[...] = jnp.zeros_like(sides) + zeros_ref[0:1]
    wide_flags[...] = jnp.zeros_like(wide_flags)
    small[...] = jnp.zeros_like(small)
    state_ref[0:3] = positions_ref[...]
    state_ref[3:6] = velocities_ref[...]
    cells_ref[0] = gas_ref[...]
    cells_ref[1] = diagonal_ref[...]
    slots_ref[...] = slots_in[...]
    small[0:rows, 0:cols] = exits_ref[...]
    small[rows : 2 * rows, 0:cols] = owners_ref[...]
    small[2 * rows : 2 * rows + 1, 0:cols] = inlets_ref[...]
    ints = jnp.zeros((1, LANES), i32)
    for r in range(rows):
        ints = ints + pltpu.roll(small[r : r + 1], EXITS + r * cols, 1)
        ints = ints + pltpu.roll(small[rows + r : rows + r + 1], OWNERS + r * cols, 1)
    ints_ref[...] = ints + pltpu.roll(small[2 * rows : 2 * rows + 1], INLETS, 1)
    wide_flags[:, :, 0 : contacts_ref.shape[2]] = contacts_ref[...].astype(f32)
    flags = []
    for r in range(rows):
        spread = pltpu.roll(wide_flags[r], 0, 1, stride=FLAG_LANES, stride_axis=0)
        flags.append(jnp.sum(spread, axis=0, keepdims=True))
        flags_ref[r : r + 1] = flags[r]
    for side in range(2):
        shown = jnp.zeros((1, LANES), f32)
        for r in range(rows):
            for k in range(DEPTH):
                c = k if side == 0 else cols - DEPTH + k
                for d in range(6):
                    row = d * rows * DEPTH + r * DEPTH + k
                    sides[side, row : row + 1] = state_ref[d, r, c : c + 1]
            turn = (r * DEPTH - (0 if side == 0 else cols - DEPTH)) * FLAG_LANES
            part = pltpu.roll(flags[r], turn % LANES, 1)
            shown = jnp.where(lane // (DEPTH * FLAG_LANES) == r, part, shown)
        sides[side, 6 * rows * DEPTH : 6 * rows * DEPTH + 1] = shown
        for z in range(levels):
            for k in range(2):
                x = k if side == 0 else across - 2 + k
                for kind in range(2):
                    for q in range(along // LANES):
                        row = LINES + ((z * 2 + k) * 2 + kind) * (along // LANES) + q
                        sides[side, row : row + 1] = cells_ref[kind, z, x : x + 1, q * LANES : (q + 1) * LANES]
    even = position()[5]
    first_ref[...] = jnp.where(even, sides[1], sides[0])
    second_ref[...] = jnp.where(even, sides[0], sides[1])


def packed(exits, owners, inlets, positions, velocities, contacts, slots, gas, diagonal):
    levels, across, along = gas.shape
    rows, cols = positions.shape[1:3]
    side = jax.ShapeDtypeStruct((LINES + levels * 4 * (along // LANES), LANES), f32)
    vmem = pl.BlockSpec(memory_space=pltpu.VMEM)
    return pl.pallas_call(
        pack_kernel,
        out_shape=(
            side,
            side,
            jax.ShapeDtypeStruct((rows, LANES), f32),
            jax.ShapeDtypeStruct((1, LANES), i32),
            jax.ShapeDtypeStruct(slots.shape, i32),
            jax.ShapeDtypeStruct((6, rows, cols, LANES), f32),
            jax.ShapeDtypeStruct((2, levels, across, along), f32),
        ),
        in_specs=[vmem] * 10,
        out_specs=(vmem,) * 7,
        scratch_shapes=[
            pltpu.VMEM((2, *side.shape), f32),
            pltpu.VMEM((rows, cols, LANES), f32),
            pltpu.VMEM((8, LANES), i32),
        ],
        compiler_params=pltpu.CompilerParams(vmem_limit_bytes=8 * MIB),
        name="pack",
    )(begun_zeros(), exits, owners, inlets, positions, velocities, contacts, slots, gas, diagonal)


def merge_kernel(state_ref, flags_ref, line_a, line_b, window_ref):
    rows, cols = state_ref.shape[1:3]
    each = rows * (cols + 2 * DEPTH)
    count = 6 * rows * DEPTH
    left, right, _, _, _, even = position()
    one, two = line_a[0 : count + 8], line_b[0 : count + 8]
    low = jnp.where(left, jnp.where(even, two, one), 0.0)
    top = jnp.where(right, jnp.where(even, one, two), 0.0)
    for d in range(6):
        for r in range(rows):
            window_ref[d * each + r * cols : d * each + (r + 1) * cols] = state_ref[d, r]
        at = d * each + rows * cols
        piece = slice(d * rows * DEPTH, (d + 1) * rows * DEPTH)
        window_ref[at : at + rows * DEPTH] = low[piece]
        window_ref[at + rows * DEPTH : at + 2 * rows * DEPTH] = top[piece]
    window_ref[6 * each : 6 * each + 8] = jnp.concatenate(
        [flags_ref[...], low[count : count + 1], top[count : count + 1], jnp.zeros((6 - rows, LANES), f32)], axis=0
    )


def merged(state, flags, lines):
    rows, cols = state.shape[1:3]
    vmem = pl.BlockSpec(memory_space=pltpu.VMEM)
    return pl.pallas_call(
        merge_kernel,
        out_shape=jax.ShapeDtypeStruct((6 * rows * (cols + 2 * DEPTH) + 8, LANES), f32),
        in_specs=[vmem] * 4,
        out_specs=vmem,
        compiler_params=pltpu.CompilerParams(vmem_limit_bytes=4 * MIB),
        name="merge",
    )(state, flags, *lines)


def line_at(lines, z, k, kind, q, quarters):
    row = LINES + ((z * 2 + k) * 2 + kind) * quarters + q
    return lines[row : row + 1]


def faces_kernel(cells_ref, line_a, line_b, scaling_ref, blocks_ref, first_ref, second_ref):
    _, levels, across, along = cells_ref.shape
    quarters = along // LANES
    left, right, _, _, even, even_c = position()
    row = lax.broadcasted_iota(i32, (across, along), 0)
    place = lax.broadcasted_iota(i32, (across, along), 1)
    scaled = []
    for z in range(levels):
        scaling_ref[z] = 1.0 / (6.0 + cells_ref[1, z])
        scaled.append(scaling_ref[z] * cells_ref[0, z])
        for q in range(quarters):
            blocks_ref[q, z * across : (z + 1) * across] = scaling_ref[z, :, q * LANES : (q + 1) * LANES]
    faces = []
    for z in range(levels):
        ends = []
        for k, present, flip in ((1, left, False), (0, right, True)):
            parts = []
            for q in range(quarters):
                kinds = []
                for kind in range(2):
                    one, two = (line_at(lines, z, k, kind, q, quarters) for lines in (line_a, line_b))
                    kinds.append(jnp.where(even_c, one, two) if flip else jnp.where(even_c, two, one))
                parts.append(jnp.where(present, kinds[0] / (6.0 + kinds[1]), 0.0))
            ends.append(jnp.concatenate(parts, axis=1))
        mid = scaled[z]
        total = scaled[levels - 1 - z]
        total = total + jnp.where(row > 0, pltpu.roll(mid, 1, 0), ends[0])
        total = total + jnp.where(row < across - 1, pltpu.roll(mid, across - 1, 0), ends[1])
        total = total + jnp.where(place > 0, pltpu.roll(mid, 1, 1), 0.0)
        total = total + jnp.where(place < along - 1, pltpu.roll(mid, along - 1, 1), 0.0)
        outer = jnp.concatenate([*ends, jnp.zeros((6, along), f32)], axis=0)
        faces.append((scaling_ref[z], mid, total, outer))
    for n in range(4):
        bottom, top = faces[0][n], faces[levels - 1][n]
        at = slice(n * across, n * across + bottom.shape[0])
        first_ref[at] = jnp.where(even, top, bottom)
        second_ref[at] = jnp.where(even, bottom, top)


def faces_of(cells, lines):
    _, levels, across, along = cells.shape
    vmem = pl.BlockSpec(memory_space=pltpu.VMEM)
    face = jax.ShapeDtypeStruct((3 * across + 8, along), f32)
    return pl.pallas_call(
        faces_kernel,
        out_shape=(
            jax.ShapeDtypeStruct((levels, across, along), f32),
            jax.ShapeDtypeStruct((along // LANES, levels * across, LANES), f32),
            face,
            face,
        ),
        in_specs=[vmem] * 3,
        out_specs=(vmem,) * 4,
        compiler_params=pltpu.CompilerParams(vmem_limit_bytes=8 * MIB),
        name="faces",
    )(cells, *lines)


def right_side_kernel(
    own_ref, shared_ref, side_a, side_b, height_a, height_b, cells_ref, scaling_ref, line_a, line_b, face_a, face_b,
    rhs_ref, near_ref, far_ref, dots_ref, first, second,
):
    levels, across, along = scaling_ref.shape
    edge = 8
    wide = across + 2 * edge
    inner = slice(edge, edge + across)
    quarters = along // LANES
    left, right, below, above, even, even_c = position()

    def low_of(is_even, one, two):
        return jnp.where(is_even, two, one)

    def high_of(is_even, one, two):
        return jnp.where(is_even, one, two)

    lane = lax.broadcasted_iota(i32, (1, LANES), 1)
    tiles = 16
    shift_q, shift_x = quarters.bit_length() - 1, across.bit_length() - 1
    for level, choose, present in ((0, low_of, below), (levels, None, None), (2 * levels, high_of, above)):
        if choose is None:
            parts = [low_of(even_c, side_a[...], side_b[...]), shared_ref[...], high_of(even_c, side_a[...], side_b[...])]
            values = [parts[0][0:tiles], own_ref[...], parts[2][0:tiles]]
        else:
            block = [
                choose(even, height_a[k * ROWS_OUT : (k + 1) * ROWS_OUT], height_b[k * ROWS_OUT : (k + 1) * ROWS_OUT])
                for k in range(3)
            ]
            parts = [low_of(even_c, block[1], block[2]), block[0], high_of(even_c, block[1], block[2])]
            values = [part[0:tiles] for part in parts]
        code = jnp.full((1, LANES), -1, i32)
        for n, part in enumerate(parts):
            owner = part[tiles : tiles + 1].astype(i32)
            x = ((owner >> shift_q) & (across - 1)) + (edge + (n - 1) * across)
            z = owner >> (shift_q + shift_x)
            here = ((lane >> 4) == n) | ((lane >> 4) == n + 3)
            here = here & (x >= edge - 2) & (x < edge + across + 2)
            if n == 0:
                here = here & left
            if n == 2:
                here = here & right
            if present is not None:
                here = here & present
            code = jnp.where(here, (z * wide + x) * quarters + (owner & (quarters - 1)), code)
        values = jnp.concatenate(values, axis=0)
        high = values.astype(bf16)
        low = (values - high.astype(f32)).astype(bf16)
        values = jnp.concatenate([high, low, jnp.zeros((LANES - 6 * tiles, LANES), bf16)], axis=0)
        spot = lax.broadcasted_iota(i32, (levels * wide, LANES), 0) * quarters
        for k in range(quarters):
            table = jnp.where(code == spot + k, 1.0, 0.0).astype(bf16)
            added = jnp.dot(table, values, preferred_element_type=f32)
            for z in range(levels):
                first[level + z, :, k * LANES : (k + 1) * LANES] = -added[z * wide : (z + 1) * wide]

    second[:, 0:edge, :] = jnp.zeros((3 * levels, edge, along), f32)
    second[:, edge + across :, :] = jnp.zeros((3 * levels, edge, along), f32)
    for z in range(levels):
        rhs = cells_ref[0, z] + first[levels + z, inner]
        rhs_ref[z] = rhs
        first[levels + z, inner] = scaling_ref[z] * rhs
        for choose, start, present, beside_at in ((low_of, edge - 2, left, 1), (high_of, edge + across, right, 0)):
            for k in range(2):
                x = slice(start + k, start + k + 1)
                for q in range(quarters):
                    part = slice(q * LANES, (q + 1) * LANES)
                    kinds = [
                        choose(even_c, *[line_at(lines, z, k, kind, q, quarters) for lines in (line_a, line_b)])
                        for kind in range(2)
                    ]
                    m = jnp.where(present, 1.0 / (6.0 + kinds[1]), 0.0)
                    first[levels + z, x, part] += m * kinds[0]
                    if k == beside_at:
                        second[levels + z, x, part] = m
    place = lax.broadcasted_iota(i32, (wide, along), 1)

    def beside(ref, z):
        mid = ref[z]
        total = ref[z - 1] + ref[z + 1] + pltpu.roll(mid, 1, 0) + pltpu.roll(mid, wide - 1, 0)
        total = total + jnp.where(place > 0, pltpu.roll(mid, 1, 1), 0.0)
        return total + jnp.where(place < along - 1, pltpu.roll(mid, along - 1, 1), 0.0)

    for z, choose, present in ((levels - 1, low_of, below), (2 * levels, high_of, above)):
        part = [slice(n * across, (n + 1) * across) for n in range(3)]
        near = beside(first, z)[inner] + choose(even, face_a[part[2]], face_b[part[2]])
        second[z, inner] = jnp.where(present, choose(even, face_a[part[0]], face_b[part[0]]) * near, 0.0)
        first[z, inner] += jnp.where(present, choose(even, face_a[part[1]], face_b[part[1]]), 0.0)
        for n, x in enumerate((edge - 1, edge + across)):
            line = slice(3 * across + n, 3 * across + n + 1)
            first[z, x : x + 1] += jnp.where(present, choose(even, face_a[line], face_b[line]), 0.0)

    dots = [jnp.zeros((8, LANES), f32)] * 4

    def folded(value):
        value = jnp.sum(value.reshape(across // 8, 8, along), axis=0)
        return sum(value[:, k * LANES : (k + 1) * LANES] for k in range(quarters))

    ends = (slice(0, edge), slice(edge + across, wide))
    for z in range(levels, 2 * levels):
        near = beside(first, z)
        for end in ends:
            second[z, end] = second[z, end] * near[end]
        near = near[inner]
        scaled = scaling_ref[z - levels] * near
        second[z, inner] = scaled
        near_ref[z - levels] = near
        start = first[z, inner]
        dots[0] = dots[0] + folded(start * rhs_ref[z - levels])
        dots[1] = dots[1] + folded(start * near)
        dots[2] = dots[2] + folded(scaled * near)
    for z in range(levels, 2 * levels):
        far = beside(second, z)[inner]
        far_ref[z - levels] = far
        dots[3] = dots[3] + folded(second[z, inner] * far)
    line = jnp.zeros((1, LANES), f32)
    for k in range(4):
        total = jnp.sum(jnp.sum(dots[k], axis=0, keepdims=True), axis=1, keepdims=True)
        line = jnp.where(lane == k, total, line)
    dots_ref[...] = jnp.broadcast_to(line, dots_ref.shape)


def right_side_of(own, shared, side, height, cells, scaling, lines, faces, devices):
    levels, across, along = scaling.shape
    vmem = pl.BlockSpec(memory_space=pltpu.VMEM)
    whole = pltpu.VMEM((3 * levels, across + 16, along), f32)
    return pl.pallas_call(
        right_side_kernel,
        out_shape=(jax.ShapeDtypeStruct(scaling.shape, f32),) * 3 + (jax.ShapeDtypeStruct((devices, LANES), f32),),
        in_specs=[vmem] * 12,
        out_specs=(vmem,) * 4,
        scratch_shapes=[whole] * 2,
        compiler_params=pltpu.CompilerParams(vmem_limit_bytes=16 * MIB),
        name="right_side",
    )(own, shared, *side, *height, cells, scaling, *lines, *faces)


def results_kernel(
    ints_ref, dots_ref, rhs_ref, near_ref, far_ref, scaling_ref, settled_ref, height_a, height_b,
    positions_out, velocities_out, pressure_out, residual_out, positions, velocities, pressure, residual, sent,
):
    rows, cols = settled_ref.shape[:2]
    levels = rhs_ref.shape[0]
    even = position()[4]
    for r in range(1, rows):
        for c in range(cols):
            kept = jnp.where(ints_ref[0, EXITS + r * cols + c] > 0, 0.0, settled_ref[r, c])
            for d in range(3):
                positions[d, r, c : c + 1] = kept[d : d + 1]
                velocities[d, r, c : c + 1] = kept[d + 3 : d + 4]
    start = 3 * ROWS_OUT
    for d in range(6):
        block = slice(start + d * cols, start + (d + 1) * cols)
        tiles = jnp.where(even, height_b[block], height_a[block])
        target = positions if d < 3 else velocities
        for k in range(cols):
            target[d % 3, 0, pl.ds(ints_ref[0, INLETS + k], 1)] = tiles[k : k + 1]
    copies = [
        pltpu.make_async_copy(positions, positions_out, sent.at[0]),
        pltpu.make_async_copy(velocities, velocities_out, sent.at[1]),
    ]
    for copy in copies:
        copy.start()
    totals = jnp.sum(dots_ref[...], axis=0, keepdims=True)
    g00, g01, g11, g12 = [totals[:, k : k + 1] for k in range(4)]
    ratio = g01 / g00
    alpha = g00 / (g00 - g01)
    square = alpha * alpha
    renewed = square * (g11 - ratio * g01)
    beta = renewed / g00
    crossed = square * (ratio * ratio * g01 - 2.0 * ratio * g11 + g12)
    curvature = renewed - crossed - beta * renewed / alpha
    later = renewed / curvature
    one = alpha + later * (1.0 - alpha + beta)
    two = later * alpha
    for z in range(levels):
        rhs, near = rhs_ref[z], near_ref[z]
        pressure[z] = scaling_ref[z] * (one * rhs + two * near)
        residual[z] = (1.0 - one) * rhs + (one - two) * near + two * far_ref[z]
        for n, (source, target) in enumerate(((pressure, pressure_out), (residual, residual_out))):
            copy = pltpu.make_async_copy(source.at[z], target.at[z], sent.at[2 + 2 * z + n])
            copy.start()
            copies.append(copy)
    for copy in copies:
        copy.wait()


def results_of(ints, dots, rhs, near, far, scaling, settled, height):
    rows, cols = settled.shape[:2]
    smem = pl.BlockSpec(memory_space=pltpu.SMEM)
    vmem = pl.BlockSpec(memory_space=pltpu.VMEM)
    particle = jax.ShapeDtypeStruct((3, rows, cols, LANES), f32)
    field = jax.ShapeDtypeStruct(rhs.shape, f32)
    return pl.pallas_call(
        results_kernel,
        out_shape=(particle, particle, field, field),
        in_specs=[smem] + [vmem] * 8,
        out_specs=(pl.BlockSpec(memory_space=pl.ANY),) * 4,
        scratch_shapes=[
            *[pltpu.VMEM(particle.shape, f32)] * 2,
            *[pltpu.VMEM(field.shape, f32)] * 2,
            pltpu.SemaphoreType.DMA((2 + 2 * rhs.shape[0],)),
        ],
        compiler_params=pltpu.CompilerParams(vmem_limit_bytes=8 * MIB),
        name="results",
    )(ints, dots, rhs, near, far, scaling, settled, *height)


def on_device(
    positions, velocities, contacts, exit_flags, inlet_slots, cell_blocks, cell_slots, gas_source, diagonal
):
    heights, groups = lax.axis_size("height"), lax.axis_size("cols")
    h, c = lax.axis_index("height"), lax.axis_index("cols")
    *sides, flags, ints, slots, state, cells = packed(
        exit_flags, cell_blocks, inlet_slots, positions, velocities, contacts.transpose(1, 2, 0), cell_slots,
        gas_source, diagonal,
    )
    lines = [
        lax.ppermute(value, ("height", "cols"), matching(heights, groups, "cols", odd, True))
        for value, odd in zip(sides, (False, True))
    ]
    window = merged(state, flags, lines)
    beside = exchanged(window, "height", False)
    own_parts = own_sums(window, *state.shape[1:3])
    scaling, blocks, *faces = faces_of(cells, lines)
    faces, beside = lax.optimization_barrier((faces, beside))
    faces = [
        lax.ppermute(value, ("height", "cols"), matching(heights, groups, "height", odd, False))
        for value, odd in zip(faces, (False, True))
    ]
    settled, leaving = particles(ints, *beside, own_parts)
    own, shared = deposits(ints, settled, slots, blocks)
    near = exchanged(shared, "cols", True)
    parcel = jnp.concatenate([shared, *near, leaving.reshape(-1, LANES)], axis=0)
    parcels = exchanged(parcel, "height", True)
    rhs, first, second, dots = right_side_of(
        own, shared, near, parcels, cells, scaling, lines, faces, heights * groups
    )
    dots = lax.all_to_all(dots, ("height", "cols"), 0, 0, tiled=True)
    return results_of(ints, dots, rhs, first, second, scaling, settled, parcels)


def solution(mesh):
    in_specs = (
        P(None, "height", "cols", None),
        P(None, "height", "cols", None),
        P(None, "height", "cols"),
        P("height", "cols"),
        P("height", "cols"),
        P("height", "cols"),
        P("height", "cols", None),
        P("height", "cols", None),
        P("height", "cols", None),
    )
    out_specs = (
        P(None, "height", "cols", None),
        P(None, "height", "cols", None),
        P("height", "cols", None),
        P("height", "cols", None),
    )
    return jax.shard_map(
        on_device, mesh=mesh, in_specs=in_specs, out_specs=out_specs, check_vma=False
    )
```

```python
import functools
import jax
import jax.numpy as jnp
from jax import lax
from jax.experimental import pallas as pl
from jax.experimental.pallas import tpu as pltpu
from jax.sharding import PartitionSpec as P

f32, bf16, i32 = jnp.float32, jnp.bfloat16, jnp.int32
spring = 0.05
cutoff_sq = 1.44
damping = 0.5
step_dt = 0.05
gravity = 1.0
deposit_gain = 2.0
LANES = 128
COMPS = 8
DEPTH = 2
ROWS_OUT = 24
FLAG_LANES = 16
MIB = 1024 * 1024
NEARS = 6
EXITS, OWNERS, INLETS = 0, 16, 32


def rounded(value):
    return value.astype(bf16).astype(f32)


def rounded_pair(value):
    high = rounded(value)
    return high, rounded(value - high)


def split(value):
    high = rounded(value)
    mid = rounded(value - high)
    return high, mid, value - high - mid


def centred(tile, r, c, rows, wide):
    row = lax.broadcasted_iota(i32, (COMPS, LANES), 0)
    side = jnp.float32(c - wide // 2)
    up = (r - rows // 2).astype(f32)
    return tile + jnp.where(row == 0, side, jnp.where(row == 2, up, 0.0))


def place_parts(tile, r, c, rows, wide):
    row = lax.broadcasted_iota(i32, (COMPS, LANES), 0)
    place = jnp.where(row < 3, centred(tile, r, c, rows, wide), 0.0)
    high, mid = rounded_pair(place)
    place = high + mid
    return high, mid, -jnp.sum(place * place, axis=0, keepdims=True)


def source_features(tile, r, c, rows, wide):
    row = lax.broadcasted_iota(i32, (COMPS, LANES), 0)
    row32 = lax.broadcasted_iota(i32, (32, LANES), 0)
    high, mid, size = place_parts(tile, r, c, rows, wide)
    size_high, size_mid, size_low = split(size)
    first = jnp.where(row < 3, high, 1.0)
    first = jnp.where(row == 3, size_high, jnp.where(row == 4, size_mid, jnp.where(row == 5, size_low, first)))
    second = jnp.where(row < 3, high, jnp.where(row == 3, 1.0, 0.0))
    kind = lax.rem(r, 3) * 4 + c % 4
    kind = kind + jnp.where(kind < 4, 12, jnp.where(kind < 9, 15, 18))
    near = jnp.concatenate([first, second, mid, mid], axis=0) + jnp.where(row32 == kind, 1.0, 0.0)
    high, mid, low = split(centred(tile, r, c, rows, wide) - damping * pltpu.roll(tile, 5, 0))
    first = jnp.where(row < 3, high, jnp.where(row == 3, 1.0, 0.0))
    second = jnp.where(row < 3, mid, jnp.where(row < 4, 0.0, pltpu.roll(low, 4, 0)))
    return near, jnp.concatenate([first, second], axis=0).astype(bf16)


def target_features(tile, r, c, rows, wide):
    row = lax.broadcasted_iota(i32, (COMPS, LANES), 0)
    row32 = lax.broadcasted_iota(i32, (32, LANES), 0)
    lane32 = lax.broadcasted_iota(i32, (32, LANES), 1)
    high, mid, size = place_parts(tile, r, c, rows, wide)
    own_high, own_mid, own_low = split(cutoff_sq + size)
    first = jnp.where(row < 3, 2.0 * high, jnp.where(row < 6, 1.0, jnp.where(row == 6, own_high, own_mid)))
    second = jnp.where(row < 3, 2.0 * mid, jnp.where(row == 3, own_low, 0.0))
    third = jnp.where(row < 3, 2.0 * high, 0.0)
    fourth = jnp.where(row < 3, 2.0 * mid, 0.0)
    kind = jnp.where(row32 < 16, row32 - 12, jnp.where(row32 < 24, row32 - 15, row32 - 18))
    is_kind = ((row32 >= 12) & (row32 < 16)) | ((row32 >= 19) & (row32 < 24)) | ((row32 >= 27) & (row32 < 30))
    kind_row = jnp.where(kind < 4, 0, jnp.where(kind < 8, 1, 2))
    up = kind_row + lax.rem(4 - lax.rem(r, 3), 3)
    up = jnp.where(up > 2, up - 3, up)
    side = kind - 4 * kind_row + (5 - c % 4) % 4
    side = jnp.where(side > 3, side - 4, side)
    if DEPTH <= c < wide - DEPTH:
        start = (c - DEPTH) * FLAG_LANES
    else:
        start = (lax.rem(r, DEPTH) * DEPTH + c % 2) * FLAG_LANES
    wanted = jnp.where(side < 3, 3 * up + side + start, LANES)
    flags = jnp.sum(jnp.where(lane32 == wanted, tile[6:7, :], 0.0), axis=1, keepdims=True)
    barred = jnp.where(is_kind, -1024.0 * (1.0 - flags), 0.0)
    return jnp.concatenate([first, second, third, fourth], axis=0) + barred


def unit_operands(tiles, r, c, rows, wide):
    features = [target_features(tile, r, c + k, rows, wide) for k, tile in enumerate(tiles)]
    features = jnp.concatenate(features, axis=1).astype(bf16)
    start = (c - 1) // 4
    ends = (c - 1, c + 2)

    def spread(part, s):
        at = 4 * (s // 4 - start) + s % 4
        return jnp.concatenate([part if k == at else jnp.zeros_like(part) for k in range(8)], axis=0)

    halves = [spread(features[:, k * LANES : (k + 1) * LANES], s) for k, s in enumerate(ends)]
    return [spread(features, c), spread(features, c + 1), jnp.concatenate(halves, axis=1)]


def pulls_row(tiles, r, columns, source_rows, rows, wide, turned, pulled, nears, founds):
    ahead = len(nears) - 1
    count = len(source_rows)
    units = [(pair, kind, i) for pair in range(len(columns)) for kind in range(3) for i in range(count)]
    blocks = wide // 4
    operands = [None] * len(columns)

    def begin(n):
        pair, kind, i = units[n]
        c = columns[pair]
        staged = (3 * pair + kind) % 2
        if i == 0:
            if kind == 0:
                operands[pair] = unit_operands(tiles[pair], r, c, rows, wide)
            pltpu.matmul_push_rhs(operands[pair][kind], staged, 0)
        start = (c - 1) // 4
        after = start + 1 if start + 1 < blocks else 0
        row = source_rows[i]
        sources = jnp.concatenate([turned(row)[start], turned(row)[after]], axis=1)
        pltpu.matmul_acc_lhs(nears[n % len(nears)], sources, load_staged_rhs=staged if i == 0 else None)

    def finish(n):
        pair, kind, i = units[n]
        c = columns[pair]
        weight = jnp.maximum(pltpu.matmul_pop(nears[n % len(nears)]), 0.0)
        high = weight.astype(bf16)
        low = (weight - high.astype(f32)).astype(bf16)
        pltpu.matmul_push_rhs(jnp.concatenate([high, low], axis=0), n % 2, 1)
        of_row = pulled(source_rows[i])
        if kind < 2:
            pulls = of_row[c + kind]
        else:
            pulls = jnp.concatenate([of_row[c - 1], of_row[c + 2]], axis=0)
        pulls = jnp.concatenate([pulls, pulls], axis=1)
        pltpu.matmul_acc_lhs(founds[2 * pair + (kind == 2)], pulls, load_staged_rhs=n % 2)

    for n in range(len(units) + ahead):
        if n < len(units):
            begin(n)
        if n >= ahead:
            finish(n - ahead)
    totals = []
    for pair in range(len(columns)):
        inner, outer = pltpu.matmul_pop(founds[2 * pair]), pltpu.matmul_pop(founds[2 * pair + 1])
        totals.append(inner + jnp.concatenate([outer[0:16, 0:LANES], outer[16:32, LANES:]], axis=1))
    return totals


def forces_of(totals, tiles, r, columns, rows, wide):
    forces = []
    for pair, c in enumerate(columns):
        for k, tile in enumerate(tiles[pair]):
            total = totals[pair][:, k * LANES : (k + 1) * LANES]
            first, second = total[0:8], total[8:16]
            moving = centred(tile, r, c + k, rows, wide) - damping * pltpu.roll(tile, 5, 0)
            forces.append((spring / cutoff_sq) * (moving * first[3:4, :] - first - second - pltpu.roll(second, 4, 0)))
    return forces


def stepped(tile, force):
    row = lax.broadcasted_iota(i32, (COMPS, LANES), 0)
    change = step_dt * force - jnp.where(row == 2, step_dt * gravity, 0.0)
    speeds = tile + pltpu.roll(change, 3, 0)
    places = tile + step_dt * pltpu.roll(speeds, 5, 0)
    return jnp.where(row < 3, places, jnp.where(row < 6, speeds, tile))


def position():
    heights, groups = lax.axis_size("height"), lax.axis_size("cols")
    h, c = lax.axis_index("height"), lax.axis_index("cols")
    return c > 0, c < groups - 1, h > 0, h < heights - 1, lax.rem(h, 2) == 0, lax.rem(c, 2) == 0


def halo_rows(rows, cols, d, r, c):
    wide = cols + 2 * DEPTH
    start = d * rows * wide
    if c < DEPTH:
        return start + rows * cols + r * DEPTH + c
    if c >= cols + DEPTH:
        return start + rows * (cols + DEPTH) + r * DEPTH + c - cols - DEPTH
    return start + r * cols + c - DEPTH


def tiles_of_block(block, place, rows, cols):
    wide = cols + 2 * DEPTH
    flag_row = 6 * rows * wide
    for r in range(rows):
        for c in range(wide):
            for d in range(6):
                row = halo_rows(rows, cols, d, r, c)
                place(r, c, d, block[row : row + 1])
            row = flag_row + (rows if c < DEPTH else rows + 1 if c >= cols + DEPTH else r)
            place(r, c, 6, block[row : row + 1])
            place(r, c, 7, jnp.zeros((1, LANES), f32))


def fill_row(tile_at, r, high, wide, turned_row, pulled_row):
    for block in range(wide // 4):
        near = []
        for c in range(4 * block, 4 * block + 4):
            places, moving = source_features(tile_at(c), r, c, high, wide)
            near.append(places)
            pulled_row[c] = moving
        turned_row[block] = jnp.concatenate(near, axis=0).T.astype(bf16)


def accumulators(wide):
    return (
        *[pltpu.ACC(0)((LANES, 2 * LANES), f32)] * NEARS,
        *[pltpu.ACC(1)((held, 2 * LANES), f32) for _ in range(wide // 2 - 1) for held in (16, 32)],
    )


def emptied(refs):
    for ref in refs:
        pltpu.matmul_pop(ref)
    return refs[:NEARS], refs[NEARS:]


def own_kernel(own_ref, state_ref, turned_ref, pulled_ref, partial_ref, *, rows, cols):
    wide = cols + 2 * DEPTH
    high = rows + 2 * DEPTH
    columns = list(range(1, wide - 1, 2))

    def place(r, c, d, value):
        state_ref[r, c, d : d + 1] = value

    tiles_of_block(own_ref, place, rows, cols)

    def one_row(r, carry):
        fill_row(lambda c: state_ref[r, c], r + DEPTH, high, wide, turned_ref.at[r], pulled_ref.at[r])
        return carry

    lax.fori_loop(0, rows, one_row, 0)

    def sums(*refs):
        nears, founds = emptied(refs)

        def one_sum(r, carry):
            tiles = [[state_ref[r, c], state_ref[r, c + 1]] for c in columns]
            totals = pulls_row(
                tiles, r + DEPTH, columns, list(range(rows)), high, wide,
                lambda row: turned_ref.at[row], lambda row: pulled_ref.at[row], nears, founds,
            )
            for pair, total in enumerate(totals):
                partial_ref[r, pair] = total
            return carry

        lax.fori_loop(0, rows, one_sum, 0)

    pl.run_scoped(sums, *accumulators(wide))


def own_sums(own, rows, cols):
    wide = cols + 2 * DEPTH
    vmem = pl.BlockSpec(memory_space=pltpu.VMEM)
    return pl.pallas_call(
        functools.partial(own_kernel, rows=rows, cols=cols),
        out_shape=(
            jax.ShapeDtypeStruct((rows, wide, COMPS, LANES), f32),
            jax.ShapeDtypeStruct((rows, wide // 4, LANES, LANES), bf16),
            jax.ShapeDtypeStruct((rows, wide, 16, LANES), bf16),
            jax.ShapeDtypeStruct((rows, wide // 2 - 1, 16, 2 * LANES), f32),
        ),
        in_specs=[vmem],
        out_specs=(vmem,) * 4,
        cost_estimate=pl.CostEstimate(flops=4 * 10**9, bytes_accessed=4096, transcendentals=0),
        compiler_params=pltpu.CompilerParams(vmem_limit_bytes=8 * MIB),
        name="own_sums",
    )(own)


def particles_kernel(
    picks_ref, first_ref, second_ref, own_ref, own_turned, own_pulled, partial_ref,
    settled_ref, leaving_ref, state, turned, pulled, begun, begun_turned, begun_pulled, blocks,
    *, rows, cols,
):
    wide = cols + 2 * DEPTH
    high = rows + 2 * DEPTH
    left, right, below, above, even, _ = position()
    one, two = first_ref[...], second_ref[...]
    blocks[0] = jnp.where(below, jnp.where(even, two, one), 0.0)
    blocks[1] = jnp.where(above, jnp.where(even, one, two), 0.0)
    for half, start in ((0, 0), (1, rows + DEPTH)):

        def place(r, c, d, value, start=start):
            state[start + r, c, d : d + 1] = value

        tiles_of_block(blocks.at[half], place, rows, cols)

    def far_row(r):
        fill_row(lambda c: state[r, c], r, high, wide, turned.at[r], pulled.at[r])

    def near_row(n, carry):
        far_row(1 + n * (rows + 1))
        return carry

    lax.fori_loop(0, 2, near_row, 0)
    for r in range(rows):
        state[DEPTH + r] = own_ref[r]
        turned[DEPTH + r] = own_turned[r]
        pulled[DEPTH + r] = own_pulled[r]

    def substeps(*refs):
        nears, founds = emptied(refs)
        sources = dict(turned=lambda row: turned.at[row], pulled=lambda row: pulled.at[row], nears=nears, founds=founds)
        columns = list(range(1, wide - 1, 2))

        later = dict(
            turned=lambda row: begun_turned.at[row], pulled=lambda row: begun_pulled.at[row], nears=nears, founds=founds
        )

        def begun_row(r):
            fill_row(lambda c: begun[r, c], r, high, wide, begun_turned.at[r], begun_pulled.at[r])

        def begin_row(r, totals):
            tiles = [[state[r, c], state[r, c + 1]] for c in columns]
            forces = forces_of(totals, tiles, r, columns, high, wide)
            begun[r, 0] = jnp.zeros((COMPS, LANES), f32)
            begun[r, wide - 1] = jnp.zeros((COMPS, LANES), f32)
            for c in range(1, wide - 1):
                inside = ((r >= DEPTH) | below) & ((r < rows + DEPTH) | above)
                if c < DEPTH:
                    inside = inside & left
                if c >= cols + DEPTH:
                    inside = inside & right
                begun[r, c] = jnp.where(inside, stepped(tiles[(c - 1) // 2][(c - 1) % 2], forces[c - 1]), 0.0)

        def outer_step(n, carry):
            r = 1 + n * (rows + 1)
            begun_row(DEPTH + n * (rows - 1))
            tiles = [[state[r, c], state[r, c + 1]] for c in columns]
            begin_row(r, pulls_row(tiles, r, columns, [r - 1, r, r + 1], high, wide, **sources))
            return carry

        def inner_step(n, carry):
            r = DEPTH + n * (rows - 1)
            far_row(n * (high - 1))
            tiles = [[state[r, c], state[r, c + 1]] for c in columns]
            totals = pulls_row(tiles, r, columns, [1 + n * (rows + 1)], high, wide, **sources)
            begin_row(r, [total + partial_ref[n * (rows - 1), pair] for pair, total in enumerate(totals)])
            return carry

        lax.fori_loop(0, 2, inner_step, 0)
        lax.fori_loop(0, 2, outer_step, 0)

        begun_row(jnp.int32(1))

        def second_step(r, carry):
            columns = list(range(DEPTH, DEPTH + cols, 2))
            tiles = [[begun[r, c], begun[r, c + 1]] for c in columns]
            begun_row(jnp.int32(high - 2))
            totals = pulls_row(tiles, r, columns, [r - 1, r, r + 1], high, wide, **later)
            forces = forces_of(totals, tiles, r, columns, high, wide)
            for c in range(cols):
                settled_ref[r - DEPTH, c] = stepped(tiles[c // 2][c % 2], forces[c])
            return carry

        lax.fori_loop(DEPTH, DEPTH + rows, second_step, 0)

    pl.run_scoped(substeps, *accumulators(wide))

    for k in range(cols):
        tile = jnp.zeros((COMPS, LANES), f32)
        for c in range(cols):
            tile = tile + picks_ref[k, c : c + 1] * settled_ref[rows - 1, c]
        for d in range(6):
            leaving_ref[d, k : k + 1] = tile[d : d + 1]


def particles(picks, first, second, own):
    rows, wide = own[0].shape[:2]
    cols, high = wide - 2 * DEPTH, rows + 2 * DEPTH
    vmem = pl.BlockSpec(memory_space=pltpu.VMEM)
    return pl.pallas_call(
        functools.partial(particles_kernel, rows=rows, cols=cols),
        out_shape=(
            jax.ShapeDtypeStruct((rows, cols, COMPS, LANES), f32),
            jax.ShapeDtypeStruct((6, cols, LANES), f32),
        ),
        in_specs=[vmem] * 7,
        out_specs=(vmem, vmem),
        scratch_shapes=[
            pltpu.VMEM((high, wide, COMPS, LANES), f32),
            pltpu.VMEM((high, wide // 4, LANES, LANES), bf16),
            pltpu.VMEM((high, wide, 16, LANES), bf16),
            pltpu.VMEM((high, wide, COMPS, LANES), f32),
            pltpu.VMEM((high, wide // 4, LANES, LANES), bf16),
            pltpu.VMEM((high, wide, 16, LANES), bf16),
            pltpu.VMEM((2, *first.shape), f32),
        ],
        cost_estimate=pl.CostEstimate(flops=10**10, bytes_accessed=4096, transcendentals=0),
        compiler_params=pltpu.CompilerParams(vmem_limit_bytes=12 * MIB),
        name="particles",
    )(picks, first, second, *own)


def deposit_kernel(settled_ref, slots_ref, weights_ref, owners_ref, own_ref, shared_ref):
    rows, cols = settled_ref.shape[:2]
    row = lax.broadcasted_iota(i32, (16, LANES), 0)
    cell = lax.broadcasted_iota(i32, (LANES, LANES), 0)
    for t in range(rows * cols):
        r, c = t // cols, t % cols
        lift_high, lift_mid, lift_low = split(deposit_gain * settled_ref[r, c, 5:6, :])
        parts = jnp.where(row == 0, lift_high, jnp.where(row == 1, lift_mid, jnp.where(row == 2, lift_low, 0.0)))
        table = jnp.where(cell == slots_ref[r, c : c + 1, :], 1.0, 0.0).astype(bf16)
        gathered = lax.dot_general(parts.astype(bf16), table, (((1,), (1,)), ((), ())), preferred_element_type=f32)
        sums = jnp.sum(gathered, axis=0, keepdims=True)
        own_ref[t : t + 1, :] = sums
        shared_ref[t : t + 1, :] = weights_ref[t : t + 1] * sums
    row = lax.broadcasted_iota(i32, (ROWS_OUT - rows * cols, LANES), 0)
    shared_ref[rows * cols :, :] = jnp.where(row == 0, owners_ref[...], 0.0)


def deposits(settled, slots, weights, owners):
    rows, cols = settled.shape[:2]
    vmem = pl.BlockSpec(memory_space=pltpu.VMEM)
    return pl.pallas_call(
        deposit_kernel,
        out_shape=(
            jax.ShapeDtypeStruct((rows * cols, LANES), f32),
            jax.ShapeDtypeStruct((ROWS_OUT, LANES), f32),
        ),
        in_specs=[vmem] * 4,
        out_specs=(vmem, vmem),
        compiler_params=pltpu.CompilerParams(vmem_limit_bytes=4 * MIB),
        name="deposits",
    )(settled, slots, weights, owners)


def marks_kernel(ints_ref, cells_ref, picks_ref, keeps_ref, places_ref, weights_ref, owners_ref, blocks):
    cols = keeps_ref.shape[0]
    tiles = weights_ref.shape[0]
    _, levels, across, along = cells_ref.shape
    quarters = along // LANES
    for z in range(levels):
        for q in range(quarters):
            blocks[q, z * across : (z + 1) * across] = cells_ref[1, z, :, q * LANES : (q + 1) * LANES]
    lane = lax.broadcasted_iota(i32, (1, LANES), 1)
    row = lax.broadcasted_iota(i32, (cols, LANES), 0)
    owner_row = jnp.zeros((1, LANES), i32)
    for t in range(tiles):
        owner = ints_ref[0, OWNERS + t]
        owner_row = jnp.where(lax.rem(lane, tiles) == t, owner, owner_row)
        line = blocks[owner % quarters, pl.ds(owner // quarters, 1), :]
        weights_ref[t : t + 1, :] = 1.0 / (6.0 + line)
    owners_ref[...] = owner_row.astype(f32)
    picks_ref[...] = jnp.zeros_like(picks_ref)
    count = jnp.int32(0)
    for c in range(cols):
        flag = ints_ref[0, EXITS + tiles - cols + c]
        keeps_ref[c : c + 1] = jnp.broadcast_to(jnp.where(flag > 0, 0.0, 1.0), (1, LANES))
        for k in range(c + 1):
            picks_ref[k, c : c + 1] = jnp.broadcast_to(jnp.where((flag > 0) & (count == k), 1.0, 0.0), (1, LANES))
        count = count + flag
        places_ref[c] = jnp.where(row == ints_ref[0, INLETS + c], 1.0, 0.0)


def marks_of(ints, cells, tiles, cols):
    _, levels, across, along = cells.shape
    smem = pl.BlockSpec(memory_space=pltpu.SMEM)
    vmem = pl.BlockSpec(memory_space=pltpu.VMEM)
    return pl.pallas_call(
        marks_kernel,
        out_shape=(
            jax.ShapeDtypeStruct((cols, cols, LANES), f32),
            jax.ShapeDtypeStruct((cols, LANES), f32),
            jax.ShapeDtypeStruct((cols, cols, LANES), f32),
            jax.ShapeDtypeStruct((tiles, LANES), f32),
            jax.ShapeDtypeStruct((1, LANES), f32),
        ),
        in_specs=[smem, vmem],
        out_specs=(vmem,) * 5,
        scratch_shapes=[pltpu.VMEM((along // LANES, levels * across, LANES), f32)],
        cost_estimate=pl.CostEstimate(flops=10**9, bytes_accessed=4096, transcendentals=0),
        compiler_params=pltpu.CompilerParams(vmem_limit_bytes=4 * MIB),
        name="marks",
    )(ints, cells)


def matching(heights, groups, axis, odd, wrap):
    size = heights if axis == "height" else groups
    pairs = []
    for h in range(heights):
        for c in range(groups):
            i = h if axis == "height" else c
            j = i ^ 1 if not odd else (i + 1 if i % 2 else i - 1)
            if 0 <= j < size or wrap:
                j = j % size
                target = (j, c) if axis == "height" else (h, j)
            else:
                target = (h, c ^ 1) if axis == "height" else (h ^ 1, c)
            pairs.append((h * groups + c, target[0] * groups + target[1]))
    return pairs


def around_pairs(heights, groups):
    pairs = []
    for h in range(heights):
        for c in range(groups):
            target = (heights - 1 - h, c) if h in (0, heights - 1) else (h, c ^ 1)
            pairs.append((h * groups + c, target[0] * groups + target[1]))
    return pairs


def exchanged(value, axis, wrap):
    heights, groups = lax.axis_size("height"), lax.axis_size("cols")
    return [
        lax.ppermute(value, ("height", "cols"), matching(heights, groups, axis, odd, wrap)) for odd in (False, True)
    ]


LINES = 32


def begin_kernel(zeros_ref):
    zeros_ref[...] = jnp.zeros_like(zeros_ref)


def begun_zeros():
    return pl.pallas_call(
        begin_kernel,
        out_shape=jax.ShapeDtypeStruct((8, LANES), f32),
        out_specs=pl.BlockSpec(memory_space=pltpu.VMEM),
        cost_estimate=pl.CostEstimate(flops=10**10, bytes_accessed=4096, transcendentals=0),
        compiler_params=pltpu.CompilerParams(vmem_limit_bytes=MIB),
        name="begin",
    )()


def pack_kernel(
    zeros_ref, exits_ref, owners_ref, inlets_ref, positions_ref, velocities_ref, contacts_ref, slots_in, gas_ref,
    diagonal_ref, first_ref, second_ref, flags_ref, ints_ref, slots_ref, state_ref, cells_ref, sides, wide_flags, small,
):
    rows, cols = state_ref.shape[1:3]
    _, levels, across, along = cells_ref.shape
    lane = lax.broadcasted_iota(i32, (1, LANES), 1)
    sides[...] = jnp.zeros_like(sides) + zeros_ref[0:1]
    wide_flags[...] = jnp.zeros_like(wide_flags)
    small[...] = jnp.zeros_like(small)
    state_ref[0:3] = positions_ref[...]
    state_ref[3:6] = velocities_ref[...]
    cells_ref[0] = gas_ref[...]
    cells_ref[1] = diagonal_ref[...]
    slots_ref[...] = slots_in[...]
    small[0:rows, 0:cols] = exits_ref[...]
    small[rows : 2 * rows, 0:cols] = owners_ref[...]
    small[2 * rows : 2 * rows + 1, 0:cols] = inlets_ref[...]
    ints = jnp.zeros((1, LANES), i32)
    for r in range(rows):
        ints = ints + pltpu.roll(small[r : r + 1], EXITS + r * cols, 1)
        ints = ints + pltpu.roll(small[rows + r : rows + r + 1], OWNERS + r * cols, 1)
    ints_ref[...] = ints + pltpu.roll(small[2 * rows : 2 * rows + 1], INLETS, 1)
    wide_flags[:, :, 0 : contacts_ref.shape[2]] = contacts_ref[...].astype(f32)
    flags = []
    for r in range(rows):
        spread = pltpu.roll(wide_flags[r], 0, 1, stride=FLAG_LANES, stride_axis=0)
        flags.append(jnp.sum(spread, axis=0, keepdims=True))
        flags_ref[r : r + 1] = flags[r]
    for side in range(2):
        shown = jnp.zeros((1, LANES), f32)
        for r in range(rows):
            for k in range(DEPTH):
                c = k if side == 0 else cols - DEPTH + k
                for d in range(6):
                    row = d * rows * DEPTH + r * DEPTH + k
                    sides[side, row : row + 1] = state_ref[d, r, c : c + 1]
            turn = (r * DEPTH - (0 if side == 0 else cols - DEPTH)) * FLAG_LANES
            part = pltpu.roll(flags[r], turn % LANES, 1)
            shown = jnp.where(lane // (DEPTH * FLAG_LANES) == r, part, shown)
        sides[side, 6 * rows * DEPTH : 6 * rows * DEPTH + 1] = shown
        for z in range(levels):
            for k in range(2):
                x = k if side == 0 else across - 2 + k
                for kind in range(2):
                    for q in range(along // LANES):
                        row = LINES + ((z * 2 + k) * 2 + kind) * (along // LANES) + q
                        sides[side, row : row + 1] = cells_ref[kind, z, x : x + 1, q * LANES : (q + 1) * LANES]
    even = position()[5]
    first_ref[...] = jnp.where(even, sides[1], sides[0])
    second_ref[...] = jnp.where(even, sides[0], sides[1])


def packed(exits, owners, inlets, positions, velocities, contacts, slots, gas, diagonal):
    levels, across, along = gas.shape
    rows, cols = positions.shape[1:3]
    side = jax.ShapeDtypeStruct((LINES + levels * 4 * (along // LANES), LANES), f32)
    vmem = pl.BlockSpec(memory_space=pltpu.VMEM)
    return pl.pallas_call(
        pack_kernel,
        out_shape=(
            side,
            side,
            jax.ShapeDtypeStruct((rows, LANES), f32),
            jax.ShapeDtypeStruct((1, LANES), i32),
            jax.ShapeDtypeStruct(slots.shape, i32),
            jax.ShapeDtypeStruct((6, rows, cols, LANES), f32),
            jax.ShapeDtypeStruct((2, levels, across, along), f32),
        ),
        in_specs=[vmem] * 10,
        out_specs=(vmem,) * 7,
        scratch_shapes=[
            pltpu.VMEM((2, *side.shape), f32),
            pltpu.VMEM((rows, cols, LANES), f32),
            pltpu.VMEM((8, LANES), i32),
        ],
        compiler_params=pltpu.CompilerParams(vmem_limit_bytes=8 * MIB),
        name="pack",
    )(begun_zeros(), exits, owners, inlets, positions, velocities, contacts, slots, gas, diagonal)


def merge_kernel(state_ref, flags_ref, line_a, line_b, owners_ref, window_ref):
    rows, cols = state_ref.shape[1:3]
    each = rows * (cols + 2 * DEPTH)
    count = 6 * rows * DEPTH
    left, right, _, _, _, even = position()
    one, two = line_a[0 : count + 8], line_b[0 : count + 8]
    low = jnp.where(left, jnp.where(even, two, one), 0.0)
    top = jnp.where(right, jnp.where(even, one, two), 0.0)
    for d in range(6):
        for r in range(rows):
            window_ref[d * each + r * cols : d * each + (r + 1) * cols] = state_ref[d, r]
        at = d * each + rows * cols
        piece = slice(d * rows * DEPTH, (d + 1) * rows * DEPTH)
        window_ref[at : at + rows * DEPTH] = low[piece]
        window_ref[at + rows * DEPTH : at + 2 * rows * DEPTH] = top[piece]
    window_ref[6 * each : 6 * each + 8] = jnp.concatenate(
        [flags_ref[...], low[count : count + 1], top[count : count + 1], jnp.zeros((6 - rows, LANES), f32)], axis=0
    )


def merged(state, flags, lines, owners):
    rows, cols = state.shape[1:3]
    vmem = pl.BlockSpec(memory_space=pltpu.VMEM)
    return pl.pallas_call(
        merge_kernel,
        out_shape=jax.ShapeDtypeStruct((6 * rows * (cols + 2 * DEPTH) + 8, LANES), f32),
        in_specs=[vmem] * 5,
        out_specs=vmem,
        compiler_params=pltpu.CompilerParams(vmem_limit_bytes=4 * MIB),
        name="merge",
    )(state, flags, *lines, owners)


def line_at(lines, z, k, kind, q, quarters):
    row = LINES + ((z * 2 + k) * 2 + kind) * quarters + q
    return lines[row : row + 1]


def faces_kernel(cells_ref, line_a, line_b, scaling_ref, first_ref, second_ref):
    _, levels, across, along = cells_ref.shape
    quarters = along // LANES
    left, right, _, _, even, even_c = position()
    row = lax.broadcasted_iota(i32, (across, along), 0)
    place = lax.broadcasted_iota(i32, (across, along), 1)
    scaled = []
    for z in range(levels):
        scaling_ref[z] = 1.0 / (6.0 + cells_ref[1, z])
        scaled.append(scaling_ref[z] * cells_ref[0, z])
    faces = []
    for z in range(levels):
        ends = []
        for k, present, flip in ((1, left, False), (0, right, True)):
            parts = []
            for q in range(quarters):
                kinds = []
                for kind in range(2):
                    one, two = (line_at(lines, z, k, kind, q, quarters) for lines in (line_a, line_b))
                    kinds.append(jnp.where(even_c, one, two) if flip else jnp.where(even_c, two, one))
                parts.append(jnp.where(present, kinds[0] / (6.0 + kinds[1]), 0.0))
            ends.append(jnp.concatenate(parts, axis=1))
        mid = scaled[z]
        total = scaled[levels - 1 - z]
        total = total + jnp.where(row > 0, pltpu.roll(mid, 1, 0), ends[0])
        total = total + jnp.where(row < across - 1, pltpu.roll(mid, across - 1, 0), ends[1])
        total = total + jnp.where(place > 0, pltpu.roll(mid, 1, 1), 0.0)
        total = total + jnp.where(place < along - 1, pltpu.roll(mid, along - 1, 1), 0.0)
        outer = jnp.concatenate([*ends, jnp.zeros((6, along), f32)], axis=0)
        faces.append((scaling_ref[z], mid, total, outer))
    for n in range(4):
        bottom, top = faces[0][n], faces[levels - 1][n]
        at = slice(n * across, n * across + bottom.shape[0])
        first_ref[at] = jnp.where(even, top, bottom)
        second_ref[at] = jnp.where(even, bottom, top)


def faces_of(cells, lines):
    _, levels, across, along = cells.shape
    vmem = pl.BlockSpec(memory_space=pltpu.VMEM)
    face = jax.ShapeDtypeStruct((3 * across + 8, along), f32)
    return pl.pallas_call(
        faces_kernel,
        out_shape=(
            jax.ShapeDtypeStruct((levels, across, along), f32),
            face,
            face,
        ),
        in_specs=[vmem] * 3,
        out_specs=(vmem,) * 3,
        compiler_params=pltpu.CompilerParams(vmem_limit_bytes=8 * MIB),
        name="faces",
    )(cells, *lines)


def right_side_kernel(
    own_ref, shared_ref, side_a, side_b, height_a, height_b, cells_ref, scaling_ref, line_a, line_b, face_a, face_b,
    rhs_ref, near_ref, far_ref, dots_ref, first, second,
):
    levels, across, along = scaling_ref.shape
    edge = 8
    wide = across + 2 * edge
    inner = slice(edge, edge + across)
    quarters = along // LANES
    left, right, below, above, even, even_c = position()

    def low_of(is_even, one, two):
        return jnp.where(is_even, two, one)

    def high_of(is_even, one, two):
        return jnp.where(is_even, one, two)

    lane = lax.broadcasted_iota(i32, (1, LANES), 1)
    tiles = 16
    shift_q, shift_x = quarters.bit_length() - 1, across.bit_length() - 1
    for level, choose, present in ((0, low_of, below), (levels, None, None), (2 * levels, high_of, above)):
        if choose is None:
            parts = [low_of(even_c, side_a[...], side_b[...]), shared_ref[...], high_of(even_c, side_a[...], side_b[...])]
            values = [parts[0][0:tiles], own_ref[...], parts[2][0:tiles]]
        else:
            block = [
                choose(even, height_a[k * ROWS_OUT : (k + 1) * ROWS_OUT], height_b[k * ROWS_OUT : (k + 1) * ROWS_OUT])
                for k in range(3)
            ]
            parts = [low_of(even_c, block[1], block[2]), block[0], high_of(even_c, block[1], block[2])]
            values = [part[0:tiles] for part in parts]
        code = jnp.full((1, LANES), -1, i32)
        for n, part in enumerate(parts):
            owner = part[tiles : tiles + 1].astype(i32)
            x = ((owner >> shift_q) & (across - 1)) + (edge + (n - 1) * across)
            z = owner >> (shift_q + shift_x)
            here = ((lane >> 4) == n) | ((lane >> 4) == n + 3)
            here = here & (x >= edge - 2) & (x < edge + across + 2)
            if n == 0:
                here = here & left
            if n == 2:
                here = here & right
            if present is not None:
                here = here & present
            code = jnp.where(here, (z * wide + x) * quarters + (owner & (quarters - 1)), code)
        values = jnp.concatenate(values, axis=0)
        high = values.astype(bf16)
        low = (values - high.astype(f32)).astype(bf16)
        values = jnp.concatenate([high, low, jnp.zeros((LANES - 6 * tiles, LANES), bf16)], axis=0)
        spot = lax.broadcasted_iota(i32, (levels * wide, LANES), 0) * quarters
        for k in range(quarters):
            table = jnp.where(code == spot + k, 1.0, 0.0).astype(bf16)
            added = jnp.dot(table, values, preferred_element_type=f32)
            for z in range(levels):
                first[level + z, :, k * LANES : (k + 1) * LANES] = -added[z * wide : (z + 1) * wide]

    second[:, 0:edge, :] = jnp.zeros((3 * levels, edge, along), f32)
    second[:, edge + across :, :] = jnp.zeros((3 * levels, edge, along), f32)
    for z in range(levels):
        rhs = cells_ref[0, z] + first[levels + z, inner]
        rhs_ref[z] = rhs
        first[levels + z, inner] = scaling_ref[z] * rhs
        for choose, start, present, beside_at in ((low_of, edge - 2, left, 1), (high_of, edge + across, right, 0)):
            for k in range(2):
                x = slice(start + k, start + k + 1)
                for q in range(quarters):
                    part = slice(q * LANES, (q + 1) * LANES)
                    kinds = [
                        choose(even_c, *[line_at(lines, z, k, kind, q, quarters) for lines in (line_a, line_b)])
                        for kind in range(2)
                    ]
                    m = jnp.where(present, 1.0 / (6.0 + kinds[1]), 0.0)
                    first[levels + z, x, part] += m * kinds[0]
                    if k == beside_at:
                        second[levels + z, x, part] = m
    place = lax.broadcasted_iota(i32, (wide, along), 1)

    def beside(ref, z):
        mid = ref[z]
        total = ref[z - 1] + ref[z + 1] + pltpu.roll(mid, 1, 0) + pltpu.roll(mid, wide - 1, 0)
        total = total + jnp.where(place > 0, pltpu.roll(mid, 1, 1), 0.0)
        return total + jnp.where(place < along - 1, pltpu.roll(mid, along - 1, 1), 0.0)

    for z, choose, present in ((levels - 1, low_of, below), (2 * levels, high_of, above)):
        part = [slice(n * across, (n + 1) * across) for n in range(3)]
        near = beside(first, z)[inner] + choose(even, face_a[part[2]], face_b[part[2]])
        second[z, inner] = jnp.where(present, choose(even, face_a[part[0]], face_b[part[0]]) * near, 0.0)
        first[z, inner] += jnp.where(present, choose(even, face_a[part[1]], face_b[part[1]]), 0.0)
        for n, x in enumerate((edge - 1, edge + across)):
            line = slice(3 * across + n, 3 * across + n + 1)
            first[z, x : x + 1] += jnp.where(present, choose(even, face_a[line], face_b[line]), 0.0)

    dots = [jnp.zeros((8, LANES), f32)] * 4

    def folded(value):
        value = jnp.sum(value.reshape(across // 8, 8, along), axis=0)
        return sum(value[:, k * LANES : (k + 1) * LANES] for k in range(quarters))

    ends = (slice(0, edge), slice(edge + across, wide))
    for z in range(levels, 2 * levels):
        near = beside(first, z)
        for end in ends:
            second[z, end] = second[z, end] * near[end]
        near = near[inner]
        scaled = scaling_ref[z - levels] * near
        second[z, inner] = scaled
        near_ref[z - levels] = near
        start = first[z, inner]
        dots[0] = dots[0] + folded(start * rhs_ref[z - levels])
        dots[1] = dots[1] + folded(start * near)
        dots[2] = dots[2] + folded(scaled * near)
    for z in range(levels, 2 * levels):
        far = beside(second, z)[inner]
        far_ref[z - levels] = far
        dots[3] = dots[3] + folded(second[z, inner] * far)
    line = jnp.zeros((1, LANES), f32)
    for k in range(4):
        total = jnp.sum(jnp.sum(dots[k], axis=0, keepdims=True), axis=1, keepdims=True)
        line = jnp.where(lane == k, total, line)
    dots_ref[...] = jnp.broadcast_to(line, dots_ref.shape)


def right_side_of(own, shared, side, height, cells, scaling, lines, faces, devices):
    levels, across, along = scaling.shape
    vmem = pl.BlockSpec(memory_space=pltpu.VMEM)
    whole = pltpu.VMEM((3 * levels, across + 16, along), f32)
    return pl.pallas_call(
        right_side_kernel,
        out_shape=(jax.ShapeDtypeStruct(scaling.shape, f32),) * 3 + (jax.ShapeDtypeStruct((devices, LANES), f32),),
        in_specs=[vmem] * 12,
        out_specs=(vmem,) * 4,
        scratch_shapes=[whole] * 2,
        compiler_params=pltpu.CompilerParams(vmem_limit_bytes=16 * MIB),
        name="right_side",
    )(own, shared, *side, *height, cells, scaling, *lines, *faces)


def results_kernel(
    keeps_ref, places_ref, dots_ref, rhs_ref, near_ref, far_ref, scaling_ref, settled_ref, height_a, height_b,
    positions_out, velocities_out, pressure_out, residual_out, positions, velocities, pressure, residual, sent,
):
    rows, cols = settled_ref.shape[:2]
    levels = rhs_ref.shape[0]
    even = position()[4]
    for r in range(1, rows):
        for c in range(cols):
            kept = settled_ref[r, c]
            if r == rows - 1:
                kept = kept * keeps_ref[c : c + 1]
            for d in range(3):
                positions[d, r, c : c + 1] = kept[d : d + 1]
                velocities[d, r, c : c + 1] = kept[d + 3 : d + 4]
    start = 3 * ROWS_OUT
    for d in range(6):
        block = slice(start + d * cols, start + (d + 1) * cols)
        tiles = jnp.where(even, height_b[block], height_a[block])
        target = positions if d < 3 else velocities
        target[d % 3, 0] = sum(places_ref[k] * tiles[k : k + 1] for k in range(cols))
    copies = [
        pltpu.make_async_copy(positions, positions_out, sent.at[0]),
        pltpu.make_async_copy(velocities, velocities_out, sent.at[1]),
    ]
    for copy in copies:
        copy.start()
    totals = jnp.sum(dots_ref[...], axis=0, keepdims=True)
    g00, g01, g11, g12 = [totals[:, k : k + 1] for k in range(4)]
    ratio = g01 / g00
    alpha = g00 / (g00 - g01)
    square = alpha * alpha
    renewed = square * (g11 - ratio * g01)
    beta = renewed / g00
    crossed = square * (ratio * ratio * g01 - 2.0 * ratio * g11 + g12)
    curvature = renewed - crossed - beta * renewed / alpha
    later = renewed / curvature
    one = alpha + later * (1.0 - alpha + beta)
    two = later * alpha
    for z in range(levels):
        rhs, near = rhs_ref[z], near_ref[z]
        pressure[z] = scaling_ref[z] * (one * rhs + two * near)
        residual[z] = (1.0 - one) * rhs + (one - two) * near + two * far_ref[z]
        for n, (source, target) in enumerate(((pressure, pressure_out), (residual, residual_out))):
            copy = pltpu.make_async_copy(source.at[z], target.at[z], sent.at[2 + 2 * z + n])
            copy.start()
            copies.append(copy)
    for copy in copies:
        copy.wait()


def results_of(keeps, places, dots, rhs, near, far, scaling, settled, height):
    rows, cols = settled.shape[:2]
    smem = pl.BlockSpec(memory_space=pltpu.SMEM)
    vmem = pl.BlockSpec(memory_space=pltpu.VMEM)
    particle = jax.ShapeDtypeStruct((3, rows, cols, LANES), f32)
    field = jax.ShapeDtypeStruct(rhs.shape, f32)
    return pl.pallas_call(
        results_kernel,
        out_shape=(particle, particle, field, field),
        in_specs=[vmem] * 10,
        out_specs=(pl.BlockSpec(memory_space=pl.ANY),) * 4,
        scratch_shapes=[
            *[pltpu.VMEM(particle.shape, f32)] * 2,
            *[pltpu.VMEM(field.shape, f32)] * 2,
            pltpu.SemaphoreType.DMA((2 + 2 * rhs.shape[0],)),
        ],
        compiler_params=pltpu.CompilerParams(vmem_limit_bytes=8 * MIB),
        name="results",
    )(keeps, places, dots, rhs, near, far, scaling, settled, *height)


def on_device(
    positions, velocities, contacts, exit_flags, inlet_slots, cell_blocks, cell_slots, gas_source, diagonal
):
    heights, groups = lax.axis_size("height"), lax.axis_size("cols")
    h, c = lax.axis_index("height"), lax.axis_index("cols")
    *sides, flags, ints, slots, state, cells = packed(
        exit_flags, cell_blocks, inlet_slots, positions, velocities, contacts.transpose(1, 2, 0), cell_slots,
        gas_source, diagonal,
    )
    lines = [
        lax.ppermute(value, ("height", "cols"), matching(heights, groups, "cols", odd, True))
        for value, odd in zip(sides, (False, True))
    ]
    rows, cols = state.shape[1:3]
    picks, keeps, places, weights, owners = marks_of(ints, cells, rows * cols, cols)
    window = merged(state, flags, lines, owners)
    beside = exchanged(window, "height", False)
    own_parts = own_sums(window, *state.shape[1:3])
    scaling, *faces = faces_of(cells, lines)
    faces, beside = lax.optimization_barrier((faces, beside))
    faces = [
        lax.ppermute(value, ("height", "cols"), matching(heights, groups, "height", odd, False))
        for value, odd in zip(faces, (False, True))
    ]
    settled, leaving = particles(picks, *beside, own_parts)
    own, shared = deposits(settled, slots, weights, owners)
    near = exchanged(shared, "cols", True)
    parcel = jnp.concatenate([shared, *near, leaving.reshape(-1, LANES)], axis=0)
    parcels = exchanged(parcel, "height", True)
    rhs, first, second, dots = right_side_of(
        own, shared, near, parcels, cells, scaling, lines, faces, heights * groups
    )
    dots = lax.all_to_all(dots, ("height", "cols"), 0, 0, tiled=True)
    return results_of(keeps, places, dots, rhs, first, second, scaling, settled, parcels)


def solution(mesh):
    in_specs = (
        P(None, "height", "cols", None),
        P(None, "height", "cols", None),
        P(None, "height", "cols"),
        P("height", "cols"),
        P("height", "cols"),
        P("height", "cols"),
        P("height", "cols", None),
        P("height", "cols", None),
        P("height", "cols", None),
    )
    out_specs = (
        P(None, "height", "cols", None),
        P(None, "height", "cols", None),
        P("height", "cols", None),
        P("height", "cols", None),
    )
    return jax.shard_map(
        on_device, mesh=mesh, in_specs=in_specs, out_specs=out_specs, check_vma=False
    )
```

```python
import functools
import jax
import jax.numpy as jnp
from jax import lax
from jax.experimental import pallas as pl
from jax.experimental.pallas import tpu as pltpu
from jax.sharding import PartitionSpec as P

f32, bf16, i32 = jnp.float32, jnp.bfloat16, jnp.int32
spring = 0.05
cutoff_sq = 1.44
damping = 0.5
step_dt = 0.05
gravity = 1.0
deposit_gain = 2.0
LANES = 128
COMPS = 8
DEPTH = 2
ROWS_OUT = 24
FLAG_LANES = 16
MIB = 1024 * 1024
NEARS = 6
EXITS, OWNERS, INLETS = 0, 16, 32


def rounded(value):
    return value.astype(bf16).astype(f32)


def rounded_pair(value):
    high = rounded(value)
    return high, rounded(value - high)


def split(value):
    high = rounded(value)
    mid = rounded(value - high)
    return high, mid, value - high - mid


def centred(tile, r, c, rows, wide):
    row = lax.broadcasted_iota(i32, (COMPS, LANES), 0)
    side = jnp.float32(c - wide // 2)
    up = (r - rows // 2).astype(f32)
    return tile + jnp.where(row == 0, side, jnp.where(row == 2, up, 0.0))


def place_parts(tile, r, c, rows, wide):
    row = lax.broadcasted_iota(i32, (COMPS, LANES), 0)
    place = jnp.where(row < 3, centred(tile, r, c, rows, wide), 0.0)
    high, mid = rounded_pair(place)
    place = high + mid
    return high, mid, -jnp.sum(place * place, axis=0, keepdims=True)


def source_features(tile, r, c, rows, wide):
    row = lax.broadcasted_iota(i32, (COMPS, LANES), 0)
    row32 = lax.broadcasted_iota(i32, (32, LANES), 0)
    high, mid, size = place_parts(tile, r, c, rows, wide)
    size_high, size_mid, size_low = split(size)
    first = jnp.where(row < 3, high, 1.0)
    first = jnp.where(row == 3, size_high, jnp.where(row == 4, size_mid, jnp.where(row == 5, size_low, first)))
    second = jnp.where(row < 3, high, jnp.where(row == 3, 1.0, 0.0))
    kind = lax.rem(r, 3) * 4 + c % 4
    kind = kind + jnp.where(kind < 4, 12, jnp.where(kind < 9, 15, 18))
    near = jnp.concatenate([first, second, mid, mid], axis=0) + jnp.where(row32 == kind, 1.0, 0.0)
    high, mid, low = split(centred(tile, r, c, rows, wide) - damping * pltpu.roll(tile, 5, 0))
    first = jnp.where(row < 3, high, jnp.where(row == 3, 1.0, 0.0))
    second = jnp.where(row < 3, mid, jnp.where(row < 4, 0.0, pltpu.roll(low, 4, 0)))
    return near, jnp.concatenate([first, second], axis=0).astype(bf16)


def target_features(tile, r, c, rows, wide):
    row = lax.broadcasted_iota(i32, (COMPS, LANES), 0)
    row32 = lax.broadcasted_iota(i32, (32, LANES), 0)
    lane32 = lax.broadcasted_iota(i32, (32, LANES), 1)
    high, mid, size = place_parts(tile, r, c, rows, wide)
    own_high, own_mid, own_low = split(cutoff_sq + size)
    first = jnp.where(row < 3, 2.0 * high, jnp.where(row < 6, 1.0, jnp.where(row == 6, own_high, own_mid)))
    second = jnp.where(row < 3, 2.0 * mid, jnp.where(row == 3, own_low, 0.0))
    third = jnp.where(row < 3, 2.0 * high, 0.0)
    fourth = jnp.where(row < 3, 2.0 * mid, 0.0)
    kind = jnp.where(row32 < 16, row32 - 12, jnp.where(row32 < 24, row32 - 15, row32 - 18))
    is_kind = ((row32 >= 12) & (row32 < 16)) | ((row32 >= 19) & (row32 < 24)) | ((row32 >= 27) & (row32 < 30))
    kind_row = jnp.where(kind < 4, 0, jnp.where(kind < 8, 1, 2))
    up = kind_row + lax.rem(4 - lax.rem(r, 3), 3)
    up = jnp.where(up > 2, up - 3, up)
    side = kind - 4 * kind_row + (5 - c % 4) % 4
    side = jnp.where(side > 3, side - 4, side)
    if DEPTH <= c < wide - DEPTH:
        start = (c - DEPTH) * FLAG_LANES
    else:
        start = (lax.rem(r, DEPTH) * DEPTH + c % 2) * FLAG_LANES
    wanted = jnp.where(side < 3, 3 * up + side + start, LANES)
    flags = jnp.sum(jnp.where(lane32 == wanted, tile[6:7, :], 0.0), axis=1, keepdims=True)
    barred = jnp.where(is_kind, -1024.0 * (1.0 - flags), 0.0)
    return jnp.concatenate([first, second, third, fourth], axis=0) + barred


def unit_operands(tiles, r, c, rows, wide):
    features = [target_features(tile, r, c + k, rows, wide) for k, tile in enumerate(tiles)]
    features = jnp.concatenate(features, axis=1).astype(bf16)
    start = (c - 1) // 4
    ends = (c - 1, c + 2)

    def spread(part, s):
        at = 4 * (s // 4 - start) + s % 4
        return jnp.concatenate([part if k == at else jnp.zeros_like(part) for k in range(8)], axis=0)

    halves = [spread(features[:, k * LANES : (k + 1) * LANES], s) for k, s in enumerate(ends)]
    return [spread(features, c), spread(features, c + 1), jnp.concatenate(halves, axis=1)]


def pulls_row(tiles, r, columns, source_rows, rows, wide, turned, pulled, nears, founds):
    ahead = len(nears) - 1
    count = len(source_rows)
    units = [(pair, kind, i) for pair in range(len(columns)) for kind in range(3) for i in range(count)]
    blocks = wide // 4
    operands = [None] * len(columns)

    def begin(n):
        pair, kind, i = units[n]
        c = columns[pair]
        staged = (3 * pair + kind) % 2
        if i == 0:
            if kind == 0:
                operands[pair] = unit_operands(tiles[pair], r, c, rows, wide)
            pltpu.matmul_push_rhs(operands[pair][kind], staged, 0)
        start = (c - 1) // 4
        after = start + 1 if start + 1 < blocks else 0
        row = source_rows[i]
        sources = jnp.concatenate([turned(row)[start], turned(row)[after]], axis=1)
        pltpu.matmul_acc_lhs(nears[n % len(nears)], sources, load_staged_rhs=staged if i == 0 else None)

    def finish(n):
        pair, kind, i = units[n]
        c = columns[pair]
        weight = jnp.maximum(pltpu.matmul_pop(nears[n % len(nears)]), 0.0)
        high = weight.astype(bf16)
        low = (weight - high.astype(f32)).astype(bf16)
        pltpu.matmul_push_rhs(jnp.concatenate([high, low], axis=0), n % 2, 1)
        of_row = pulled(source_rows[i])
        if kind < 2:
            pulls = of_row[c + kind]
        else:
            pulls = jnp.concatenate([of_row[c - 1], of_row[c + 2]], axis=0)
        pulls = jnp.concatenate([pulls, pulls], axis=1)
        pltpu.matmul_acc_lhs(founds[2 * pair + (kind == 2)], pulls, load_staged_rhs=n % 2)

    for n in range(len(units) + ahead):
        if n < len(units):
            begin(n)
        if n >= ahead:
            finish(n - ahead)
    totals = []
    for pair in range(len(columns)):
        inner, outer = pltpu.matmul_pop(founds[2 * pair]), pltpu.matmul_pop(founds[2 * pair + 1])
        totals.append(inner + jnp.concatenate([outer[0:16, 0:LANES], outer[16:32, LANES:]], axis=1))
    return totals


def forces_of(totals, tiles, r, columns, rows, wide):
    forces = []
    for pair, c in enumerate(columns):
        for k, tile in enumerate(tiles[pair]):
            total = totals[pair][:, k * LANES : (k + 1) * LANES]
            first, second = total[0:8], total[8:16]
            moving = centred(tile, r, c + k, rows, wide) - damping * pltpu.roll(tile, 5, 0)
            forces.append((spring / cutoff_sq) * (moving * first[3:4, :] - first - second - pltpu.roll(second, 4, 0)))
    return forces


def stepped(tile, force):
    row = lax.broadcasted_iota(i32, (COMPS, LANES), 0)
    change = step_dt * force - jnp.where(row == 2, step_dt * gravity, 0.0)
    speeds = tile + pltpu.roll(change, 3, 0)
    places = tile + step_dt * pltpu.roll(speeds, 5, 0)
    return jnp.where(row < 3, places, jnp.where(row < 6, speeds, tile))


def position():
    heights, groups = lax.axis_size("height"), lax.axis_size("cols")
    h, c = lax.axis_index("height"), lax.axis_index("cols")
    return c > 0, c < groups - 1, h > 0, h < heights - 1, lax.rem(h, 2) == 0, lax.rem(c, 2) == 0


def halo_rows(rows, cols, d, r, c):
    wide = cols + 2 * DEPTH
    start = d * rows * wide
    if c < DEPTH:
        return start + rows * cols + r * DEPTH + c
    if c >= cols + DEPTH:
        return start + rows * (cols + DEPTH) + r * DEPTH + c - cols - DEPTH
    return start + r * cols + c - DEPTH


def tiles_of_block(block, place, rows, cols):
    wide = cols + 2 * DEPTH
    flag_row = 6 * rows * wide
    for r in range(rows):
        for c in range(wide):
            for d in range(6):
                row = halo_rows(rows, cols, d, r, c)
                place(r, c, d, block[row : row + 1])
            row = flag_row + (rows if c < DEPTH else rows + 1 if c >= cols + DEPTH else r)
            place(r, c, 6, block[row : row + 1])
            place(r, c, 7, jnp.zeros((1, LANES), f32))


def fill_row(tile_at, r, high, wide, turned_row, pulled_row):
    for block in range(wide // 4):
        near = []
        for c in range(4 * block, 4 * block + 4):
            places, moving = source_features(tile_at(c), r, c, high, wide)
            near.append(places)
            pulled_row[c] = moving
        turned_row[block] = jnp.concatenate(near, axis=0).T.astype(bf16)


def accumulators(wide):
    return (
        *[pltpu.ACC(0)((LANES, 2 * LANES), f32)] * NEARS,
        *[pltpu.ACC(1)((held, 2 * LANES), f32) for _ in range(wide // 2 - 1) for held in (16, 32)],
    )


def emptied(refs):
    for ref in refs:
        pltpu.matmul_pop(ref)
    return refs[:NEARS], refs[NEARS:]


def own_kernel(own_ref, state_ref, turned_ref, pulled_ref, partial_ref, *, rows, cols):
    wide = cols + 2 * DEPTH
    high = rows + 2 * DEPTH
    columns = list(range(1, wide - 1, 2))

    def place(r, c, d, value):
        state_ref[r, c, d : d + 1] = value

    tiles_of_block(own_ref, place, rows, cols)

    def one_row(r, carry):
        fill_row(lambda c: state_ref[r, c], r + DEPTH, high, wide, turned_ref.at[r], pulled_ref.at[r])
        return carry

    lax.fori_loop(0, rows, one_row, 0)

    def sums(*refs):
        nears, founds = emptied(refs)

        def one_sum(r, carry):
            tiles = [[state_ref[r, c], state_ref[r, c + 1]] for c in columns]
            totals = pulls_row(
                tiles, r + DEPTH, columns, list(range(rows)), high, wide,
                lambda row: turned_ref.at[row], lambda row: pulled_ref.at[row], nears, founds,
            )
            for pair, total in enumerate(totals):
                partial_ref[r, pair] = total
            return carry

        lax.fori_loop(0, rows, one_sum, 0)

    pl.run_scoped(sums, *accumulators(wide))


def own_sums(own, rows, cols):
    wide = cols + 2 * DEPTH
    vmem = pl.BlockSpec(memory_space=pltpu.VMEM)
    return pl.pallas_call(
        functools.partial(own_kernel, rows=rows, cols=cols),
        out_shape=(
            jax.ShapeDtypeStruct((rows, wide, COMPS, LANES), f32),
            jax.ShapeDtypeStruct((rows, wide // 4, LANES, LANES), bf16),
            jax.ShapeDtypeStruct((rows, wide, 16, LANES), bf16),
            jax.ShapeDtypeStruct((rows, wide // 2 - 1, 16, 2 * LANES), f32),
        ),
        in_specs=[vmem],
        out_specs=(vmem,) * 4,
        cost_estimate=pl.CostEstimate(flops=4 * 10**9, bytes_accessed=4096, transcendentals=0),
        compiler_params=pltpu.CompilerParams(vmem_limit_bytes=8 * MIB),
        name="own_sums",
    )(own)


def particles_kernel(
    picks_ref, first_ref, second_ref, own_ref, own_turned, own_pulled, partial_ref,
    settled_ref, leaving_ref, state, turned, pulled, begun, begun_turned, begun_pulled, blocks,
    *, rows, cols,
):
    wide = cols + 2 * DEPTH
    high = rows + 2 * DEPTH
    left, right, below, above, even, _ = position()
    one, two = first_ref[...], second_ref[...]
    blocks[0] = jnp.where(below, jnp.where(even, two, one), 0.0)
    blocks[1] = jnp.where(above, jnp.where(even, one, two), 0.0)
    for half, start in ((0, 0), (1, rows + DEPTH)):

        def place(r, c, d, value, start=start):
            state[start + r, c, d : d + 1] = value

        tiles_of_block(blocks.at[half], place, rows, cols)

    def far_row(r):
        fill_row(lambda c: state[r, c], r, high, wide, turned.at[r], pulled.at[r])

    def near_row(n, carry):
        far_row(1 + n * (rows + 1))
        return carry

    lax.fori_loop(0, 2, near_row, 0)
    for r in range(rows):
        state[DEPTH + r] = own_ref[r]
        turned[DEPTH + r] = own_turned[r]
        pulled[DEPTH + r] = own_pulled[r]

    def substeps(*refs):
        nears, founds = emptied(refs)
        sources = dict(turned=lambda row: turned.at[row], pulled=lambda row: pulled.at[row], nears=nears, founds=founds)
        columns = list(range(1, wide - 1, 2))

        later = dict(
            turned=lambda row: begun_turned.at[row], pulled=lambda row: begun_pulled.at[row], nears=nears, founds=founds
        )

        def begun_row(r):
            fill_row(lambda c: begun[r, c], r, high, wide, begun_turned.at[r], begun_pulled.at[r])

        def begin_row(r, totals):
            tiles = [[state[r, c], state[r, c + 1]] for c in columns]
            forces = forces_of(totals, tiles, r, columns, high, wide)
            begun[r, 0] = jnp.zeros((COMPS, LANES), f32)
            begun[r, wide - 1] = jnp.zeros((COMPS, LANES), f32)
            for c in range(1, wide - 1):
                inside = ((r >= DEPTH) | below) & ((r < rows + DEPTH) | above)
                if c < DEPTH:
                    inside = inside & left
                if c >= cols + DEPTH:
                    inside = inside & right
                begun[r, c] = jnp.where(inside, stepped(tiles[(c - 1) // 2][(c - 1) % 2], forces[c - 1]), 0.0)

        def outer_step(n, carry):
            r = 1 + n * (rows + 1)
            begun_row(DEPTH + n * (rows - 1))
            tiles = [[state[r, c], state[r, c + 1]] for c in columns]
            begin_row(r, pulls_row(tiles, r, columns, [r - 1, r, r + 1], high, wide, **sources))
            return carry

        def inner_step(n, carry):
            r = DEPTH + n * (rows - 1)
            far_row(n * (high - 1))
            tiles = [[state[r, c], state[r, c + 1]] for c in columns]
            totals = pulls_row(tiles, r, columns, [1 + n * (rows + 1)], high, wide, **sources)
            begin_row(r, [total + partial_ref[n * (rows - 1), pair] for pair, total in enumerate(totals)])
            return carry

        lax.fori_loop(0, 2, inner_step, 0)
        lax.fori_loop(0, 2, outer_step, 0)

        begun_row(jnp.int32(1))

        def second_step(r, carry):
            columns = list(range(DEPTH, DEPTH + cols, 2))
            tiles = [[begun[r, c], begun[r, c + 1]] for c in columns]
            begun_row(jnp.int32(high - 2))
            totals = pulls_row(tiles, r, columns, [r - 1, r, r + 1], high, wide, **later)
            forces = forces_of(totals, tiles, r, columns, high, wide)
            for c in range(cols):
                settled_ref[r - DEPTH, c] = stepped(tiles[c // 2][c % 2], forces[c])
            return carry

        lax.fori_loop(DEPTH, DEPTH + rows, second_step, 0)

    pl.run_scoped(substeps, *accumulators(wide))

    for k in range(cols):
        tile = jnp.zeros((COMPS, LANES), f32)
        for c in range(cols):
            tile = tile + picks_ref[k, c : c + 1] * settled_ref[rows - 1, c]
        for d in range(6):
            leaving_ref[d, k : k + 1] = tile[d : d + 1]


def particles(picks, first, second, own):
    rows, wide = own[0].shape[:2]
    cols, high = wide - 2 * DEPTH, rows + 2 * DEPTH
    vmem = pl.BlockSpec(memory_space=pltpu.VMEM)
    return pl.pallas_call(
        functools.partial(particles_kernel, rows=rows, cols=cols),
        out_shape=(
            jax.ShapeDtypeStruct((rows, cols, COMPS, LANES), f32),
            jax.ShapeDtypeStruct((6, cols, LANES), f32),
        ),
        in_specs=[vmem] * 7,
        out_specs=(vmem, vmem),
        scratch_shapes=[
            pltpu.VMEM((high, wide, COMPS, LANES), f32),
            pltpu.VMEM((high, wide // 4, LANES, LANES), bf16),
            pltpu.VMEM((high, wide, 16, LANES), bf16),
            pltpu.VMEM((high, wide, COMPS, LANES), f32),
            pltpu.VMEM((high, wide // 4, LANES, LANES), bf16),
            pltpu.VMEM((high, wide, 16, LANES), bf16),
            pltpu.VMEM((2, *first.shape), f32),
        ],
        cost_estimate=pl.CostEstimate(flops=10**10, bytes_accessed=4096, transcendentals=0),
        compiler_params=pltpu.CompilerParams(vmem_limit_bytes=12 * MIB),
        name="particles",
    )(picks, first, second, *own)


def deposit_kernel(settled_ref, slots_ref, weights_ref, owners_ref, own_ref, shared_ref):
    rows, cols = settled_ref.shape[:2]
    row = lax.broadcasted_iota(i32, (16, LANES), 0)
    cell = lax.broadcasted_iota(i32, (LANES, LANES), 0)
    for t in range(rows * cols):
        r, c = t // cols, t % cols
        lift_high, lift_mid, lift_low = split(deposit_gain * settled_ref[r, c, 5:6, :])
        parts = jnp.where(row == 0, lift_high, jnp.where(row == 1, lift_mid, jnp.where(row == 2, lift_low, 0.0)))
        table = jnp.where(cell == slots_ref[r, c : c + 1, :], 1.0, 0.0).astype(bf16)
        gathered = lax.dot_general(parts.astype(bf16), table, (((1,), (1,)), ((), ())), preferred_element_type=f32)
        sums = jnp.sum(gathered, axis=0, keepdims=True)
        own_ref[t : t + 1, :] = sums
        shared_ref[t : t + 1, :] = weights_ref[t : t + 1] * sums
    row = lax.broadcasted_iota(i32, (ROWS_OUT - rows * cols, LANES), 0)
    shared_ref[rows * cols :, :] = jnp.where(row == 0, owners_ref[...], 0.0)


def deposits(settled, slots, weights, owners):
    rows, cols = settled.shape[:2]
    vmem = pl.BlockSpec(memory_space=pltpu.VMEM)
    return pl.pallas_call(
        deposit_kernel,
        out_shape=(
            jax.ShapeDtypeStruct((rows * cols, LANES), f32),
            jax.ShapeDtypeStruct((ROWS_OUT, LANES), f32),
        ),
        in_specs=[vmem] * 4,
        out_specs=(vmem, vmem),
        compiler_params=pltpu.CompilerParams(vmem_limit_bytes=4 * MIB),
        name="deposits",
    )(settled, slots, weights, owners)


def marks_kernel(ints_ref, cells_ref, picks_ref, keeps_ref, places_ref, weights_ref, owners_ref, blocks):
    cols = keeps_ref.shape[0]
    tiles = weights_ref.shape[0]
    _, levels, across, along = cells_ref.shape
    quarters = along // LANES
    for z in range(levels):
        for q in range(quarters):
            blocks[q, z * across : (z + 1) * across] = cells_ref[1, z, :, q * LANES : (q + 1) * LANES]
    lane = lax.broadcasted_iota(i32, (1, LANES), 1)
    row = lax.broadcasted_iota(i32, (cols, LANES), 0)
    owner_row = jnp.zeros((1, LANES), i32)
    for t in range(tiles):
        owner = ints_ref[0, OWNERS + t]
        owner_row = jnp.where(lax.rem(lane, tiles) == t, owner, owner_row)
        line = blocks[owner % quarters, pl.ds(owner // quarters, 1), :]
        weights_ref[t : t + 1, :] = 1.0 / (6.0 + line)
    owners_ref[...] = owner_row.astype(f32)
    picks_ref[...] = jnp.zeros_like(picks_ref)
    count = jnp.int32(0)
    for c in range(cols):
        flag = ints_ref[0, EXITS + tiles - cols + c]
        keeps_ref[c : c + 1] = jnp.broadcast_to(jnp.where(flag > 0, 0.0, 1.0), (1, LANES))
        for k in range(c + 1):
            picks_ref[k, c : c + 1] = jnp.broadcast_to(jnp.where((flag > 0) & (count == k), 1.0, 0.0), (1, LANES))
        count = count + flag
        places_ref[c] = jnp.where(row == ints_ref[0, INLETS + c], 1.0, 0.0)


def marks_of(ints, cells, tiles, cols):
    _, levels, across, along = cells.shape
    smem = pl.BlockSpec(memory_space=pltpu.SMEM)
    vmem = pl.BlockSpec(memory_space=pltpu.VMEM)
    return pl.pallas_call(
        marks_kernel,
        out_shape=(
            jax.ShapeDtypeStruct((cols, cols, LANES), f32),
            jax.ShapeDtypeStruct((cols, LANES), f32),
            jax.ShapeDtypeStruct((cols, cols, LANES), f32),
            jax.ShapeDtypeStruct((tiles, LANES), f32),
            jax.ShapeDtypeStruct((1, LANES), f32),
        ),
        in_specs=[smem, vmem],
        out_specs=(vmem,) * 5,
        scratch_shapes=[pltpu.VMEM((along // LANES, levels * across, LANES), f32)],
        cost_estimate=pl.CostEstimate(flops=10**9, bytes_accessed=4096, transcendentals=0),
        compiler_params=pltpu.CompilerParams(vmem_limit_bytes=4 * MIB),
        name="marks",
    )(ints, cells)


def matching(heights, groups, axis, odd, wrap):
    size = heights if axis == "height" else groups
    pairs = []
    for h in range(heights):
        for c in range(groups):
            i = h if axis == "height" else c
            j = i ^ 1 if not odd else (i + 1 if i % 2 else i - 1)
            if 0 <= j < size or wrap:
                j = j % size
                target = (j, c) if axis == "height" else (h, j)
            else:
                target = (h, c ^ 1) if axis == "height" else (h ^ 1, c)
            pairs.append((h * groups + c, target[0] * groups + target[1]))
    return pairs


def around_pairs(heights, groups):
    pairs = []
    for h in range(heights):
        for c in range(groups):
            target = (heights - 1 - h, c) if h in (0, heights - 1) else (h, c ^ 1)
            pairs.append((h * groups + c, target[0] * groups + target[1]))
    return pairs


def exchanged(value, axis, wrap):
    heights, groups = lax.axis_size("height"), lax.axis_size("cols")
    second, first = [
        lax.ppermute(value, ("height", "cols"), matching(heights, groups, axis, odd, wrap)) for odd in (True, False)
    ]
    return [first, second]


LINES = 32


def begin_kernel(zeros_ref):
    zeros_ref[...] = jnp.zeros_like(zeros_ref)


def begun_zeros():
    return pl.pallas_call(
        begin_kernel,
        out_shape=jax.ShapeDtypeStruct((8, LANES), f32),
        out_specs=pl.BlockSpec(memory_space=pltpu.VMEM),
        cost_estimate=pl.CostEstimate(flops=10**10, bytes_accessed=4096, transcendentals=0),
        compiler_params=pltpu.CompilerParams(vmem_limit_bytes=MIB),
        name="begin",
    )()


def pack_kernel(
    zeros_ref, exits_ref, owners_ref, inlets_ref, positions_ref, velocities_ref, contacts_ref, slots_in, gas_ref,
    diagonal_ref, first_ref, second_ref, flags_ref, ints_ref, slots_ref, state_ref, cells_ref, sides, wide_flags, small,
):
    rows, cols = state_ref.shape[1:3]
    _, levels, across, along = cells_ref.shape
    lane = lax.broadcasted_iota(i32, (1, LANES), 1)
    sides[...] = jnp.zeros_like(sides) + zeros_ref[0:1]
    wide_flags[...] = jnp.zeros_like(wide_flags)
    small[...] = jnp.zeros_like(small)
    state_ref[0:3] = positions_ref[...]
    state_ref[3:6] = velocities_ref[...]
    cells_ref[0] = gas_ref[...]
    cells_ref[1] = diagonal_ref[...]
    slots_ref[...] = slots_in[...]
    small[0:rows, 0:cols] = exits_ref[...]
    small[rows : 2 * rows, 0:cols] = owners_ref[...]
    small[2 * rows : 2 * rows + 1, 0:cols] = inlets_ref[...]
    ints = jnp.zeros((1, LANES), i32)
    for r in range(rows):
        ints = ints + pltpu.roll(small[r : r + 1], EXITS + r * cols, 1)
        ints = ints + pltpu.roll(small[rows + r : rows + r + 1], OWNERS + r * cols, 1)
    ints_ref[...] = ints + pltpu.roll(small[2 * rows : 2 * rows + 1], INLETS, 1)
    wide_flags[:, :, 0 : contacts_ref.shape[2]] = contacts_ref[...].astype(f32)
    flags = []
    for r in range(rows):
        spread = pltpu.roll(wide_flags[r], 0, 1, stride=FLAG_LANES, stride_axis=0)
        flags.append(jnp.sum(spread, axis=0, keepdims=True))
        flags_ref[r : r + 1] = flags[r]
    for side in range(2):
        shown = jnp.zeros((1, LANES), f32)
        for r in range(rows):
            for k in range(DEPTH):
                c = k if side == 0 else cols - DEPTH + k
                for d in range(6):
                    row = d * rows * DEPTH + r * DEPTH + k
                    sides[side, row : row + 1] = state_ref[d, r, c : c + 1]
            turn = (r * DEPTH - (0 if side == 0 else cols - DEPTH)) * FLAG_LANES
            part = pltpu.roll(flags[r], turn % LANES, 1)
            shown = jnp.where(lane // (DEPTH * FLAG_LANES) == r, part, shown)
        sides[side, 6 * rows * DEPTH : 6 * rows * DEPTH + 1] = shown
        for z in range(levels):
            for k in range(2):
                x = k if side == 0 else across - 2 + k
                for kind in range(2):
                    for q in range(along // LANES):
                        row = LINES + ((z * 2 + k) * 2 + kind) * (along // LANES) + q
                        sides[side, row : row + 1] = cells_ref[kind, z, x : x + 1, q * LANES : (q + 1) * LANES]
    even = position()[5]
    first_ref[...] = jnp.where(even, sides[1], sides[0])
    second_ref[...] = jnp.where(even, sides[0], sides[1])


def packed(exits, owners, inlets, positions, velocities, contacts, slots, gas, diagonal):
    levels, across, along = gas.shape
    rows, cols = positions.shape[1:3]
    side = jax.ShapeDtypeStruct((LINES + levels * 4 * (along // LANES), LANES), f32)
    vmem = pl.BlockSpec(memory_space=pltpu.VMEM)
    return pl.pallas_call(
        pack_kernel,
        out_shape=(
            side,
            side,
            jax.ShapeDtypeStruct((rows, LANES), f32),
            jax.ShapeDtypeStruct((1, LANES), i32),
            jax.ShapeDtypeStruct(slots.shape, i32),
            jax.ShapeDtypeStruct((6, rows, cols, LANES), f32),
            jax.ShapeDtypeStruct((2, levels, across, along), f32),
        ),
        in_specs=[vmem] * 10,
        out_specs=(vmem,) * 7,
        scratch_shapes=[
            pltpu.VMEM((2, *side.shape), f32),
            pltpu.VMEM((rows, cols, LANES), f32),
            pltpu.VMEM((8, LANES), i32),
        ],
        compiler_params=pltpu.CompilerParams(vmem_limit_bytes=8 * MIB),
        name="pack",
    )(begun_zeros(), exits, owners, inlets, positions, velocities, contacts, slots, gas, diagonal)


def merge_kernel(state_ref, flags_ref, line_a, line_b, owners_ref, window_ref):
    rows, cols = state_ref.shape[1:3]
    each = rows * (cols + 2 * DEPTH)
    count = 6 * rows * DEPTH
    left, right, _, _, _, even = position()
    one, two = line_a[0 : count + 8], line_b[0 : count + 8]
    low = jnp.where(left, jnp.where(even, two, one), 0.0)
    top = jnp.where(right, jnp.where(even, one, two), 0.0)
    for d in range(6):
        for r in range(rows):
            window_ref[d * each + r * cols : d * each + (r + 1) * cols] = state_ref[d, r]
        at = d * each + rows * cols
        piece = slice(d * rows * DEPTH, (d + 1) * rows * DEPTH)
        window_ref[at : at + rows * DEPTH] = low[piece]
        window_ref[at + rows * DEPTH : at + 2 * rows * DEPTH] = top[piece]
    window_ref[6 * each : 6 * each + 8] = jnp.concatenate(
        [flags_ref[...], low[count : count + 1], top[count : count + 1], jnp.zeros((6 - rows, LANES), f32)], axis=0
    )


def merged(state, flags, lines, owners):
    rows, cols = state.shape[1:3]
    vmem = pl.BlockSpec(memory_space=pltpu.VMEM)
    return pl.pallas_call(
        merge_kernel,
        out_shape=jax.ShapeDtypeStruct((6 * rows * (cols + 2 * DEPTH) + 8, LANES), f32),
        in_specs=[vmem] * 5,
        out_specs=vmem,
        compiler_params=pltpu.CompilerParams(vmem_limit_bytes=4 * MIB),
        name="merge",
    )(state, flags, *lines, owners)


def line_at(lines, z, k, kind, q, quarters):
    row = LINES + ((z * 2 + k) * 2 + kind) * quarters + q
    return lines[row : row + 1]


def faces_kernel(cells_ref, line_a, line_b, scaling_ref, first_ref, second_ref):
    _, levels, across, along = cells_ref.shape
    quarters = along // LANES
    left, right, _, _, even, even_c = position()
    row = lax.broadcasted_iota(i32, (across, along), 0)
    place = lax.broadcasted_iota(i32, (across, along), 1)
    scaled = []
    for z in range(levels):
        scaling_ref[z] = 1.0 / (6.0 + cells_ref[1, z])
        scaled.append(scaling_ref[z] * cells_ref[0, z])
    faces = []
    for z in range(levels):
        ends = []
        for k, present, flip in ((1, left, False), (0, right, True)):
            parts = []
            for q in range(quarters):
                kinds = []
                for kind in range(2):
                    one, two = (line_at(lines, z, k, kind, q, quarters) for lines in (line_a, line_b))
                    kinds.append(jnp.where(even_c, one, two) if flip else jnp.where(even_c, two, one))
                parts.append(jnp.where(present, kinds[0] / (6.0 + kinds[1]), 0.0))
            ends.append(jnp.concatenate(parts, axis=1))
        mid = scaled[z]
        total = scaled[levels - 1 - z]
        total = total + jnp.where(row > 0, pltpu.roll(mid, 1, 0), ends[0])
        total = total + jnp.where(row < across - 1, pltpu.roll(mid, across - 1, 0), ends[1])
        total = total + jnp.where(place > 0, pltpu.roll(mid, 1, 1), 0.0)
        total = total + jnp.where(place < along - 1, pltpu.roll(mid, along - 1, 1), 0.0)
        outer = jnp.concatenate([*ends, jnp.zeros((6, along), f32)], axis=0)
        faces.append((scaling_ref[z], mid, total, outer))
    for n in range(4):
        bottom, top = faces[0][n], faces[levels - 1][n]
        at = slice(n * across, n * across + bottom.shape[0])
        first_ref[at] = jnp.where(even, top, bottom)
        second_ref[at] = jnp.where(even, bottom, top)


def faces_of(cells, lines):
    _, levels, across, along = cells.shape
    vmem = pl.BlockSpec(memory_space=pltpu.VMEM)
    face = jax.ShapeDtypeStruct((3 * across + 8, along), f32)
    return pl.pallas_call(
        faces_kernel,
        out_shape=(
            jax.ShapeDtypeStruct((levels, across, along), f32),
            face,
            face,
        ),
        in_specs=[vmem] * 3,
        out_specs=(vmem,) * 3,
        compiler_params=pltpu.CompilerParams(vmem_limit_bytes=8 * MIB),
        name="faces",
    )(cells, *lines)


EDGE = 8
TILES = 16


def placed(parts, values, present, levels, across, along):
    quarters = along // LANES
    wide = across + 2 * EDGE
    left, right = position()[:2]
    lane = lax.broadcasted_iota(i32, (1, LANES), 1)
    shift_q, shift_x = quarters.bit_length() - 1, across.bit_length() - 1
    code = jnp.full((1, LANES), -1, i32)
    for n, part in enumerate(parts):
        owner = part[TILES : TILES + 1].astype(i32)
        x = ((owner >> shift_q) & (across - 1)) + (EDGE + (n - 1) * across)
        z = owner >> (shift_q + shift_x)
        here = ((lane >> 4) == n) | ((lane >> 4) == n + 3)
        here = here & (x >= EDGE - 2) & (x < EDGE + across + 2)
        if n == 0:
            here = here & left
        if n == 2:
            here = here & right
        if present is not None:
            here = here & present
        code = jnp.where(here, (z * wide + x) * quarters + (owner & (quarters - 1)), code)
    values = jnp.concatenate(values, axis=0)
    high = values.astype(bf16)
    low = (values - high.astype(f32)).astype(bf16)
    values = jnp.concatenate([high, low, jnp.zeros((LANES - 6 * TILES, LANES), bf16)], axis=0)
    spot = lax.broadcasted_iota(i32, (levels * wide, LANES), 0) * quarters
    found = []
    for k in range(quarters):
        table = jnp.where(code == spot + k, 1.0, 0.0).astype(bf16)
        found.append(jnp.dot(table, values, preferred_element_type=f32))
    return found


def low_of(is_even, one, two):
    return jnp.where(is_even, two, one)


def high_of(is_even, one, two):
    return jnp.where(is_even, one, two)


def across_and_along(mid):
    wide, along = mid.shape
    place = lax.broadcasted_iota(i32, (wide, along), 1)
    total = pltpu.roll(mid, 1, 0) + pltpu.roll(mid, wide - 1, 0)
    total = total + jnp.where(place > 0, pltpu.roll(mid, 1, 1), 0.0)
    return total + jnp.where(place < along - 1, pltpu.roll(mid, along - 1, 1), 0.0)


def right_side_kernel(
    own_ref, shared_ref, side_a, side_b, cells_ref, scaling_ref, line_a, line_b, rhs_ref, mid_ref, part_ref, ends_ref
):
    levels, across, along = scaling_ref.shape
    wide = across + 2 * EDGE
    inner = slice(EDGE, EDGE + across)
    quarters = along // LANES
    left, right, _, _, _, even_c = position()
    parts = [low_of(even_c, side_a[...], side_b[...]), shared_ref[...], high_of(even_c, side_a[...], side_b[...])]
    values = [parts[0][0:TILES], own_ref[...], parts[2][0:TILES]]
    for k, found in enumerate(placed(parts, values, None, levels, across, along)):
        for z in range(levels):
            mid_ref[z, :, k * LANES : (k + 1) * LANES] = -found[z * wide : (z + 1) * wide]
    ends_ref[...] = jnp.zeros_like(ends_ref)
    for z in range(levels):
        rhs = cells_ref[0, z] + mid_ref[z, inner]
        rhs_ref[z] = rhs
        mid_ref[z, inner] = scaling_ref[z] * rhs
        for choose, start, present, beside_at, end in (
            (low_of, EDGE - 2, left, 1, EDGE - 1),
            (high_of, EDGE + across, right, 0, EDGE),
        ):
            for k in range(2):
                x = slice(start + k, start + k + 1)
                for q in range(quarters):
                    part = slice(q * LANES, (q + 1) * LANES)
                    kinds = [
                        choose(even_c, *[line_at(lines, z, k, kind, q, quarters) for lines in (line_a, line_b)])
                        for kind in range(2)
                    ]
                    m = jnp.where(present, 1.0 / (6.0 + kinds[1]), 0.0)
                    mid_ref[z, x, part] += m * kinds[0]
                    if k == beside_at:
                        ends_ref[z, end : end + 1, part] = m
    for z in range(levels):
        total = across_and_along(mid_ref[z])
        if z > 0:
            total = total + mid_ref[z - 1]
        if z < levels - 1:
            total = total + mid_ref[z + 1]
        part_ref[z] = total


def right_side_of(own, shared, side, cells, scaling, lines):
    levels, across, along = scaling.shape
    vmem = pl.BlockSpec(memory_space=pltpu.VMEM)
    whole = jax.ShapeDtypeStruct((levels, across + 2 * EDGE, along), f32)
    return pl.pallas_call(
        right_side_kernel,
        out_shape=(
            jax.ShapeDtypeStruct(scaling.shape, f32),
            whole,
            whole,
            jax.ShapeDtypeStruct((levels, 2 * EDGE, along), f32),
        ),
        in_specs=[vmem] * 8,
        out_specs=(vmem,) * 4,
        cost_estimate=pl.CostEstimate(flops=10**9, bytes_accessed=4096, transcendentals=0),
        compiler_params=pltpu.CompilerParams(vmem_limit_bytes=8 * MIB),
        name="right_side",
    )(own, shared, *side, cells, scaling, *lines)


def products_kernel(
    height_b, height_a, rhs_ref, mid_ref, part_ref, ends_ref, scaling_ref, face_a, face_b,
    near_ref, far_ref, dots_ref, outer, second,
):
    levels, across, along = scaling_ref.shape
    wide = across + 2 * EDGE
    inner = slice(EDGE, EDGE + across)
    quarters = along // LANES
    _, _, below, above, even, even_c = position()
    for start, choose, present in ((0, low_of, below), (levels, high_of, above)):
        block = [
            choose(even, height_a[k * ROWS_OUT : (k + 1) * ROWS_OUT], height_b[k * ROWS_OUT : (k + 1) * ROWS_OUT])
            for k in range(3)
        ]
        parts = [low_of(even_c, block[1], block[2]), block[0], high_of(even_c, block[1], block[2])]
        values = [part[0:TILES] for part in parts]
        for k, found in enumerate(placed(parts, values, present, levels, across, along)):
            for z in range(levels):
                outer[start + z, :, k * LANES : (k + 1) * LANES] = -found[z * wide : (z + 1) * wide]
    for n, (layer, far_layer, own_layer, choose, present) in enumerate(
        ((levels - 1, levels - 2, 0, low_of, below), (levels, levels + 1, levels - 1, high_of, above))
    ):
        at = 0 if n == 0 else levels + 1
        second[at, 0:EDGE] = jnp.zeros((EDGE, along), f32)
        second[at, EDGE + across :] = jnp.zeros((EDGE, along), f32)
        part = [slice(n * across, (n + 1) * across) for n in range(3)]
        near = across_and_along(outer[layer]) + outer[far_layer] + mid_ref[own_layer]
        near = near[inner] + choose(even, face_a[part[2]], face_b[part[2]])
        second[at, inner] = jnp.where(present, choose(even, face_a[part[0]], face_b[part[0]]) * near, 0.0)
        outer[layer, inner] += jnp.where(present, choose(even, face_a[part[1]], face_b[part[1]]), 0.0)
        for n, x in enumerate((EDGE - 1, EDGE + across)):
            line = slice(3 * across + n, 3 * across + n + 1)
            outer[layer, x : x + 1] += jnp.where(present, choose(even, face_a[line], face_b[line]), 0.0)

    dots = [jnp.zeros((8, LANES), f32)] * 4

    def folded(value):
        value = jnp.sum(value.reshape(across // 8, 8, along), axis=0)
        return sum(value[:, k * LANES : (k + 1) * LANES] for k in range(quarters))

    for z in range(levels):
        near = part_ref[z]
        if z == 0:
            near = near + outer[levels - 1]
        if z == levels - 1:
            near = near + outer[levels]
        second[z + 1, 0:EDGE] = ends_ref[z, 0:EDGE] * near[0:EDGE]
        second[z + 1, EDGE + across :] = ends_ref[z, EDGE:] * near[EDGE + across :]
        near = near[inner]
        scaled = scaling_ref[z] * near
        second[z + 1, inner] = scaled
        near_ref[z] = near
        start = mid_ref[z, inner]
        dots[0] = dots[0] + folded(start * rhs_ref[z])
        dots[1] = dots[1] + folded(start * near)
        dots[2] = dots[2] + folded(scaled * near)
    for z in range(levels):
        far = (across_and_along(second[z + 1]) + second[z] + second[z + 2])[inner]
        far_ref[z] = far
        dots[3] = dots[3] + folded(second[z + 1, inner] * far)
    lane = lax.broadcasted_iota(i32, (1, LANES), 1)
    line = jnp.zeros((1, LANES), f32)
    for k in range(4):
        total = jnp.sum(jnp.sum(dots[k], axis=0, keepdims=True), axis=1, keepdims=True)
        line = jnp.where(lane == k, total, line)
    dots_ref[...] = jnp.broadcast_to(line, dots_ref.shape)


def products_of(height, rhs, mid, part, ends, scaling, faces, devices):
    levels, across, along = scaling.shape
    vmem = pl.BlockSpec(memory_space=pltpu.VMEM)
    return pl.pallas_call(
        products_kernel,
        out_shape=(jax.ShapeDtypeStruct(scaling.shape, f32),) * 2 + (jax.ShapeDtypeStruct((devices, LANES), f32),),
        in_specs=[vmem] * 9,
        out_specs=(vmem,) * 3,
        scratch_shapes=[
            pltpu.VMEM((2 * levels, across + 2 * EDGE, along), f32),
            pltpu.VMEM((levels + 2, across + 2 * EDGE, along), f32),
        ],
        compiler_params=pltpu.CompilerParams(vmem_limit_bytes=16 * MIB),
        name="products",
    )(*reversed(height), rhs, mid, part, ends, scaling, *faces)


def results_kernel(
    keeps_ref, places_ref, dots_ref, rhs_ref, near_ref, far_ref, scaling_ref, settled_ref, height_a, height_b,
    positions_out, velocities_out, pressure_out, residual_out, positions, velocities, pressure, residual, sent,
):
    rows, cols = settled_ref.shape[:2]
    levels = rhs_ref.shape[0]
    even = position()[4]
    for r in range(1, rows):
        for c in range(cols):
            kept = settled_ref[r, c]
            if r == rows - 1:
                kept = kept * keeps_ref[c : c + 1]
            for d in range(3):
                positions[d, r, c : c + 1] = kept[d : d + 1]
                velocities[d, r, c : c + 1] = kept[d + 3 : d + 4]
    start = 3 * ROWS_OUT
    for d in range(6):
        block = slice(start + d * cols, start + (d + 1) * cols)
        tiles = jnp.where(even, height_b[block], height_a[block])
        target = positions if d < 3 else velocities
        target[d % 3, 0] = sum(places_ref[k] * tiles[k : k + 1] for k in range(cols))
    copies = [
        pltpu.make_async_copy(positions, positions_out, sent.at[0]),
        pltpu.make_async_copy(velocities, velocities_out, sent.at[1]),
    ]
    for copy in copies:
        copy.start()
    totals = jnp.sum(dots_ref[...], axis=0, keepdims=True)
    g00, g01, g11, g12 = [totals[:, k : k + 1] for k in range(4)]
    ratio = g01 / g00
    alpha = g00 / (g00 - g01)
    square = alpha * alpha
    renewed = square * (g11 - ratio * g01)
    beta = renewed / g00
    crossed = square * (ratio * ratio * g01 - 2.0 * ratio * g11 + g12)
    curvature = renewed - crossed - beta * renewed / alpha
    later = renewed / curvature
    one = alpha + later * (1.0 - alpha + beta)
    two = later * alpha
    for z in range(levels):
        rhs, near = rhs_ref[z], near_ref[z]
        pressure[z] = scaling_ref[z] * (one * rhs + two * near)
        residual[z] = (1.0 - one) * rhs + (one - two) * near + two * far_ref[z]
        for n, (source, target) in enumerate(((pressure, pressure_out), (residual, residual_out))):
            copy = pltpu.make_async_copy(source.at[z], target.at[z], sent.at[2 + 2 * z + n])
            copy.start()
            copies.append(copy)
    for copy in copies:
        copy.wait()


def results_of(keeps, places, dots, rhs, near, far, scaling, settled, height):
    rows, cols = settled.shape[:2]
    smem = pl.BlockSpec(memory_space=pltpu.SMEM)
    vmem = pl.BlockSpec(memory_space=pltpu.VMEM)
    particle = jax.ShapeDtypeStruct((3, rows, cols, LANES), f32)
    field = jax.ShapeDtypeStruct(rhs.shape, f32)
    return pl.pallas_call(
        results_kernel,
        out_shape=(particle, particle, field, field),
        in_specs=[vmem] * 10,
        out_specs=(pl.BlockSpec(memory_space=pl.ANY),) * 4,
        scratch_shapes=[
            *[pltpu.VMEM(particle.shape, f32)] * 2,
            *[pltpu.VMEM(field.shape, f32)] * 2,
            pltpu.SemaphoreType.DMA((2 + 2 * rhs.shape[0],)),
        ],
        compiler_params=pltpu.CompilerParams(vmem_limit_bytes=8 * MIB),
        name="results",
    )(keeps, places, dots, rhs, near, far, scaling, settled, *height)


def on_device(
    positions, velocities, contacts, exit_flags, inlet_slots, cell_blocks, cell_slots, gas_source, diagonal
):
    heights, groups = lax.axis_size("height"), lax.axis_size("cols")
    h, c = lax.axis_index("height"), lax.axis_index("cols")
    *sides, flags, ints, slots, state, cells = packed(
        exit_flags, cell_blocks, inlet_slots, positions, velocities, contacts.transpose(1, 2, 0), cell_slots,
        gas_source, diagonal,
    )
    lines = [
        lax.ppermute(value, ("height", "cols"), matching(heights, groups, "cols", odd, True))
        for value, odd in zip(sides, (False, True))
    ]
    rows, cols = state.shape[1:3]
    picks, keeps, places, weights, owners = marks_of(ints, cells, rows * cols, cols)
    window = merged(state, flags, lines, owners)
    beside = exchanged(window, "height", False)
    own_parts = own_sums(window, *state.shape[1:3])
    scaling, *faces = faces_of(cells, lines)
    faces, beside = lax.optimization_barrier((faces, beside))
    faces = [
        lax.ppermute(value, ("height", "cols"), matching(heights, groups, "height", odd, False))
        for value, odd in zip(faces, (False, True))
    ]
    settled, leaving = particles(picks, *beside, own_parts)
    own, shared = deposits(settled, slots, weights, owners)
    near = exchanged(shared, "cols", True)
    parcel = jnp.concatenate([shared, *near, leaving.reshape(-1, LANES)], axis=0)
    parcels = exchanged(parcel, "height", True)
    rhs, mid, part, ends = right_side_of(own, shared, near, cells, scaling, lines)
    first, second, dots = products_of(parcels, rhs, mid, part, ends, scaling, faces, heights * groups)
    dots = lax.all_to_all(dots, ("height", "cols"), 0, 0, tiled=True)
    return results_of(keeps, places, dots, rhs, first, second, scaling, settled, parcels)


def solution(mesh):
    in_specs = (
        P(None, "height", "cols", None),
        P(None, "height", "cols", None),
        P(None, "height", "cols"),
        P("height", "cols"),
        P("height", "cols"),
        P("height", "cols"),
        P("height", "cols", None),
        P("height", "cols", None),
        P("height", "cols", None),
    )
    out_specs = (
        P(None, "height", "cols", None),
        P(None, "height", "cols", None),
        P("height", "cols", None),
        P("height", "cols", None),
    )
    return jax.shard_map(
        on_device, mesh=mesh, in_specs=in_specs, out_specs=out_specs, check_vma=False
    )
```

```python
import functools
import jax
import jax.numpy as jnp
from jax import lax
from jax.experimental import pallas as pl
from jax.experimental.pallas import tpu as pltpu
from jax.sharding import PartitionSpec as P

f32, bf16, i32 = jnp.float32, jnp.bfloat16, jnp.int32
spring = 0.05
cutoff_sq = 1.44
damping = 0.5
step_dt = 0.05
gravity = 1.0
deposit_gain = 2.0
LANES = 128
COMPS = 8
DEPTH = 2
ROWS_OUT = 24
FLAG_LANES = 16
MIB = 1024 * 1024
NEARS = 6
EXITS, OWNERS, INLETS = 0, 16, 32


def rounded(value):
    return value.astype(bf16).astype(f32)


def rounded_pair(value):
    high = rounded(value)
    return high, rounded(value - high)


def split(value):
    high = rounded(value)
    mid = rounded(value - high)
    return high, mid, value - high - mid


def centred(tile, r, c, rows, wide):
    row = lax.broadcasted_iota(i32, (COMPS, LANES), 0)
    side = jnp.float32(c - wide // 2)
    up = (r - rows // 2).astype(f32)
    return tile + jnp.where(row == 0, side, jnp.where(row == 2, up, 0.0))


def place_parts(tile, r, c, rows, wide):
    row = lax.broadcasted_iota(i32, (COMPS, LANES), 0)
    place = jnp.where(row < 3, centred(tile, r, c, rows, wide), 0.0)
    high, mid = rounded_pair(place)
    place = high + mid
    return high, mid, -jnp.sum(place * place, axis=0, keepdims=True)


def source_features(tile, r, c, rows, wide):
    row = lax.broadcasted_iota(i32, (COMPS, LANES), 0)
    row32 = lax.broadcasted_iota(i32, (32, LANES), 0)
    high, mid, size = place_parts(tile, r, c, rows, wide)
    size_high, size_mid, size_low = split(size)
    first = jnp.where(row < 3, high, 1.0)
    first = jnp.where(row == 3, size_high, jnp.where(row == 4, size_mid, jnp.where(row == 5, size_low, first)))
    second = jnp.where(row < 3, high, jnp.where(row == 3, 1.0, 0.0))
    kind = lax.rem(r, 3) * 4 + c % 4
    kind = kind + jnp.where(kind < 4, 12, jnp.where(kind < 9, 15, 18))
    near = jnp.concatenate([first, second, mid, mid], axis=0) + jnp.where(row32 == kind, 1.0, 0.0)
    high, mid, low = split(centred(tile, r, c, rows, wide) - damping * pltpu.roll(tile, 5, 0))
    first = jnp.where(row < 3, high, jnp.where(row == 3, 1.0, 0.0))
    second = jnp.where(row < 3, mid, jnp.where(row < 4, 0.0, pltpu.roll(low, 4, 0)))
    return near, jnp.concatenate([first, second], axis=0).astype(bf16)


def target_features(tile, r, c, rows, wide):
    row = lax.broadcasted_iota(i32, (COMPS, LANES), 0)
    row32 = lax.broadcasted_iota(i32, (32, LANES), 0)
    lane32 = lax.broadcasted_iota(i32, (32, LANES), 1)
    high, mid, size = place_parts(tile, r, c, rows, wide)
    own_high, own_mid, own_low = split(cutoff_sq + size)
    first = jnp.where(row < 3, 2.0 * high, jnp.where(row < 6, 1.0, jnp.where(row == 6, own_high, own_mid)))
    second = jnp.where(row < 3, 2.0 * mid, jnp.where(row == 3, own_low, 0.0))
    third = jnp.where(row < 3, 2.0 * high, 0.0)
    fourth = jnp.where(row < 3, 2.0 * mid, 0.0)
    kind = jnp.where(row32 < 16, row32 - 12, jnp.where(row32 < 24, row32 - 15, row32 - 18))
    is_kind = ((row32 >= 12) & (row32 < 16)) | ((row32 >= 19) & (row32 < 24)) | ((row32 >= 27) & (row32 < 30))
    kind_row = jnp.where(kind < 4, 0, jnp.where(kind < 8, 1, 2))
    up = kind_row + lax.rem(4 - lax.rem(r, 3), 3)
    up = jnp.where(up > 2, up - 3, up)
    side = kind - 4 * kind_row + (5 - c % 4) % 4
    side = jnp.where(side > 3, side - 4, side)
    if DEPTH <= c < wide - DEPTH:
        start = (c - DEPTH) * FLAG_LANES
    else:
        start = (lax.rem(r, DEPTH) * DEPTH + c % 2) * FLAG_LANES
    wanted = jnp.where(side < 3, 3 * up + side + start, LANES)
    flags = jnp.sum(jnp.where(lane32 == wanted, tile[6:7, :], 0.0), axis=1, keepdims=True)
    barred = jnp.where(is_kind, -1024.0 * (1.0 - flags), 0.0)
    return jnp.concatenate([first, second, third, fourth], axis=0) + barred


def unit_operands(tiles, r, c, rows, wide):
    features = [target_features(tile, r, c + k, rows, wide) for k, tile in enumerate(tiles)]
    features = jnp.concatenate(features, axis=1).astype(bf16)
    start = (c - 1) // 4
    ends = (c - 1, c + 2)

    def spread(part, s):
        at = 4 * (s // 4 - start) + s % 4
        return jnp.concatenate([part if k == at else jnp.zeros_like(part) for k in range(8)], axis=0)

    halves = [spread(features[:, k * LANES : (k + 1) * LANES], s) for k, s in enumerate(ends)]
    return [spread(features, c), spread(features, c + 1), jnp.concatenate(halves, axis=1)]


def pulls_row(tiles, r, columns, source_rows, rows, wide, turned, pulled, nears, founds):
    ahead = len(nears) - 1
    count = len(source_rows)
    units = [(pair, kind, i) for pair in range(len(columns)) for kind in range(3) for i in range(count)]
    blocks = wide // 4
    operands = [None] * len(columns)

    def begin(n):
        pair, kind, i = units[n]
        c = columns[pair]
        staged = (3 * pair + kind) % 2
        if i == 0:
            if kind == 0:
                operands[pair] = unit_operands(tiles[pair], r, c, rows, wide)
            pltpu.matmul_push_rhs(operands[pair][kind], staged, 0)
        start = (c - 1) // 4
        after = start + 1 if start + 1 < blocks else 0
        row = source_rows[i]
        sources = jnp.concatenate([turned(row)[start], turned(row)[after]], axis=1)
        pltpu.matmul_acc_lhs(nears[n % len(nears)], sources, load_staged_rhs=staged if i == 0 else None)

    def finish(n):
        pair, kind, i = units[n]
        c = columns[pair]
        weight = jnp.maximum(pltpu.matmul_pop(nears[n % len(nears)]), 0.0)
        high = weight.astype(bf16)
        low = (weight - high.astype(f32)).astype(bf16)
        pltpu.matmul_push_rhs(jnp.concatenate([high, low], axis=0), n % 2, 1)
        of_row = pulled(source_rows[i])
        if kind < 2:
            pulls = of_row[c + kind]
        else:
            pulls = jnp.concatenate([of_row[c - 1], of_row[c + 2]], axis=0)
        pulls = jnp.concatenate([pulls, pulls], axis=1)
        pltpu.matmul_acc_lhs(founds[2 * pair + (kind == 2)], pulls, load_staged_rhs=n % 2)

    for n in range(len(units) + ahead):
        if n < len(units):
            begin(n)
        if n >= ahead:
            finish(n - ahead)
    totals = []
    for pair in range(len(columns)):
        inner, outer = pltpu.matmul_pop(founds[2 * pair]), pltpu.matmul_pop(founds[2 * pair + 1])
        totals.append(inner + jnp.concatenate([outer[0:16, 0:LANES], outer[16:32, LANES:]], axis=1))
    return totals


def forces_of(totals, tiles, r, columns, rows, wide):
    forces = []
    for pair, c in enumerate(columns):
        for k, tile in enumerate(tiles[pair]):
            total = totals[pair][:, k * LANES : (k + 1) * LANES]
            first, second = total[0:8], total[8:16]
            moving = centred(tile, r, c + k, rows, wide) - damping * pltpu.roll(tile, 5, 0)
            forces.append((spring / cutoff_sq) * (moving * first[3:4, :] - first - second - pltpu.roll(second, 4, 0)))
    return forces


def stepped(tile, force):
    row = lax.broadcasted_iota(i32, (COMPS, LANES), 0)
    change = step_dt * force - jnp.where(row == 2, step_dt * gravity, 0.0)
    speeds = tile + pltpu.roll(change, 3, 0)
    places = tile + step_dt * pltpu.roll(speeds, 5, 0)
    return jnp.where(row < 3, places, jnp.where(row < 6, speeds, tile))


def position():
    heights, groups = lax.axis_size("height"), lax.axis_size("cols")
    h, c = lax.axis_index("height"), lax.axis_index("cols")
    return c > 0, c < groups - 1, h > 0, h < heights - 1, lax.rem(h, 2) == 0, lax.rem(c, 2) == 0


def halo_rows(rows, cols, d, r, c):
    wide = cols + 2 * DEPTH
    start = d * rows * wide
    if c < DEPTH:
        return start + rows * cols + r * DEPTH + c
    if c >= cols + DEPTH:
        return start + rows * (cols + DEPTH) + r * DEPTH + c - cols - DEPTH
    return start + r * cols + c - DEPTH


def tiles_of_block(block, place, rows, cols):
    wide = cols + 2 * DEPTH
    flag_row = 6 * rows * wide
    for r in range(rows):
        for c in range(wide):
            for d in range(6):
                row = halo_rows(rows, cols, d, r, c)
                place(r, c, d, block[row : row + 1])
            row = flag_row + (rows if c < DEPTH else rows + 1 if c >= cols + DEPTH else r)
            place(r, c, 6, block[row : row + 1])
            place(r, c, 7, jnp.zeros((1, LANES), f32))


def fill_row(tile_at, r, high, wide, turned_row, pulled_row):
    for block in range(wide // 4):
        near = []
        for c in range(4 * block, 4 * block + 4):
            places, moving = source_features(tile_at(c), r, c, high, wide)
            near.append(places)
            pulled_row[c] = moving
        turned_row[block] = jnp.concatenate(near, axis=0).T.astype(bf16)


def accumulators(wide):
    return (
        *[pltpu.ACC(0)((LANES, 2 * LANES), f32)] * NEARS,
        *[pltpu.ACC(1)((held, 2 * LANES), f32) for _ in range(wide // 2 - 1) for held in (16, 32)],
    )


def emptied(refs):
    for ref in refs:
        pltpu.matmul_pop(ref)
    return refs[:NEARS], refs[NEARS:]


def own_kernel(own_ref, state_ref, turned_ref, pulled_ref, partial_ref, *, rows, cols):
    wide = cols + 2 * DEPTH
    high = rows + 2 * DEPTH
    columns = list(range(1, wide - 1, 2))

    def place(r, c, d, value):
        state_ref[r, c, d : d + 1] = value

    tiles_of_block(own_ref, place, rows, cols)

    def one_row(r, carry):
        fill_row(lambda c: state_ref[r, c], r + DEPTH, high, wide, turned_ref.at[r], pulled_ref.at[r])
        return carry

    lax.fori_loop(0, rows, one_row, 0)

    def sums(*refs):
        nears, founds = emptied(refs)

        def one_sum(r, carry):
            tiles = [[state_ref[r, c], state_ref[r, c + 1]] for c in columns]
            totals = pulls_row(
                tiles, r + DEPTH, columns, list(range(rows)), high, wide,
                lambda row: turned_ref.at[row], lambda row: pulled_ref.at[row], nears, founds,
            )
            for pair, total in enumerate(totals):
                partial_ref[r, pair] = total
            return carry

        lax.fori_loop(0, rows, one_sum, 0)

    pl.run_scoped(sums, *accumulators(wide))


def own_sums(own, rows, cols):
    wide = cols + 2 * DEPTH
    vmem = pl.BlockSpec(memory_space=pltpu.VMEM)
    return pl.pallas_call(
        functools.partial(own_kernel, rows=rows, cols=cols),
        out_shape=(
            jax.ShapeDtypeStruct((rows, wide, COMPS, LANES), f32),
            jax.ShapeDtypeStruct((rows, wide // 4, LANES, LANES), bf16),
            jax.ShapeDtypeStruct((rows, wide, 16, LANES), bf16),
            jax.ShapeDtypeStruct((rows, wide // 2 - 1, 16, 2 * LANES), f32),
        ),
        in_specs=[vmem],
        out_specs=(vmem,) * 4,
        cost_estimate=pl.CostEstimate(flops=4 * 10**9, bytes_accessed=4096, transcendentals=0),
        compiler_params=pltpu.CompilerParams(vmem_limit_bytes=8 * MIB),
        name="own_sums",
    )(own)


def particles_kernel(
    picks_ref, first_ref, second_ref, own_ref, own_turned, own_pulled, partial_ref,
    settled_ref, leaving_ref, state, turned, pulled, begun, begun_turned, begun_pulled, blocks,
    *, rows, cols,
):
    wide = cols + 2 * DEPTH
    high = rows + 2 * DEPTH
    left, right, below, above, even, _ = position()
    one, two = first_ref[...], second_ref[...]
    blocks[0] = jnp.where(below, jnp.where(even, two, one), 0.0)
    blocks[1] = jnp.where(above, jnp.where(even, one, two), 0.0)
    for half, start in ((0, 0), (1, rows + DEPTH)):

        def place(r, c, d, value, start=start):
            state[start + r, c, d : d + 1] = value

        tiles_of_block(blocks.at[half], place, rows, cols)

    def far_row(r):
        fill_row(lambda c: state[r, c], r, high, wide, turned.at[r], pulled.at[r])

    def near_row(n, carry):
        far_row(1 + n * (rows + 1))
        return carry

    lax.fori_loop(0, 2, near_row, 0)
    for r in range(rows):
        state[DEPTH + r] = own_ref[r]
        turned[DEPTH + r] = own_turned[r]
        pulled[DEPTH + r] = own_pulled[r]

    def substeps(*refs):
        nears, founds = emptied(refs)
        sources = dict(turned=lambda row: turned.at[row], pulled=lambda row: pulled.at[row], nears=nears, founds=founds)
        columns = list(range(1, wide - 1, 2))

        later = dict(
            turned=lambda row: begun_turned.at[row], pulled=lambda row: begun_pulled.at[row], nears=nears, founds=founds
        )

        def begun_row(r):
            fill_row(lambda c: begun[r, c], r, high, wide, begun_turned.at[r], begun_pulled.at[r])

        def begin_row(r, totals):
            tiles = [[state[r, c], state[r, c + 1]] for c in columns]
            forces = forces_of(totals, tiles, r, columns, high, wide)
            begun[r, 0] = jnp.zeros((COMPS, LANES), f32)
            begun[r, wide - 1] = jnp.zeros((COMPS, LANES), f32)
            for c in range(1, wide - 1):
                inside = ((r >= DEPTH) | below) & ((r < rows + DEPTH) | above)
                if c < DEPTH:
                    inside = inside & left
                if c >= cols + DEPTH:
                    inside = inside & right
                begun[r, c] = jnp.where(inside, stepped(tiles[(c - 1) // 2][(c - 1) % 2], forces[c - 1]), 0.0)

        def outer_step(n, carry):
            r = 1 + n * (rows + 1)
            begun_row(DEPTH + n * (rows - 1))
            tiles = [[state[r, c], state[r, c + 1]] for c in columns]
            begin_row(r, pulls_row(tiles, r, columns, [r - 1, r, r + 1], high, wide, **sources))
            return carry

        def inner_step(n, carry):
            r = DEPTH + n * (rows - 1)
            far_row(n * (high - 1))
            tiles = [[state[r, c], state[r, c + 1]] for c in columns]
            totals = pulls_row(tiles, r, columns, [1 + n * (rows + 1)], high, wide, **sources)
            begin_row(r, [total + partial_ref[n * (rows - 1), pair] for pair, total in enumerate(totals)])
            return carry

        lax.fori_loop(0, 2, inner_step, 0)
        lax.fori_loop(0, 2, outer_step, 0)

        begun_row(jnp.int32(1))

        def second_step(r, carry):
            columns = list(range(DEPTH, DEPTH + cols, 2))
            tiles = [[begun[r, c], begun[r, c + 1]] for c in columns]
            begun_row(jnp.int32(high - 2))
            totals = pulls_row(tiles, r, columns, [r - 1, r, r + 1], high, wide, **later)
            forces = forces_of(totals, tiles, r, columns, high, wide)
            for c in range(cols):
                settled_ref[r - DEPTH, c] = stepped(tiles[c // 2][c % 2], forces[c])
            return carry

        lax.fori_loop(DEPTH, DEPTH + rows, second_step, 0)

    pl.run_scoped(substeps, *accumulators(wide))

    for k in range(cols):
        tile = jnp.zeros((COMPS, LANES), f32)
        for c in range(cols):
            tile = tile + picks_ref[k, c : c + 1] * settled_ref[rows - 1, c]
        for d in range(6):
            leaving_ref[d, k : k + 1] = tile[d : d + 1]


def particles(picks, first, second, own):
    rows, wide = own[0].shape[:2]
    cols, high = wide - 2 * DEPTH, rows + 2 * DEPTH
    vmem = pl.BlockSpec(memory_space=pltpu.VMEM)
    return pl.pallas_call(
        functools.partial(particles_kernel, rows=rows, cols=cols),
        out_shape=(
            jax.ShapeDtypeStruct((rows, cols, COMPS, LANES), f32),
            jax.ShapeDtypeStruct((6, cols, LANES), f32),
        ),
        in_specs=[vmem] * 7,
        out_specs=(vmem, vmem),
        scratch_shapes=[
            pltpu.VMEM((high, wide, COMPS, LANES), f32),
            pltpu.VMEM((high, wide // 4, LANES, LANES), bf16),
            pltpu.VMEM((high, wide, 16, LANES), bf16),
            pltpu.VMEM((high, wide, COMPS, LANES), f32),
            pltpu.VMEM((high, wide // 4, LANES, LANES), bf16),
            pltpu.VMEM((high, wide, 16, LANES), bf16),
            pltpu.VMEM((2, *first.shape), f32),
        ],
        cost_estimate=pl.CostEstimate(flops=10**10, bytes_accessed=4096, transcendentals=0),
        compiler_params=pltpu.CompilerParams(vmem_limit_bytes=12 * MIB),
        name="particles",
    )(picks, first, second, *own)


def deposit_kernel(settled_ref, slots_ref, weights_ref, owners_ref, own_ref, shared_ref):
    rows, cols = settled_ref.shape[:2]
    row = lax.broadcasted_iota(i32, (16, LANES), 0)
    cell = lax.broadcasted_iota(i32, (LANES, LANES), 0)
    for t in range(rows * cols):
        r, c = t // cols, t % cols
        lift_high, lift_mid, lift_low = split(deposit_gain * settled_ref[r, c, 5:6, :])
        parts = jnp.where(row == 0, lift_high, jnp.where(row == 1, lift_mid, jnp.where(row == 2, lift_low, 0.0)))
        table = jnp.where(cell == slots_ref[r, c : c + 1, :], 1.0, 0.0).astype(bf16)
        gathered = lax.dot_general(parts.astype(bf16), table, (((1,), (1,)), ((), ())), preferred_element_type=f32)
        sums = jnp.sum(gathered, axis=0, keepdims=True)
        own_ref[t : t + 1, :] = sums
        shared_ref[t : t + 1, :] = weights_ref[t : t + 1] * sums
    row = lax.broadcasted_iota(i32, (ROWS_OUT - rows * cols, LANES), 0)
    shared_ref[rows * cols :, :] = jnp.where(row == 0, owners_ref[...], 0.0)


def deposits(settled, slots, weights, owners):
    rows, cols = settled.shape[:2]
    vmem = pl.BlockSpec(memory_space=pltpu.VMEM)
    return pl.pallas_call(
        deposit_kernel,
        out_shape=(
            jax.ShapeDtypeStruct((rows * cols, LANES), f32),
            jax.ShapeDtypeStruct((ROWS_OUT, LANES), f32),
        ),
        in_specs=[vmem] * 4,
        out_specs=(vmem, vmem),
        compiler_params=pltpu.CompilerParams(vmem_limit_bytes=4 * MIB),
        name="deposits",
    )(settled, slots, weights, owners)


def marks_kernel(ints_ref, cells_ref, picks_ref, keeps_ref, places_ref, weights_ref, owners_ref, blocks):
    cols = keeps_ref.shape[0]
    tiles = weights_ref.shape[0]
    _, levels, across, along = cells_ref.shape
    quarters = along // LANES
    for z in range(levels):
        for q in range(quarters):
            blocks[q, z * across : (z + 1) * across] = cells_ref[1, z, :, q * LANES : (q + 1) * LANES]
    lane = lax.broadcasted_iota(i32, (1, LANES), 1)
    row = lax.broadcasted_iota(i32, (cols, LANES), 0)
    owner_row = jnp.zeros((1, LANES), i32)
    for t in range(tiles):
        owner = ints_ref[0, OWNERS + t]
        owner_row = jnp.where(lax.rem(lane, tiles) == t, owner, owner_row)
        line = blocks[owner % quarters, pl.ds(owner // quarters, 1), :]
        weights_ref[t : t + 1, :] = 1.0 / (6.0 + line)
    owners_ref[...] = owner_row.astype(f32)
    picks_ref[...] = jnp.zeros_like(picks_ref)
    count = jnp.int32(0)
    for c in range(cols):
        flag = ints_ref[0, EXITS + tiles - cols + c]
        keeps_ref[c : c + 1] = jnp.broadcast_to(jnp.where(flag > 0, 0.0, 1.0), (1, LANES))
        for k in range(c + 1):
            picks_ref[k, c : c + 1] = jnp.broadcast_to(jnp.where((flag > 0) & (count == k), 1.0, 0.0), (1, LANES))
        count = count + flag
        places_ref[c] = jnp.where(row == ints_ref[0, INLETS + c], 1.0, 0.0)


def marks_of(ints, cells, tiles, cols):
    _, levels, across, along = cells.shape
    smem = pl.BlockSpec(memory_space=pltpu.SMEM)
    vmem = pl.BlockSpec(memory_space=pltpu.VMEM)
    return pl.pallas_call(
        marks_kernel,
        out_shape=(
            jax.ShapeDtypeStruct((cols, cols, LANES), f32),
            jax.ShapeDtypeStruct((cols, LANES), f32),
            jax.ShapeDtypeStruct((cols, cols, LANES), f32),
            jax.ShapeDtypeStruct((tiles, LANES), f32),
            jax.ShapeDtypeStruct((1, LANES), f32),
        ),
        in_specs=[smem, vmem],
        out_specs=(vmem,) * 5,
        scratch_shapes=[pltpu.VMEM((along // LANES, levels * across, LANES), f32)],
        cost_estimate=pl.CostEstimate(flops=10**9, bytes_accessed=4096, transcendentals=0),
        compiler_params=pltpu.CompilerParams(vmem_limit_bytes=4 * MIB),
        name="marks",
    )(ints, cells)


def matching(heights, groups, axis, odd, wrap):
    size = heights if axis == "height" else groups
    pairs = []
    for h in range(heights):
        for c in range(groups):
            i = h if axis == "height" else c
            j = i ^ 1 if not odd else (i + 1 if i % 2 else i - 1)
            if 0 <= j < size or wrap:
                j = j % size
                target = (j, c) if axis == "height" else (h, j)
            else:
                target = (h, c ^ 1) if axis == "height" else (h ^ 1, c)
            pairs.append((h * groups + c, target[0] * groups + target[1]))
    return pairs


def around_pairs(heights, groups):
    pairs = []
    for h in range(heights):
        for c in range(groups):
            target = (heights - 1 - h, c) if h in (0, heights - 1) else (h, c ^ 1)
            pairs.append((h * groups + c, target[0] * groups + target[1]))
    return pairs


def exchanged(value, axis, wrap):
    heights, groups = lax.axis_size("height"), lax.axis_size("cols")
    second, first = [
        lax.ppermute(value, ("height", "cols"), matching(heights, groups, axis, odd, wrap)) for odd in (True, False)
    ]
    return [first, second]


LINES = 32


def begin_kernel(zeros_ref):
    zeros_ref[...] = jnp.zeros_like(zeros_ref)


def begun_zeros():
    return pl.pallas_call(
        begin_kernel,
        out_shape=jax.ShapeDtypeStruct((8, LANES), f32),
        out_specs=pl.BlockSpec(memory_space=pltpu.VMEM),
        cost_estimate=pl.CostEstimate(flops=10**10, bytes_accessed=4096, transcendentals=0),
        compiler_params=pltpu.CompilerParams(vmem_limit_bytes=MIB),
        name="begin",
    )()


def pack_kernel(
    zeros_ref, exits_ref, owners_ref, inlets_ref, positions_ref, velocities_ref, contacts_ref, slots_in, gas_ref,
    diagonal_ref, first_ref, second_ref, flags_ref, ints_ref, slots_ref, state_ref, cells_ref, sides, wide_flags, small,
):
    rows, cols = state_ref.shape[1:3]
    _, levels, across, along = cells_ref.shape
    lane = lax.broadcasted_iota(i32, (1, LANES), 1)
    sides[...] = jnp.zeros_like(sides) + zeros_ref[0:1]
    wide_flags[...] = jnp.zeros_like(wide_flags)
    small[...] = jnp.zeros_like(small)
    state_ref[0:3] = positions_ref[...]
    state_ref[3:6] = velocities_ref[...]
    cells_ref[0] = gas_ref[...]
    cells_ref[1] = diagonal_ref[...]
    slots_ref[...] = slots_in[...]
    small[0:rows, 0:cols] = exits_ref[...]
    small[rows : 2 * rows, 0:cols] = owners_ref[...]
    small[2 * rows : 2 * rows + 1, 0:cols] = inlets_ref[...]
    ints = jnp.zeros((1, LANES), i32)
    for r in range(rows):
        ints = ints + pltpu.roll(small[r : r + 1], EXITS + r * cols, 1)
        ints = ints + pltpu.roll(small[rows + r : rows + r + 1], OWNERS + r * cols, 1)
    ints_ref[...] = ints + pltpu.roll(small[2 * rows : 2 * rows + 1], INLETS, 1)
    wide_flags[:, :, 0 : contacts_ref.shape[2]] = contacts_ref[...].astype(f32)
    flags = []
    for r in range(rows):
        spread = pltpu.roll(wide_flags[r], 0, 1, stride=FLAG_LANES, stride_axis=0)
        flags.append(jnp.sum(spread, axis=0, keepdims=True))
        flags_ref[r : r + 1] = flags[r]
    for side in range(2):
        shown = jnp.zeros((1, LANES), f32)
        for r in range(rows):
            for k in range(DEPTH):
                c = k if side == 0 else cols - DEPTH + k
                for d in range(6):
                    row = d * rows * DEPTH + r * DEPTH + k
                    sides[side, row : row + 1] = state_ref[d, r, c : c + 1]
            turn = (r * DEPTH - (0 if side == 0 else cols - DEPTH)) * FLAG_LANES
            part = pltpu.roll(flags[r], turn % LANES, 1)
            shown = jnp.where(lane // (DEPTH * FLAG_LANES) == r, part, shown)
        sides[side, 6 * rows * DEPTH : 6 * rows * DEPTH + 1] = shown
        for z in range(levels):
            for k in range(2):
                x = k if side == 0 else across - 2 + k
                for kind in range(2):
                    for q in range(along // LANES):
                        row = LINES + ((z * 2 + k) * 2 + kind) * (along // LANES) + q
                        sides[side, row : row + 1] = cells_ref[kind, z, x : x + 1, q * LANES : (q + 1) * LANES]
    even = position()[5]
    first_ref[...] = jnp.where(even, sides[1], sides[0])
    second_ref[...] = jnp.where(even, sides[0], sides[1])


def packed(exits, owners, inlets, positions, velocities, contacts, slots, gas, diagonal):
    levels, across, along = gas.shape
    rows, cols = positions.shape[1:3]
    side = jax.ShapeDtypeStruct((LINES + levels * 4 * (along // LANES), LANES), f32)
    vmem = pl.BlockSpec(memory_space=pltpu.VMEM)
    return pl.pallas_call(
        pack_kernel,
        out_shape=(
            side,
            side,
            jax.ShapeDtypeStruct((rows, LANES), f32),
            jax.ShapeDtypeStruct((1, LANES), i32),
            jax.ShapeDtypeStruct(slots.shape, i32),
            jax.ShapeDtypeStruct((6, rows, cols, LANES), f32),
            jax.ShapeDtypeStruct((2, levels, across, along), f32),
        ),
        in_specs=[vmem] * 10,
        out_specs=(vmem,) * 7,
        scratch_shapes=[
            pltpu.VMEM((2, *side.shape), f32),
            pltpu.VMEM((rows, cols, LANES), f32),
            pltpu.VMEM((8, LANES), i32),
        ],
        compiler_params=pltpu.CompilerParams(vmem_limit_bytes=8 * MIB),
        name="pack",
    )(begun_zeros(), exits, owners, inlets, positions, velocities, contacts, slots, gas, diagonal)


def merge_kernel(state_ref, flags_ref, line_a, line_b, owners_ref, window_ref):
    rows, cols = state_ref.shape[1:3]
    each = rows * (cols + 2 * DEPTH)
    count = 6 * rows * DEPTH
    left, right, _, _, _, even = position()
    one, two = line_a[0 : count + 8], line_b[0 : count + 8]
    low = jnp.where(left, jnp.where(even, two, one), 0.0)
    top = jnp.where(right, jnp.where(even, one, two), 0.0)
    for d in range(6):
        for r in range(rows):
            window_ref[d * each + r * cols : d * each + (r + 1) * cols] = state_ref[d, r]
        at = d * each + rows * cols
        piece = slice(d * rows * DEPTH, (d + 1) * rows * DEPTH)
        window_ref[at : at + rows * DEPTH] = low[piece]
        window_ref[at + rows * DEPTH : at + 2 * rows * DEPTH] = top[piece]
    window_ref[6 * each : 6 * each + 8] = jnp.concatenate(
        [flags_ref[...], low[count : count + 1], top[count : count + 1], jnp.zeros((6 - rows, LANES), f32)], axis=0
    )


def merged(state, flags, lines, owners):
    rows, cols = state.shape[1:3]
    vmem = pl.BlockSpec(memory_space=pltpu.VMEM)
    return pl.pallas_call(
        merge_kernel,
        out_shape=jax.ShapeDtypeStruct((6 * rows * (cols + 2 * DEPTH) + 8, LANES), f32),
        in_specs=[vmem] * 5,
        out_specs=vmem,
        compiler_params=pltpu.CompilerParams(vmem_limit_bytes=4 * MIB),
        name="merge",
    )(state, flags, *lines, owners)


def line_at(lines, z, k, kind, q, quarters):
    row = LINES + ((z * 2 + k) * 2 + kind) * quarters + q
    return lines[row : row + 1]


def faces_kernel(cells_ref, line_a, line_b, scaling_ref, first_ref, second_ref):
    _, levels, across, along = cells_ref.shape
    quarters = along // LANES
    left, right, _, _, even, even_c = position()
    row = lax.broadcasted_iota(i32, (across, along), 0)
    place = lax.broadcasted_iota(i32, (across, along), 1)
    scaled = []
    for z in range(levels):
        scaling_ref[z] = 1.0 / (6.0 + cells_ref[1, z])
        scaled.append(scaling_ref[z] * cells_ref[0, z])
    faces = []
    for z in range(levels):
        ends = []
        for k, present, flip in ((1, left, False), (0, right, True)):
            parts = []
            for q in range(quarters):
                kinds = []
                for kind in range(2):
                    one, two = (line_at(lines, z, k, kind, q, quarters) for lines in (line_a, line_b))
                    kinds.append(jnp.where(even_c, one, two) if flip else jnp.where(even_c, two, one))
                parts.append(jnp.where(present, kinds[0] / (6.0 + kinds[1]), 0.0))
            ends.append(jnp.concatenate(parts, axis=1))
        mid = scaled[z]
        total = scaled[levels - 1 - z]
        total = total + jnp.where(row > 0, pltpu.roll(mid, 1, 0), ends[0])
        total = total + jnp.where(row < across - 1, pltpu.roll(mid, across - 1, 0), ends[1])
        total = total + jnp.where(place > 0, pltpu.roll(mid, 1, 1), 0.0)
        total = total + jnp.where(place < along - 1, pltpu.roll(mid, along - 1, 1), 0.0)
        outer = jnp.concatenate([*ends, jnp.zeros((6, along), f32)], axis=0)
        faces.append((scaling_ref[z], mid, total, outer))
    for n in range(4):
        bottom, top = faces[0][n], faces[levels - 1][n]
        at = slice(n * across, n * across + bottom.shape[0])
        first_ref[at] = jnp.where(even, top, bottom)
        second_ref[at] = jnp.where(even, bottom, top)


def faces_of(cells, lines):
    _, levels, across, along = cells.shape
    vmem = pl.BlockSpec(memory_space=pltpu.VMEM)
    face = jax.ShapeDtypeStruct((3 * across + 8, along), f32)
    return pl.pallas_call(
        faces_kernel,
        out_shape=(
            jax.ShapeDtypeStruct((levels, across, along), f32),
            face,
            face,
        ),
        in_specs=[vmem] * 3,
        out_specs=(vmem,) * 3,
        compiler_params=pltpu.CompilerParams(vmem_limit_bytes=8 * MIB),
        name="faces",
    )(cells, *lines)


EDGE = 8
TILES = 16
PARCEL = 3 * TILES + 8


def parcel_kernel(shared_ref, side_a, side_b, leaving_ref, parcel_ref):
    refs = (shared_ref, side_a, side_b)
    for k, ref in enumerate(refs):
        parcel_ref[k * TILES : (k + 1) * TILES] = ref[0:TILES]
    rows = [ref[TILES : TILES + 1] for ref in refs]
    parcel_ref[3 * TILES : PARCEL] = jnp.concatenate([*rows, jnp.zeros((5, LANES), f32)], axis=0)
    count = leaving_ref.shape[1]
    for d in range(6):
        parcel_ref[PARCEL + d * count : PARCEL + (d + 1) * count] = leaving_ref[d]


def parcel_of(shared, side, leaving):
    vmem = pl.BlockSpec(memory_space=pltpu.VMEM)
    return pl.pallas_call(
        parcel_kernel,
        out_shape=jax.ShapeDtypeStruct((PARCEL + leaving.shape[0] * leaving.shape[1], LANES), f32),
        in_specs=[vmem] * 4,
        out_specs=vmem,
        compiler_params=pltpu.CompilerParams(vmem_limit_bytes=4 * MIB),
        name="parcel",
    )(shared, *side, leaving)


def placed(owners, values, present, levels, across, along):
    quarters = along // LANES
    wide = across + 2 * EDGE
    left, right = position()[:2]
    lane = lax.broadcasted_iota(i32, (1, LANES), 1)
    shift_q, shift_x = quarters.bit_length() - 1, across.bit_length() - 1
    code = jnp.full((1, LANES), -1, i32)
    for n, owner in enumerate(owners):
        owner = owner.astype(i32)
        x = ((owner >> shift_q) & (across - 1)) + (EDGE + (n - 1) * across)
        z = owner >> (shift_q + shift_x)
        here = ((lane >> 4) == n) | ((lane >> 4) == n + 3)
        here = here & (x >= EDGE - 2) & (x < EDGE + across + 2)
        if n == 0:
            here = here & left
        if n == 2:
            here = here & right
        if present is not None:
            here = here & present
        code = jnp.where(here, (z * wide + x) * quarters + (owner & (quarters - 1)), code)
    values = jnp.concatenate(values, axis=0)
    high = values.astype(bf16)
    low = (values - high.astype(f32)).astype(bf16)
    values = jnp.concatenate([high, low, jnp.zeros((LANES - 6 * TILES, LANES), bf16)], axis=0)
    spot = lax.broadcasted_iota(i32, (levels * wide, LANES), 0) * quarters
    found = []
    for k in range(quarters):
        table = jnp.where(code == spot + k, 1.0, 0.0).astype(bf16)
        found.append(jnp.dot(table, values, preferred_element_type=f32))
    return found


def low_of(is_even, one, two):
    return jnp.where(is_even, two, one)


def high_of(is_even, one, two):
    return jnp.where(is_even, one, two)


def across_and_along(mid):
    wide, along = mid.shape
    place = lax.broadcasted_iota(i32, (wide, along), 1)
    total = pltpu.roll(mid, 1, 0) + pltpu.roll(mid, wide - 1, 0)
    total = total + jnp.where(place > 0, pltpu.roll(mid, 1, 1), 0.0)
    return total + jnp.where(place < along - 1, pltpu.roll(mid, along - 1, 1), 0.0)


def right_side_kernel(
    own_ref, shared_ref, side_a, side_b, cells_ref, scaling_ref, line_a, line_b, rhs_ref, mid_ref, part_ref, ends_ref
):
    levels, across, along = scaling_ref.shape
    wide = across + 2 * EDGE
    inner = slice(EDGE, EDGE + across)
    quarters = along // LANES
    left, right, _, _, _, even_c = position()
    parts = [low_of(even_c, side_a[...], side_b[...]), shared_ref[...], high_of(even_c, side_a[...], side_b[...])]
    values = [parts[0][0:TILES], own_ref[...], parts[2][0:TILES]]
    owners = [part[TILES : TILES + 1] for part in parts]
    for k, found in enumerate(placed(owners, values, None, levels, across, along)):
        for z in range(levels):
            mid_ref[z, :, k * LANES : (k + 1) * LANES] = -found[z * wide : (z + 1) * wide]
    ends_ref[...] = jnp.zeros_like(ends_ref)
    for z in range(levels):
        rhs = cells_ref[0, z] + mid_ref[z, inner]
        rhs_ref[z] = rhs
        mid_ref[z, inner] = scaling_ref[z] * rhs
        for choose, start, present, beside_at, end in (
            (low_of, EDGE - 2, left, 1, EDGE - 1),
            (high_of, EDGE + across, right, 0, EDGE),
        ):
            for k in range(2):
                x = slice(start + k, start + k + 1)
                for q in range(quarters):
                    part = slice(q * LANES, (q + 1) * LANES)
                    kinds = [
                        choose(even_c, *[line_at(lines, z, k, kind, q, quarters) for lines in (line_a, line_b)])
                        for kind in range(2)
                    ]
                    m = jnp.where(present, 1.0 / (6.0 + kinds[1]), 0.0)
                    mid_ref[z, x, part] += m * kinds[0]
                    if k == beside_at:
                        ends_ref[z, end : end + 1, part] = m
    for z in range(levels):
        total = across_and_along(mid_ref[z])
        if z > 0:
            total = total + mid_ref[z - 1]
        if z < levels - 1:
            total = total + mid_ref[z + 1]
        part_ref[z] = total


def right_side_of(own, shared, side, cells, scaling, lines):
    levels, across, along = scaling.shape
    vmem = pl.BlockSpec(memory_space=pltpu.VMEM)
    whole = jax.ShapeDtypeStruct((levels, across + 2 * EDGE, along), f32)
    return pl.pallas_call(
        right_side_kernel,
        out_shape=(
            jax.ShapeDtypeStruct(scaling.shape, f32),
            whole,
            whole,
            jax.ShapeDtypeStruct((levels, 2 * EDGE, along), f32),
        ),
        in_specs=[vmem] * 8,
        out_specs=(vmem,) * 4,
        cost_estimate=pl.CostEstimate(flops=10**9, bytes_accessed=4096, transcendentals=0),
        compiler_params=pltpu.CompilerParams(vmem_limit_bytes=8 * MIB),
        name="right_side",
    )(own, shared, *side, cells, scaling, *lines)


def products_kernel(
    height_b, height_a, rhs_ref, mid_ref, part_ref, ends_ref, scaling_ref, face_a, face_b,
    near_ref, far_ref, dots_ref, outer, second,
):
    levels, across, along = scaling_ref.shape
    wide = across + 2 * EDGE
    inner = slice(EDGE, EDGE + across)
    quarters = along // LANES
    _, _, below, above, even, even_c = position()
    for start, choose, present in ((0, low_of, below), (levels, high_of, above)):
        block = choose(even, height_a[0:PARCEL], height_b[0:PARCEL])
        tiles = [block[k * TILES : (k + 1) * TILES] for k in range(3)]
        rows = [block[3 * TILES + k : 3 * TILES + k + 1] for k in range(3)]
        values = [low_of(even_c, tiles[1], tiles[2]), tiles[0], high_of(even_c, tiles[1], tiles[2])]
        owners = [low_of(even_c, rows[1], rows[2]), rows[0], high_of(even_c, rows[1], rows[2])]
        for k, found in enumerate(placed(owners, values, present, levels, across, along)):
            for z in range(levels):
                outer[start + z, :, k * LANES : (k + 1) * LANES] = -found[z * wide : (z + 1) * wide]
    for n, (layer, far_layer, own_layer, choose, present) in enumerate(
        ((levels - 1, levels - 2, 0, low_of, below), (levels, levels + 1, levels - 1, high_of, above))
    ):
        at = 0 if n == 0 else levels + 1
        second[at, 0:EDGE] = jnp.zeros((EDGE, along), f32)
        second[at, EDGE + across :] = jnp.zeros((EDGE, along), f32)
        part = [slice(n * across, (n + 1) * across) for n in range(3)]
        near = across_and_along(outer[layer]) + outer[far_layer] + mid_ref[own_layer]
        near = near[inner] + choose(even, face_a[part[2]], face_b[part[2]])
        second[at, inner] = jnp.where(present, choose(even, face_a[part[0]], face_b[part[0]]) * near, 0.0)
        outer[layer, inner] += jnp.where(present, choose(even, face_a[part[1]], face_b[part[1]]), 0.0)
        for n, x in enumerate((EDGE - 1, EDGE + across)):
            line = slice(3 * across + n, 3 * across + n + 1)
            outer[layer, x : x + 1] += jnp.where(present, choose(even, face_a[line], face_b[line]), 0.0)

    dots = [jnp.zeros((8, LANES), f32)] * 4

    def folded(value):
        value = jnp.sum(value.reshape(across // 8, 8, along), axis=0)
        return sum(value[:, k * LANES : (k + 1) * LANES] for k in range(quarters))

    for z in range(levels):
        near = part_ref[z]
        if z == 0:
            near = near + outer[levels - 1]
        if z == levels - 1:
            near = near + outer[levels]
        second[z + 1, 0:EDGE] = ends_ref[z, 0:EDGE] * near[0:EDGE]
        second[z + 1, EDGE + across :] = ends_ref[z, EDGE:] * near[EDGE + across :]
        near = near[inner]
        scaled = scaling_ref[z] * near
        second[z + 1, inner] = scaled
        near_ref[z] = near
        start = mid_ref[z, inner]
        dots[0] = dots[0] + folded(start * rhs_ref[z])
        dots[1] = dots[1] + folded(start * near)
        dots[2] = dots[2] + folded(scaled * near)
    for z in range(levels):
        far = (across_and_along(second[z + 1]) + second[z] + second[z + 2])[inner]
        far_ref[z] = far
        dots[3] = dots[3] + folded(second[z + 1, inner] * far)
    lane = lax.broadcasted_iota(i32, (1, LANES), 1)
    line = jnp.zeros((1, LANES), f32)
    for k in range(4):
        total = jnp.sum(jnp.sum(dots[k], axis=0, keepdims=True), axis=1, keepdims=True)
        line = jnp.where(lane == k, total, line)
    dots_ref[...] = jnp.broadcast_to(line, dots_ref.shape)


def products_of(height, rhs, mid, part, ends, scaling, faces, devices):
    levels, across, along = scaling.shape
    vmem = pl.BlockSpec(memory_space=pltpu.VMEM)
    return pl.pallas_call(
        products_kernel,
        out_shape=(jax.ShapeDtypeStruct(scaling.shape, f32),) * 2 + (jax.ShapeDtypeStruct((devices, LANES), f32),),
        in_specs=[vmem] * 9,
        out_specs=(vmem,) * 3,
        scratch_shapes=[
            pltpu.VMEM((2 * levels, across + 2 * EDGE, along), f32),
            pltpu.VMEM((levels + 2, across + 2 * EDGE, along), f32),
        ],
        compiler_params=pltpu.CompilerParams(vmem_limit_bytes=16 * MIB),
        name="products",
    )(*reversed(height), rhs, mid, part, ends, scaling, *faces)


def results_kernel(
    keeps_ref, places_ref, dots_ref, rhs_ref, near_ref, far_ref, scaling_ref, settled_ref, height_a, height_b,
    positions_out, velocities_out, pressure_out, residual_out, positions, velocities, pressure, residual, sent,
):
    rows, cols = settled_ref.shape[:2]
    levels = rhs_ref.shape[0]
    even = position()[4]
    for r in range(1, rows):
        for c in range(cols):
            kept = settled_ref[r, c]
            if r == rows - 1:
                kept = kept * keeps_ref[c : c + 1]
            for d in range(3):
                positions[d, r, c : c + 1] = kept[d : d + 1]
                velocities[d, r, c : c + 1] = kept[d + 3 : d + 4]
    start = PARCEL
    for d in range(6):
        block = slice(start + d * cols, start + (d + 1) * cols)
        tiles = jnp.where(even, height_b[block], height_a[block])
        target = positions if d < 3 else velocities
        target[d % 3, 0] = sum(places_ref[k] * tiles[k : k + 1] for k in range(cols))
    copies = [
        pltpu.make_async_copy(positions, positions_out, sent.at[0]),
        pltpu.make_async_copy(velocities, velocities_out, sent.at[1]),
    ]
    for copy in copies:
        copy.start()
    totals = jnp.sum(dots_ref[...], axis=0, keepdims=True)
    g00, g01, g11, g12 = [totals[:, k : k + 1] for k in range(4)]
    ratio = g01 / g00
    alpha = g00 / (g00 - g01)
    square = alpha * alpha
    renewed = square * (g11 - ratio * g01)
    beta = renewed / g00
    crossed = square * (ratio * ratio * g01 - 2.0 * ratio * g11 + g12)
    curvature = renewed - crossed - beta * renewed / alpha
    later = renewed / curvature
    one = alpha + later * (1.0 - alpha + beta)
    two = later * alpha
    for z in range(levels):
        rhs, near = rhs_ref[z], near_ref[z]
        pressure[z] = scaling_ref[z] * (one * rhs + two * near)
        residual[z] = (1.0 - one) * rhs + (one - two) * near + two * far_ref[z]
        for n, (source, target) in enumerate(((pressure, pressure_out), (residual, residual_out))):
            copy = pltpu.make_async_copy(source.at[z], target.at[z], sent.at[2 + 2 * z + n])
            copy.start()
            copies.append(copy)
    for copy in copies:
        copy.wait()


def results_of(keeps, places, dots, rhs, near, far, scaling, settled, height):
    rows, cols = settled.shape[:2]
    smem = pl.BlockSpec(memory_space=pltpu.SMEM)
    vmem = pl.BlockSpec(memory_space=pltpu.VMEM)
    particle = jax.ShapeDtypeStruct((3, rows, cols, LANES), f32)
    field = jax.ShapeDtypeStruct(rhs.shape, f32)
    return pl.pallas_call(
        results_kernel,
        out_shape=(particle, particle, field, field),
        in_specs=[vmem] * 10,
        out_specs=(pl.BlockSpec(memory_space=pl.ANY),) * 4,
        scratch_shapes=[
            *[pltpu.VMEM(particle.shape, f32)] * 2,
            *[pltpu.VMEM(field.shape, f32)] * 2,
            pltpu.SemaphoreType.DMA((2 + 2 * rhs.shape[0],)),
        ],
        compiler_params=pltpu.CompilerParams(vmem_limit_bytes=8 * MIB),
        name="results",
    )(keeps, places, dots, rhs, near, far, scaling, settled, *height)


def on_device(
    positions, velocities, contacts, exit_flags, inlet_slots, cell_blocks, cell_slots, gas_source, diagonal
):
    heights, groups = lax.axis_size("height"), lax.axis_size("cols")
    h, c = lax.axis_index("height"), lax.axis_index("cols")
    *sides, flags, ints, slots, state, cells = packed(
        exit_flags, cell_blocks, inlet_slots, positions, velocities, contacts.transpose(1, 2, 0), cell_slots,
        gas_source, diagonal,
    )
    lines = [
        lax.ppermute(value, ("height", "cols"), matching(heights, groups, "cols", odd, True))
        for value, odd in zip(sides, (False, True))
    ]
    rows, cols = state.shape[1:3]
    picks, keeps, places, weights, owners = marks_of(ints, cells, rows * cols, cols)
    window = merged(state, flags, lines, owners)
    beside = exchanged(window, "height", False)
    own_parts = own_sums(window, *state.shape[1:3])
    scaling, *faces = faces_of(cells, lines)
    faces, beside = lax.optimization_barrier((faces, beside))
    faces = [
        lax.ppermute(value, ("height", "cols"), matching(heights, groups, "height", odd, False))
        for value, odd in zip(faces, (False, True))
    ]
    settled, leaving = particles(picks, *beside, own_parts)
    own, shared = deposits(settled, slots, weights, owners)
    near = exchanged(shared, "cols", True)
    parcel = parcel_of(shared, near, leaving)
    parcels = exchanged(parcel, "height", True)
    rhs, mid, part, ends = right_side_of(own, shared, near, cells, scaling, lines)
    first, second, dots = products_of(parcels, rhs, mid, part, ends, scaling, faces, heights * groups)
    dots = lax.all_to_all(dots, ("height", "cols"), 0, 0, tiled=True)
    return results_of(keeps, places, dots, rhs, first, second, scaling, settled, parcels)


def solution(mesh):
    in_specs = (
        P(None, "height", "cols", None),
        P(None, "height", "cols", None),
        P(None, "height", "cols"),
        P("height", "cols"),
        P("height", "cols"),
        P("height", "cols"),
        P("height", "cols", None),
        P("height", "cols", None),
        P("height", "cols", None),
    )
    out_specs = (
        P(None, "height", "cols", None),
        P(None, "height", "cols", None),
        P("height", "cols", None),
        P("height", "cols", None),
    )
    return jax.shard_map(
        on_device, mesh=mesh, in_specs=in_specs, out_specs=out_specs, check_vma=False
    )
```

```python
import functools
import jax
import jax.numpy as jnp
from jax import lax
from jax.experimental import pallas as pl
from jax.experimental.pallas import tpu as pltpu
from jax.sharding import PartitionSpec as P

f32, bf16, i32 = jnp.float32, jnp.bfloat16, jnp.int32
spring = 0.05
cutoff_sq = 1.44
damping = 0.5
step_dt = 0.05
gravity = 1.0
deposit_gain = 2.0
LANES = 128
COMPS = 8
DEPTH = 2
ROWS_OUT = 24
FLAG_LANES = 16
MIB = 1024 * 1024
NEARS = 6
EXITS, OWNERS, INLETS = 0, 16, 32


def rounded(value):
    return value.astype(bf16).astype(f32)


def rounded_pair(value):
    high = rounded(value)
    return high, rounded(value - high)


def split(value):
    high = rounded(value)
    mid = rounded(value - high)
    return high, mid, value - high - mid


def centred(tile, r, c, rows, wide):
    row = lax.broadcasted_iota(i32, (COMPS, LANES), 0)
    side = jnp.float32(c - wide // 2)
    up = (r - rows // 2).astype(f32)
    return tile + jnp.where(row == 0, side, jnp.where(row == 2, up, 0.0))


def place_parts(tile, r, c, rows, wide):
    row = lax.broadcasted_iota(i32, (COMPS, LANES), 0)
    place = jnp.where(row < 3, centred(tile, r, c, rows, wide), 0.0)
    high, mid = rounded_pair(place)
    place = high + mid
    return high, mid, -jnp.sum(place * place, axis=0, keepdims=True)


def source_features(tile, r, c, rows, wide):
    row = lax.broadcasted_iota(i32, (COMPS, LANES), 0)
    row32 = lax.broadcasted_iota(i32, (32, LANES), 0)
    high, mid, size = place_parts(tile, r, c, rows, wide)
    size_high, size_mid, size_low = split(size)
    first = jnp.where(row < 3, high, 1.0)
    first = jnp.where(row == 3, size_high, jnp.where(row == 4, size_mid, jnp.where(row == 5, size_low, first)))
    second = jnp.where(row < 3, high, jnp.where(row == 3, 1.0, 0.0))
    kind = lax.rem(r, 3) * 4 + c % 4
    kind = kind + jnp.where(kind < 4, 12, jnp.where(kind < 9, 15, 18))
    near = jnp.concatenate([first, second, mid, mid], axis=0) + jnp.where(row32 == kind, 1.0, 0.0)
    high, mid, low = split(centred(tile, r, c, rows, wide) - damping * pltpu.roll(tile, 5, 0))
    first = jnp.where(row < 3, high, jnp.where(row == 3, 1.0, 0.0))
    second = jnp.where(row < 3, mid, jnp.where(row < 4, 0.0, pltpu.roll(low, 4, 0)))
    return near, jnp.concatenate([first, second], axis=0).astype(bf16)


def target_features(tile, r, c, rows, wide):
    row = lax.broadcasted_iota(i32, (COMPS, LANES), 0)
    row32 = lax.broadcasted_iota(i32, (32, LANES), 0)
    lane32 = lax.broadcasted_iota(i32, (32, LANES), 1)
    high, mid, size = place_parts(tile, r, c, rows, wide)
    own_high, own_mid, own_low = split(cutoff_sq + size)
    first = jnp.where(row < 3, 2.0 * high, jnp.where(row < 6, 1.0, jnp.where(row == 6, own_high, own_mid)))
    second = jnp.where(row < 3, 2.0 * mid, jnp.where(row == 3, own_low, 0.0))
    third = jnp.where(row < 3, 2.0 * high, 0.0)
    fourth = jnp.where(row < 3, 2.0 * mid, 0.0)
    kind = jnp.where(row32 < 16, row32 - 12, jnp.where(row32 < 24, row32 - 15, row32 - 18))
    is_kind = ((row32 >= 12) & (row32 < 16)) | ((row32 >= 19) & (row32 < 24)) | ((row32 >= 27) & (row32 < 30))
    kind_row = jnp.where(kind < 4, 0, jnp.where(kind < 8, 1, 2))
    up = kind_row + lax.rem(4 - lax.rem(r, 3), 3)
    up = jnp.where(up > 2, up - 3, up)
    side = kind - 4 * kind_row + (5 - c % 4) % 4
    side = jnp.where(side > 3, side - 4, side)
    if DEPTH <= c < wide - DEPTH:
        start = (c - DEPTH) * FLAG_LANES
    else:
        start = (lax.rem(r, DEPTH) * DEPTH + c % 2) * FLAG_LANES
    wanted = jnp.where(side < 3, 3 * up + side + start, LANES)
    flags = jnp.sum(jnp.where(lane32 == wanted, tile[6:7, :], 0.0), axis=1, keepdims=True)
    barred = jnp.where(is_kind, -1024.0 * (1.0 - flags), 0.0)
    return jnp.concatenate([first, second, third, fourth], axis=0) + barred


def unit_operands(tiles, r, c, rows, wide):
    features = [target_features(tile, r, c + k, rows, wide) for k, tile in enumerate(tiles)]
    features = jnp.concatenate(features, axis=1).astype(bf16)
    start = (c - 1) // 4
    ends = (c - 1, c + 2)

    def spread(part, s):
        at = 4 * (s // 4 - start) + s % 4
        return jnp.concatenate([part if k == at else jnp.zeros_like(part) for k in range(8)], axis=0)

    halves = [spread(features[:, k * LANES : (k + 1) * LANES], s) for k, s in enumerate(ends)]
    return [spread(features, c), spread(features, c + 1), jnp.concatenate(halves, axis=1)]


def pulls_row(tiles, r, columns, source_rows, rows, wide, turned, pulled, nears, founds):
    ahead = len(nears) - 1
    count = len(source_rows)
    units = [(pair, kind, i) for pair in range(len(columns)) for kind in range(3) for i in range(count)]
    blocks = wide // 4
    operands = [None] * len(columns)

    def begin(n):
        pair, kind, i = units[n]
        c = columns[pair]
        staged = (3 * pair + kind) % 2
        if i == 0:
            if kind == 0:
                operands[pair] = unit_operands(tiles[pair], r, c, rows, wide)
            pltpu.matmul_push_rhs(operands[pair][kind], staged, 0)
        start = (c - 1) // 4
        after = start + 1 if start + 1 < blocks else 0
        row = source_rows[i]
        sources = jnp.concatenate([turned(row)[start], turned(row)[after]], axis=1)
        pltpu.matmul_acc_lhs(nears[n % len(nears)], sources, load_staged_rhs=staged if i == 0 else None)

    def finish(n):
        pair, kind, i = units[n]
        c = columns[pair]
        weight = jnp.maximum(pltpu.matmul_pop(nears[n % len(nears)]), 0.0)
        high = weight.astype(bf16)
        low = (weight - high.astype(f32)).astype(bf16)
        pltpu.matmul_push_rhs(jnp.concatenate([high, low], axis=0), n % 2, 1)
        of_row = pulled(source_rows[i])
        if kind < 2:
            pulls = of_row[c + kind]
        else:
            pulls = jnp.concatenate([of_row[c - 1], of_row[c + 2]], axis=0)
        pulls = jnp.concatenate([pulls, pulls], axis=1)
        pltpu.matmul_acc_lhs(founds[2 * pair + (kind == 2)], pulls, load_staged_rhs=n % 2)

    for n in range(len(units) + ahead):
        if n < len(units):
            begin(n)
        if n >= ahead:
            finish(n - ahead)
    totals = []
    for pair in range(len(columns)):
        inner, outer = pltpu.matmul_pop(founds[2 * pair]), pltpu.matmul_pop(founds[2 * pair + 1])
        totals.append(inner + jnp.concatenate([outer[0:16, 0:LANES], outer[16:32, LANES:]], axis=1))
    return totals


def forces_of(totals, tiles, r, columns, rows, wide):
    forces = []
    for pair, c in enumerate(columns):
        for k, tile in enumerate(tiles[pair]):
            total = totals[pair][:, k * LANES : (k + 1) * LANES]
            first, second = total[0:8], total[8:16]
            moving = centred(tile, r, c + k, rows, wide) - damping * pltpu.roll(tile, 5, 0)
            forces.append((spring / cutoff_sq) * (moving * first[3:4, :] - first - second - pltpu.roll(second, 4, 0)))
    return forces


def stepped(tile, force):
    row = lax.broadcasted_iota(i32, (COMPS, LANES), 0)
    change = step_dt * force - jnp.where(row == 2, step_dt * gravity, 0.0)
    speeds = tile + pltpu.roll(change, 3, 0)
    places = tile + step_dt * pltpu.roll(speeds, 5, 0)
    return jnp.where(row < 3, places, jnp.where(row < 6, speeds, tile))


def position():
    heights, groups = lax.axis_size("height"), lax.axis_size("cols")
    h, c = lax.axis_index("height"), lax.axis_index("cols")
    return c > 0, c < groups - 1, h > 0, h < heights - 1, lax.rem(h, 2) == 0, lax.rem(c, 2) == 0


def halo_rows(rows, cols, d, r, c):
    wide = cols + 2 * DEPTH
    start = d * rows * wide
    if c < DEPTH:
        return start + rows * cols + r * DEPTH + c
    if c >= cols + DEPTH:
        return start + rows * (cols + DEPTH) + r * DEPTH + c - cols - DEPTH
    return start + r * cols + c - DEPTH


def tiles_of_block(block, place, rows, cols):
    wide = cols + 2 * DEPTH
    flag_row = 6 * rows * wide
    for r in range(rows):
        for c in range(wide):
            for d in range(6):
                row = halo_rows(rows, cols, d, r, c)
                place(r, c, d, block[row : row + 1])
            row = flag_row + (rows if c < DEPTH else rows + 1 if c >= cols + DEPTH else r)
            place(r, c, 6, block[row : row + 1])
            place(r, c, 7, jnp.zeros((1, LANES), f32))


def fill_row(tile_at, r, high, wide, turned_row, pulled_row):
    for block in range(wide // 4):
        near = []
        for c in range(4 * block, 4 * block + 4):
            places, moving = source_features(tile_at(c), r, c, high, wide)
            near.append(places)
            pulled_row[c] = moving
        turned_row[block] = jnp.concatenate(near, axis=0).T.astype(bf16)


def accumulators(wide):
    return (
        *[pltpu.ACC(0)((LANES, 2 * LANES), f32)] * NEARS,
        *[pltpu.ACC(1)((held, 2 * LANES), f32) for _ in range(wide // 2 - 1) for held in (16, 32)],
    )


def emptied(refs):
    for ref in refs:
        pltpu.matmul_pop(ref)
    return refs[:NEARS], refs[NEARS:]


def own_kernel(own_ref, state_ref, turned_ref, pulled_ref, partial_ref, *, rows, cols):
    wide = cols + 2 * DEPTH
    high = rows + 2 * DEPTH
    columns = list(range(1, wide - 1, 2))

    def place(r, c, d, value):
        state_ref[r, c, d : d + 1] = value

    tiles_of_block(own_ref, place, rows, cols)

    def one_row(r, carry):
        fill_row(lambda c: state_ref[r, c], r + DEPTH, high, wide, turned_ref.at[r], pulled_ref.at[r])
        return carry

    lax.fori_loop(0, rows, one_row, 0)

    def sums(*refs):
        nears, founds = emptied(refs)

        def one_sum(r, carry):
            tiles = [[state_ref[r, c], state_ref[r, c + 1]] for c in columns]
            totals = pulls_row(
                tiles, r + DEPTH, columns, list(range(rows)), high, wide,
                lambda row: turned_ref.at[row], lambda row: pulled_ref.at[row], nears, founds,
            )
            for pair, total in enumerate(totals):
                partial_ref[r, pair] = total
            return carry

        lax.fori_loop(0, rows, one_sum, 0)

    pl.run_scoped(sums, *accumulators(wide))


def own_sums(own, rows, cols):
    wide = cols + 2 * DEPTH
    vmem = pl.BlockSpec(memory_space=pltpu.VMEM)
    return pl.pallas_call(
        functools.partial(own_kernel, rows=rows, cols=cols),
        out_shape=(
            jax.ShapeDtypeStruct((rows, wide, COMPS, LANES), f32),
            jax.ShapeDtypeStruct((rows, wide // 4, LANES, LANES), bf16),
            jax.ShapeDtypeStruct((rows, wide, 16, LANES), bf16),
            jax.ShapeDtypeStruct((rows, wide // 2 - 1, 16, 2 * LANES), f32),
        ),
        in_specs=[vmem],
        out_specs=(vmem,) * 4,
        cost_estimate=pl.CostEstimate(flops=4 * 10**9, bytes_accessed=4096, transcendentals=0),
        compiler_params=pltpu.CompilerParams(vmem_limit_bytes=8 * MIB),
        name="own_sums",
    )(own)


def particles_kernel(
    picks_ref, first_ref, second_ref, own_ref, own_turned, own_pulled, partial_ref,
    settled_ref, leaving_ref, state, turned, pulled, begun, begun_turned, begun_pulled, blocks,
    *, rows, cols,
):
    wide = cols + 2 * DEPTH
    high = rows + 2 * DEPTH
    left, right, below, above, even, _ = position()
    one, two = first_ref[...], second_ref[...]
    blocks[0] = jnp.where(below, jnp.where(even, two, one), 0.0)
    blocks[1] = jnp.where(above, jnp.where(even, one, two), 0.0)
    for half, start in ((0, 0), (1, rows + DEPTH)):

        def place(r, c, d, value, start=start):
            state[start + r, c, d : d + 1] = value

        tiles_of_block(blocks.at[half], place, rows, cols)

    def far_row(r):
        fill_row(lambda c: state[r, c], r, high, wide, turned.at[r], pulled.at[r])

    def near_row(n, carry):
        far_row(1 + n * (rows + 1))
        return carry

    lax.fori_loop(0, 2, near_row, 0)
    for r in range(rows):
        state[DEPTH + r] = own_ref[r]
        turned[DEPTH + r] = own_turned[r]
        pulled[DEPTH + r] = own_pulled[r]

    def substeps(*refs):
        nears, founds = refs[:NEARS], refs[NEARS:]
        sources = dict(turned=lambda row: turned.at[row], pulled=lambda row: pulled.at[row], nears=nears, founds=founds)
        columns = list(range(1, wide - 1, 2))

        later = dict(
            turned=lambda row: begun_turned.at[row], pulled=lambda row: begun_pulled.at[row], nears=nears, founds=founds
        )

        def begun_row(r):
            fill_row(lambda c: begun[r, c], r, high, wide, begun_turned.at[r], begun_pulled.at[r])

        def begin_row(r, totals):
            tiles = [[state[r, c], state[r, c + 1]] for c in columns]
            forces = forces_of(totals, tiles, r, columns, high, wide)
            begun[r, 0] = jnp.zeros((COMPS, LANES), f32)
            begun[r, wide - 1] = jnp.zeros((COMPS, LANES), f32)
            for c in range(1, wide - 1):
                inside = ((r >= DEPTH) | below) & ((r < rows + DEPTH) | above)
                if c < DEPTH:
                    inside = inside & left
                if c >= cols + DEPTH:
                    inside = inside & right
                begun[r, c] = jnp.where(inside, stepped(tiles[(c - 1) // 2][(c - 1) % 2], forces[c - 1]), 0.0)

        def outer_step(n, carry):
            r = 1 + n * (rows + 1)
            begun_row(DEPTH + n * (rows - 1))
            tiles = [[state[r, c], state[r, c + 1]] for c in columns]
            begin_row(r, pulls_row(tiles, r, columns, [r - 1, r, r + 1], high, wide, **sources))
            return carry

        def inner_step(n, carry):
            r = DEPTH + n * (rows - 1)
            far_row(n * (high - 1))
            tiles = [[state[r, c], state[r, c + 1]] for c in columns]
            totals = pulls_row(tiles, r, columns, [1 + n * (rows + 1)], high, wide, **sources)
            begin_row(r, [total + partial_ref[n * (rows - 1), pair] for pair, total in enumerate(totals)])
            return carry

        lax.fori_loop(0, 2, inner_step, 0)
        lax.fori_loop(0, 2, outer_step, 0)

        begun_row(jnp.int32(1))

        def second_step(r, carry):
            columns = list(range(DEPTH, DEPTH + cols, 2))
            tiles = [[begun[r, c], begun[r, c + 1]] for c in columns]
            begun_row(jnp.int32(high - 2))
            totals = pulls_row(tiles, r, columns, [r - 1, r, r + 1], high, wide, **later)
            forces = forces_of(totals, tiles, r, columns, high, wide)
            for c in range(cols):
                settled_ref[r - DEPTH, c] = stepped(tiles[c // 2][c % 2], forces[c])
            return carry

        lax.fori_loop(DEPTH, DEPTH + rows, second_step, 0)

    pl.run_scoped(substeps, *accumulators(wide))

    for k in range(cols):
        tile = jnp.zeros((COMPS, LANES), f32)
        for c in range(cols):
            tile = tile + picks_ref[k, c : c + 1] * settled_ref[rows - 1, c]
        for d in range(6):
            leaving_ref[d, k : k + 1] = tile[d : d + 1]


def particles(picks, first, second, own):
    rows, wide = own[0].shape[:2]
    cols, high = wide - 2 * DEPTH, rows + 2 * DEPTH
    vmem = pl.BlockSpec(memory_space=pltpu.VMEM)
    return pl.pallas_call(
        functools.partial(particles_kernel, rows=rows, cols=cols),
        out_shape=(
            jax.ShapeDtypeStruct((rows, cols, COMPS, LANES), f32),
            jax.ShapeDtypeStruct((6, cols, LANES), f32),
        ),
        in_specs=[vmem] * 7,
        out_specs=(vmem, vmem),
        scratch_shapes=[
            pltpu.VMEM((high, wide, COMPS, LANES), f32),
            pltpu.VMEM((high, wide // 4, LANES, LANES), bf16),
            pltpu.VMEM((high, wide, 16, LANES), bf16),
            pltpu.VMEM((high, wide, COMPS, LANES), f32),
            pltpu.VMEM((high, wide // 4, LANES, LANES), bf16),
            pltpu.VMEM((high, wide, 16, LANES), bf16),
            pltpu.VMEM((2, *first.shape), f32),
        ],
        cost_estimate=pl.CostEstimate(flops=10**10, bytes_accessed=4096, transcendentals=0),
        compiler_params=pltpu.CompilerParams(vmem_limit_bytes=12 * MIB),
        name="particles",
    )(picks, first, second, *own)


def deposit_kernel(settled_ref, slots_ref, weights_ref, owners_ref, own_ref, shared_ref):
    rows, cols = settled_ref.shape[:2]
    row = lax.broadcasted_iota(i32, (16, LANES), 0)
    cell = lax.broadcasted_iota(i32, (LANES, LANES), 0)
    for t in range(rows * cols):
        r, c = t // cols, t % cols
        lift_high, lift_mid, lift_low = split(deposit_gain * settled_ref[r, c, 5:6, :])
        parts = jnp.where(row == 0, lift_high, jnp.where(row == 1, lift_mid, jnp.where(row == 2, lift_low, 0.0)))
        table = jnp.where(cell == slots_ref[r, c : c + 1, :], 1.0, 0.0).astype(bf16)
        gathered = lax.dot_general(parts.astype(bf16), table, (((1,), (1,)), ((), ())), preferred_element_type=f32)
        sums = jnp.sum(gathered, axis=0, keepdims=True)
        own_ref[t : t + 1, :] = sums
        shared_ref[t : t + 1, :] = weights_ref[t : t + 1] * sums
    row = lax.broadcasted_iota(i32, (ROWS_OUT - rows * cols, LANES), 0)
    shared_ref[rows * cols :, :] = jnp.where(row == 0, owners_ref[...], 0.0)


def deposits(settled, slots, weights, owners):
    rows, cols = settled.shape[:2]
    vmem = pl.BlockSpec(memory_space=pltpu.VMEM)
    return pl.pallas_call(
        deposit_kernel,
        out_shape=(
            jax.ShapeDtypeStruct((rows * cols, LANES), f32),
            jax.ShapeDtypeStruct((ROWS_OUT, LANES), f32),
        ),
        in_specs=[vmem] * 4,
        out_specs=(vmem, vmem),
        compiler_params=pltpu.CompilerParams(vmem_limit_bytes=4 * MIB),
        name="deposits",
    )(settled, slots, weights, owners)


def marks_kernel(ints_ref, cells_ref, picks_ref, keeps_ref, places_ref, weights_ref, owners_ref, blocks):
    cols = keeps_ref.shape[0]
    tiles = weights_ref.shape[0]
    _, levels, across, along = cells_ref.shape
    quarters = along // LANES
    for z in range(levels):
        for q in range(quarters):
            blocks[q, z * across : (z + 1) * across] = cells_ref[1, z, :, q * LANES : (q + 1) * LANES]
    lane = lax.broadcasted_iota(i32, (1, LANES), 1)
    row = lax.broadcasted_iota(i32, (cols, LANES), 0)
    owner_row = jnp.zeros((1, LANES), i32)
    for t in range(tiles):
        owner = ints_ref[0, OWNERS + t]
        owner_row = jnp.where(lax.rem(lane, tiles) == t, owner, owner_row)
        line = blocks[owner % quarters, pl.ds(owner // quarters, 1), :]
        weights_ref[t : t + 1, :] = 1.0 / (6.0 + line)
    owners_ref[...] = owner_row.astype(f32)
    picks_ref[...] = jnp.zeros_like(picks_ref)
    count = jnp.int32(0)
    for c in range(cols):
        flag = ints_ref[0, EXITS + tiles - cols + c]
        keeps_ref[c : c + 1] = jnp.broadcast_to(jnp.where(flag > 0, 0.0, 1.0), (1, LANES))
        for k in range(c + 1):
            picks_ref[k, c : c + 1] = jnp.broadcast_to(jnp.where((flag > 0) & (count == k), 1.0, 0.0), (1, LANES))
        count = count + flag
        places_ref[c] = jnp.where(row == ints_ref[0, INLETS + c], 1.0, 0.0)


def marks_of(ints, cells, tiles, cols):
    _, levels, across, along = cells.shape
    smem = pl.BlockSpec(memory_space=pltpu.SMEM)
    vmem = pl.BlockSpec(memory_space=pltpu.VMEM)
    return pl.pallas_call(
        marks_kernel,
        out_shape=(
            jax.ShapeDtypeStruct((cols, cols, LANES), f32),
            jax.ShapeDtypeStruct((cols, LANES), f32),
            jax.ShapeDtypeStruct((cols, cols, LANES), f32),
            jax.ShapeDtypeStruct((tiles, LANES), f32),
            jax.ShapeDtypeStruct((1, LANES), f32),
        ),
        in_specs=[smem, vmem],
        out_specs=(vmem,) * 5,
        scratch_shapes=[pltpu.VMEM((along // LANES, levels * across, LANES), f32)],
        cost_estimate=pl.CostEstimate(flops=10**9, bytes_accessed=4096, transcendentals=0),
        compiler_params=pltpu.CompilerParams(vmem_limit_bytes=4 * MIB),
        name="marks",
    )(ints, cells)


def matching(heights, groups, axis, odd, wrap):
    size = heights if axis == "height" else groups
    pairs = []
    for h in range(heights):
        for c in range(groups):
            i = h if axis == "height" else c
            j = i ^ 1 if not odd else (i + 1 if i % 2 else i - 1)
            if 0 <= j < size or wrap:
                j = j % size
                target = (j, c) if axis == "height" else (h, j)
            else:
                target = (h, c ^ 1) if axis == "height" else (h ^ 1, c)
            pairs.append((h * groups + c, target[0] * groups + target[1]))
    return pairs


def around_pairs(heights, groups):
    pairs = []
    for h in range(heights):
        for c in range(groups):
            target = (heights - 1 - h, c) if h in (0, heights - 1) else (h, c ^ 1)
            pairs.append((h * groups + c, target[0] * groups + target[1]))
    return pairs


def exchanged(value, axis, wrap):
    heights, groups = lax.axis_size("height"), lax.axis_size("cols")
    second, first = [
        lax.ppermute(value, ("height", "cols"), matching(heights, groups, axis, odd, wrap)) for odd in (True, False)
    ]
    return [first, second]


LINES = 32


def begin_kernel(zeros_ref):
    zeros_ref[...] = jnp.zeros_like(zeros_ref)


def begun_zeros():
    return pl.pallas_call(
        begin_kernel,
        out_shape=jax.ShapeDtypeStruct((8, LANES), f32),
        out_specs=pl.BlockSpec(memory_space=pltpu.VMEM),
        cost_estimate=pl.CostEstimate(flops=10**10, bytes_accessed=4096, transcendentals=0),
        compiler_params=pltpu.CompilerParams(vmem_limit_bytes=MIB),
        name="begin",
    )()


def pack_kernel(
    zeros_ref, exits_ref, owners_ref, inlets_ref, positions_ref, velocities_ref, contacts_ref, slots_in, gas_ref,
    diagonal_ref, first_ref, second_ref, flags_ref, ints_ref, slots_ref, state_ref, cells_ref, sides, wide_flags, small,
):
    rows, cols = state_ref.shape[1:3]
    _, levels, across, along = cells_ref.shape
    lane = lax.broadcasted_iota(i32, (1, LANES), 1)
    sides[...] = jnp.zeros_like(sides) + zeros_ref[0:1]
    wide_flags[...] = jnp.zeros_like(wide_flags)
    small[...] = jnp.zeros_like(small)
    state_ref[0:3] = positions_ref[...]
    state_ref[3:6] = velocities_ref[...]
    cells_ref[0] = gas_ref[...]
    cells_ref[1] = diagonal_ref[...]
    slots_ref[...] = slots_in[...]
    small[0:rows, 0:cols] = exits_ref[...]
    small[rows : 2 * rows, 0:cols] = owners_ref[...]
    small[2 * rows : 2 * rows + 1, 0:cols] = inlets_ref[...]
    ints = jnp.zeros((1, LANES), i32)
    for r in range(rows):
        ints = ints + pltpu.roll(small[r : r + 1], EXITS + r * cols, 1)
        ints = ints + pltpu.roll(small[rows + r : rows + r + 1], OWNERS + r * cols, 1)
    ints_ref[...] = ints + pltpu.roll(small[2 * rows : 2 * rows + 1], INLETS, 1)
    wide_flags[:, :, 0 : contacts_ref.shape[2]] = contacts_ref[...].astype(f32)
    flags = []
    for r in range(rows):
        spread = pltpu.roll(wide_flags[r], 0, 1, stride=FLAG_LANES, stride_axis=0)
        flags.append(jnp.sum(spread, axis=0, keepdims=True))
        flags_ref[r : r + 1] = flags[r]
    for side in range(2):
        shown = jnp.zeros((1, LANES), f32)
        for r in range(rows):
            for k in range(DEPTH):
                c = k if side == 0 else cols - DEPTH + k
                for d in range(6):
                    row = d * rows * DEPTH + r * DEPTH + k
                    sides[side, row : row + 1] = state_ref[d, r, c : c + 1]
            turn = (r * DEPTH - (0 if side == 0 else cols - DEPTH)) * FLAG_LANES
            part = pltpu.roll(flags[r], turn % LANES, 1)
            shown = jnp.where(lane // (DEPTH * FLAG_LANES) == r, part, shown)
        sides[side, 6 * rows * DEPTH : 6 * rows * DEPTH + 1] = shown
        for z in range(levels):
            for k in range(2):
                x = k if side == 0 else across - 2 + k
                for kind in range(2):
                    for q in range(along // LANES):
                        row = LINES + ((z * 2 + k) * 2 + kind) * (along // LANES) + q
                        sides[side, row : row + 1] = cells_ref[kind, z, x : x + 1, q * LANES : (q + 1) * LANES]
    even = position()[5]
    first_ref[...] = jnp.where(even, sides[1], sides[0])
    second_ref[...] = jnp.where(even, sides[0], sides[1])


def packed(exits, owners, inlets, positions, velocities, contacts, slots, gas, diagonal):
    levels, across, along = gas.shape
    rows, cols = positions.shape[1:3]
    side = jax.ShapeDtypeStruct((LINES + levels * 4 * (along // LANES), LANES), f32)
    vmem = pl.BlockSpec(memory_space=pltpu.VMEM)
    return pl.pallas_call(
        pack_kernel,
        out_shape=(
            side,
            side,
            jax.ShapeDtypeStruct((rows, LANES), f32),
            jax.ShapeDtypeStruct((1, LANES), i32),
            jax.ShapeDtypeStruct(slots.shape, i32),
            jax.ShapeDtypeStruct((6, rows, cols, LANES), f32),
            jax.ShapeDtypeStruct((2, levels, across, along), f32),
        ),
        in_specs=[vmem] * 10,
        out_specs=(vmem,) * 7,
        scratch_shapes=[
            pltpu.VMEM((2, *side.shape), f32),
            pltpu.VMEM((rows, cols, LANES), f32),
            pltpu.VMEM((8, LANES), i32),
        ],
        compiler_params=pltpu.CompilerParams(vmem_limit_bytes=8 * MIB),
        name="pack",
    )(begun_zeros(), exits, owners, inlets, positions, velocities, contacts, slots, gas, diagonal)


def merge_kernel(state_ref, flags_ref, line_a, line_b, owners_ref, window_ref):
    rows, cols = state_ref.shape[1:3]
    each = rows * (cols + 2 * DEPTH)
    count = 6 * rows * DEPTH
    left, right, _, _, _, even = position()
    one, two = line_a[0 : count + 8], line_b[0 : count + 8]
    low = jnp.where(left, jnp.where(even, two, one), 0.0)
    top = jnp.where(right, jnp.where(even, one, two), 0.0)
    for d in range(6):
        for r in range(rows):
            window_ref[d * each + r * cols : d * each + (r + 1) * cols] = state_ref[d, r]
        at = d * each + rows * cols
        piece = slice(d * rows * DEPTH, (d + 1) * rows * DEPTH)
        window_ref[at : at + rows * DEPTH] = low[piece]
        window_ref[at + rows * DEPTH : at + 2 * rows * DEPTH] = top[piece]
    window_ref[6 * each : 6 * each + 8] = jnp.concatenate(
        [flags_ref[...], low[count : count + 1], top[count : count + 1], jnp.zeros((6 - rows, LANES), f32)], axis=0
    )


def merged(state, flags, lines, owners):
    rows, cols = state.shape[1:3]
    vmem = pl.BlockSpec(memory_space=pltpu.VMEM)
    return pl.pallas_call(
        merge_kernel,
        out_shape=jax.ShapeDtypeStruct((6 * rows * (cols + 2 * DEPTH) + 8, LANES), f32),
        in_specs=[vmem] * 5,
        out_specs=vmem,
        compiler_params=pltpu.CompilerParams(vmem_limit_bytes=4 * MIB),
        name="merge",
    )(state, flags, *lines, owners)


def line_at(lines, z, k, kind, q, quarters):
    row = LINES + ((z * 2 + k) * 2 + kind) * quarters + q
    return lines[row : row + 1]


def faces_kernel(cells_ref, line_a, line_b, scaling_ref, first_ref, second_ref):
    _, levels, across, along = cells_ref.shape
    quarters = along // LANES
    left, right, _, _, even, even_c = position()
    row = lax.broadcasted_iota(i32, (across, along), 0)
    place = lax.broadcasted_iota(i32, (across, along), 1)
    scaled = []
    for z in range(levels):
        scaling_ref[z] = 1.0 / (6.0 + cells_ref[1, z])
        scaled.append(scaling_ref[z] * cells_ref[0, z])
    faces = []
    for z in range(levels):
        ends = []
        for k, present, flip in ((1, left, False), (0, right, True)):
            parts = []
            for q in range(quarters):
                kinds = []
                for kind in range(2):
                    one, two = (line_at(lines, z, k, kind, q, quarters) for lines in (line_a, line_b))
                    kinds.append(jnp.where(even_c, one, two) if flip else jnp.where(even_c, two, one))
                parts.append(jnp.where(present, kinds[0] / (6.0 + kinds[1]), 0.0))
            ends.append(jnp.concatenate(parts, axis=1))
        mid = scaled[z]
        total = scaled[levels - 1 - z]
        total = total + jnp.where(row > 0, pltpu.roll(mid, 1, 0), ends[0])
        total = total + jnp.where(row < across - 1, pltpu.roll(mid, across - 1, 0), ends[1])
        total = total + jnp.where(place > 0, pltpu.roll(mid, 1, 1), 0.0)
        total = total + jnp.where(place < along - 1, pltpu.roll(mid, along - 1, 1), 0.0)
        outer = jnp.concatenate([*ends, jnp.zeros((6, along), f32)], axis=0)
        faces.append((scaling_ref[z], mid, total, outer))
    for n in range(4):
        bottom, top = faces[0][n], faces[levels - 1][n]
        at = slice(n * across, n * across + bottom.shape[0])
        first_ref[at] = jnp.where(even, top, bottom)
        second_ref[at] = jnp.where(even, bottom, top)


def faces_of(cells, lines):
    _, levels, across, along = cells.shape
    vmem = pl.BlockSpec(memory_space=pltpu.VMEM)
    face = jax.ShapeDtypeStruct((3 * across + 8, along), f32)
    return pl.pallas_call(
        faces_kernel,
        out_shape=(
            jax.ShapeDtypeStruct((levels, across, along), f32),
            face,
            face,
        ),
        in_specs=[vmem] * 3,
        out_specs=(vmem,) * 3,
        compiler_params=pltpu.CompilerParams(vmem_limit_bytes=8 * MIB),
        name="faces",
    )(cells, *lines)


EDGE = 8
TILES = 16


def placed(parts, values, present, levels, across, along):
    quarters = along // LANES
    wide = across + 2 * EDGE
    left, right = position()[:2]
    lane = lax.broadcasted_iota(i32, (1, LANES), 1)
    shift_q, shift_x = quarters.bit_length() - 1, across.bit_length() - 1
    code = jnp.full((1, LANES), -1, i32)
    for n, part in enumerate(parts):
        owner = part[TILES : TILES + 1].astype(i32)
        x = ((owner >> shift_q) & (across - 1)) + (EDGE + (n - 1) * across)
        z = owner >> (shift_q + shift_x)
        here = ((lane >> 4) == n) | ((lane >> 4) == n + 3)
        here = here & (x >= EDGE - 2) & (x < EDGE + across + 2)
        if n == 0:
            here = here & left
        if n == 2:
            here = here & right
        if present is not None:
            here = here & present
        code = jnp.where(here, (z * wide + x) * quarters + (owner & (quarters - 1)), code)
    values = jnp.concatenate(values, axis=0)
    high = values.astype(bf16)
    low = (values - high.astype(f32)).astype(bf16)
    values = jnp.concatenate([high, low, jnp.zeros((LANES - 6 * TILES, LANES), bf16)], axis=0)
    spot = lax.broadcasted_iota(i32, (levels * wide, LANES), 0) * quarters
    found = []
    for k in range(quarters):
        table = jnp.where(code == spot + k, 1.0, 0.0).astype(bf16)
        found.append(jnp.dot(table, values, preferred_element_type=f32))
    return found


def low_of(is_even, one, two):
    return jnp.where(is_even, two, one)


def high_of(is_even, one, two):
    return jnp.where(is_even, one, two)


def across_and_along(mid):
    wide, along = mid.shape
    place = lax.broadcasted_iota(i32, (wide, along), 1)
    total = pltpu.roll(mid, 1, 0) + pltpu.roll(mid, wide - 1, 0)
    total = total + jnp.where(place > 0, pltpu.roll(mid, 1, 1), 0.0)
    return total + jnp.where(place < along - 1, pltpu.roll(mid, along - 1, 1), 0.0)


def right_side_kernel(
    own_ref, shared_ref, side_a, side_b, cells_ref, scaling_ref, line_a, line_b, rhs_ref, mid_ref, part_ref, ends_ref
):
    levels, across, along = scaling_ref.shape
    wide = across + 2 * EDGE
    inner = slice(EDGE, EDGE + across)
    quarters = along // LANES
    left, right, _, _, _, even_c = position()
    parts = [low_of(even_c, side_a[...], side_b[...]), shared_ref[...], high_of(even_c, side_a[...], side_b[...])]
    values = [parts[0][0:TILES], own_ref[...], parts[2][0:TILES]]
    for k, found in enumerate(placed(parts, values, None, levels, across, along)):
        for z in range(levels):
            mid_ref[z, :, k * LANES : (k + 1) * LANES] = -found[z * wide : (z + 1) * wide]
    ends_ref[...] = jnp.zeros_like(ends_ref)
    for z in range(levels):
        rhs = cells_ref[0, z] + mid_ref[z, inner]
        rhs_ref[z] = rhs
        mid_ref[z, inner] = scaling_ref[z] * rhs
        for choose, start, present, beside_at, end in (
            (low_of, EDGE - 2, left, 1, EDGE - 1),
            (high_of, EDGE + across, right, 0, EDGE),
        ):
            for k in range(2):
                x = slice(start + k, start + k + 1)
                for q in range(quarters):
                    part = slice(q * LANES, (q + 1) * LANES)
                    kinds = [
                        choose(even_c, *[line_at(lines, z, k, kind, q, quarters) for lines in (line_a, line_b)])
                        for kind in range(2)
                    ]
                    m = jnp.where(present, 1.0 / (6.0 + kinds[1]), 0.0)
                    mid_ref[z, x, part] += m * kinds[0]
                    if k == beside_at:
                        ends_ref[z, end : end + 1, part] = m
    for z in range(levels):
        total = across_and_along(mid_ref[z])
        if z > 0:
            total = total + mid_ref[z - 1]
        if z < levels - 1:
            total = total + mid_ref[z + 1]
        part_ref[z] = total


def right_side_of(own, shared, side, cells, scaling, lines):
    levels, across, along = scaling.shape
    vmem = pl.BlockSpec(memory_space=pltpu.VMEM)
    whole = jax.ShapeDtypeStruct((levels, across + 2 * EDGE, along), f32)
    return pl.pallas_call(
        right_side_kernel,
        out_shape=(
            jax.ShapeDtypeStruct(scaling.shape, f32),
            whole,
            whole,
            jax.ShapeDtypeStruct((levels, 2 * EDGE, along), f32),
        ),
        in_specs=[vmem] * 8,
        out_specs=(vmem,) * 4,
        cost_estimate=pl.CostEstimate(flops=10**9, bytes_accessed=4096, transcendentals=0),
        compiler_params=pltpu.CompilerParams(vmem_limit_bytes=8 * MIB),
        name="right_side",
    )(own, shared, *side, cells, scaling, *lines)


def products_kernel(
    height_b, height_a, rhs_ref, mid_ref, part_ref, ends_ref, scaling_ref, face_a, face_b,
    near_ref, far_ref, dots_ref, outer, second,
):
    levels, across, along = scaling_ref.shape
    wide = across + 2 * EDGE
    inner = slice(EDGE, EDGE + across)
    quarters = along // LANES
    _, _, below, above, even, even_c = position()
    for start, choose, present in ((0, low_of, below), (levels, high_of, above)):
        block = [
            choose(even, height_a[k * ROWS_OUT : (k + 1) * ROWS_OUT], height_b[k * ROWS_OUT : (k + 1) * ROWS_OUT])
            for k in range(3)
        ]
        parts = [low_of(even_c, block[1], block[2]), block[0], high_of(even_c, block[1], block[2])]
        values = [part[0:TILES] for part in parts]
        for k, found in enumerate(placed(parts, values, present, levels, across, along)):
            for z in range(levels):
                outer[start + z, :, k * LANES : (k + 1) * LANES] = -found[z * wide : (z + 1) * wide]
    for n, (layer, far_layer, own_layer, choose, present) in enumerate(
        ((levels - 1, levels - 2, 0, low_of, below), (levels, levels + 1, levels - 1, high_of, above))
    ):
        at = 0 if n == 0 else levels + 1
        second[at, 0:EDGE] = jnp.zeros((EDGE, along), f32)
        second[at, EDGE + across :] = jnp.zeros((EDGE, along), f32)
        part = [slice(n * across, (n + 1) * across) for n in range(3)]
        near = across_and_along(outer[layer]) + outer[far_layer] + mid_ref[own_layer]
        near = near[inner] + choose(even, face_a[part[2]], face_b[part[2]])
        second[at, inner] = jnp.where(present, choose(even, face_a[part[0]], face_b[part[0]]) * near, 0.0)
        outer[layer, inner] += jnp.where(present, choose(even, face_a[part[1]], face_b[part[1]]), 0.0)
        for n, x in enumerate((EDGE - 1, EDGE + across)):
            line = slice(3 * across + n, 3 * across + n + 1)
            outer[layer, x : x + 1] += jnp.where(present, choose(even, face_a[line], face_b[line]), 0.0)

    dots = [jnp.zeros((8, LANES), f32)] * 4

    def folded(value):
        value = jnp.sum(value.reshape(across // 8, 8, along), axis=0)
        return sum(value[:, k * LANES : (k + 1) * LANES] for k in range(quarters))

    for z in range(levels):
        near = part_ref[z]
        if z == 0:
            near = near + outer[levels - 1]
        if z == levels - 1:
            near = near + outer[levels]
        second[z + 1, 0:EDGE] = ends_ref[z, 0:EDGE] * near[0:EDGE]
        second[z + 1, EDGE + across :] = ends_ref[z, EDGE:] * near[EDGE + across :]
        near = near[inner]
        scaled = scaling_ref[z] * near
        second[z + 1, inner] = scaled
        near_ref[z] = near
        start = mid_ref[z, inner]
        dots[0] = dots[0] + folded(start * rhs_ref[z])
        dots[1] = dots[1] + folded(start * near)
        dots[2] = dots[2] + folded(scaled * near)
    for z in range(levels):
        far = (across_and_along(second[z + 1]) + second[z] + second[z + 2])[inner]
        far_ref[z] = far
        dots[3] = dots[3] + folded(second[z + 1, inner] * far)
    lane = lax.broadcasted_iota(i32, (1, LANES), 1)
    line = jnp.zeros((1, LANES), f32)
    for k in range(4):
        total = jnp.sum(jnp.sum(dots[k], axis=0, keepdims=True), axis=1, keepdims=True)
        line = jnp.where(lane == k, total, line)
    dots_ref[...] = jnp.broadcast_to(line, dots_ref.shape)


def products_of(height, rhs, mid, part, ends, scaling, faces, devices):
    levels, across, along = scaling.shape
    vmem = pl.BlockSpec(memory_space=pltpu.VMEM)
    return pl.pallas_call(
        products_kernel,
        out_shape=(jax.ShapeDtypeStruct(scaling.shape, f32),) * 2 + (jax.ShapeDtypeStruct((devices, LANES), f32),),
        in_specs=[vmem] * 9,
        out_specs=(vmem,) * 3,
        scratch_shapes=[
            pltpu.VMEM((2 * levels, across + 2 * EDGE, along), f32),
            pltpu.VMEM((levels + 2, across + 2 * EDGE, along), f32),
        ],
        compiler_params=pltpu.CompilerParams(vmem_limit_bytes=16 * MIB),
        name="products",
    )(*reversed(height), rhs, mid, part, ends, scaling, *faces)


def results_kernel(
    keeps_ref, places_ref, dots_ref, rhs_ref, near_ref, far_ref, scaling_ref, settled_ref, height_a, height_b,
    positions_out, velocities_out, pressure_out, residual_out, positions, velocities, pressure, residual, sent,
):
    rows, cols = settled_ref.shape[:2]
    levels = rhs_ref.shape[0]
    even = position()[4]
    for r in range(1, rows):
        for c in range(cols):
            kept = settled_ref[r, c]
            if r == rows - 1:
                kept = kept * keeps_ref[c : c + 1]
            for d in range(3):
                positions[d, r, c : c + 1] = kept[d : d + 1]
                velocities[d, r, c : c + 1] = kept[d + 3 : d + 4]
    start = 3 * ROWS_OUT
    for d in range(6):
        block = slice(start + d * cols, start + (d + 1) * cols)
        tiles = jnp.where(even, height_b[block], height_a[block])
        target = positions if d < 3 else velocities
        target[d % 3, 0] = sum(places_ref[k] * tiles[k : k + 1] for k in range(cols))
    copies = [
        pltpu.make_async_copy(positions, positions_out, sent.at[0]),
        pltpu.make_async_copy(velocities, velocities_out, sent.at[1]),
    ]
    for copy in copies:
        copy.start()
    totals = jnp.sum(dots_ref[...], axis=0, keepdims=True)
    g00, g01, g11, g12 = [totals[:, k : k + 1] for k in range(4)]
    ratio = g01 / g00
    alpha = g00 / (g00 - g01)
    square = alpha * alpha
    renewed = square * (g11 - ratio * g01)
    beta = renewed / g00
    crossed = square * (ratio * ratio * g01 - 2.0 * ratio * g11 + g12)
    curvature = renewed - crossed - beta * renewed / alpha
    later = renewed / curvature
    one = alpha + later * (1.0 - alpha + beta)
    two = later * alpha
    for z in range(levels):
        rhs, near = rhs_ref[z], near_ref[z]
        pressure[z] = scaling_ref[z] * (one * rhs + two * near)
        residual[z] = (1.0 - one) * rhs + (one - two) * near + two * far_ref[z]
        for n, (source, target) in enumerate(((pressure, pressure_out), (residual, residual_out))):
            copy = pltpu.make_async_copy(source.at[z], target.at[z], sent.at[2 + 2 * z + n])
            copy.start()
            copies.append(copy)
    for copy in copies:
        copy.wait()


def results_of(keeps, places, dots, rhs, near, far, scaling, settled, height):
    rows, cols = settled.shape[:2]
    smem = pl.BlockSpec(memory_space=pltpu.SMEM)
    vmem = pl.BlockSpec(memory_space=pltpu.VMEM)
    particle = jax.ShapeDtypeStruct((3, rows, cols, LANES), f32)
    field = jax.ShapeDtypeStruct(rhs.shape, f32)
    return pl.pallas_call(
        results_kernel,
        out_shape=(particle, particle, field, field),
        in_specs=[vmem] * 10,
        out_specs=(pl.BlockSpec(memory_space=pl.ANY),) * 4,
        scratch_shapes=[
            *[pltpu.VMEM(particle.shape, f32)] * 2,
            *[pltpu.VMEM(field.shape, f32)] * 2,
            pltpu.SemaphoreType.DMA((2 + 2 * rhs.shape[0],)),
        ],
        compiler_params=pltpu.CompilerParams(vmem_limit_bytes=8 * MIB),
        name="results",
    )(keeps, places, dots, rhs, near, far, scaling, settled, *height)


def on_device(
    positions, velocities, contacts, exit_flags, inlet_slots, cell_blocks, cell_slots, gas_source, diagonal
):
    heights, groups = lax.axis_size("height"), lax.axis_size("cols")
    h, c = lax.axis_index("height"), lax.axis_index("cols")
    *sides, flags, ints, slots, state, cells = packed(
        exit_flags, cell_blocks, inlet_slots, positions, velocities, contacts.transpose(1, 2, 0), cell_slots,
        gas_source, diagonal,
    )
    lines = [
        lax.ppermute(value, ("height", "cols"), matching(heights, groups, "cols", odd, True))
        for value, odd in zip(sides, (False, True))
    ]
    rows, cols = state.shape[1:3]
    picks, keeps, places, weights, owners = marks_of(ints, cells, rows * cols, cols)
    window = merged(state, flags, lines, owners)
    beside = exchanged(window, "height", False)
    own_parts = own_sums(window, *state.shape[1:3])
    scaling, *faces = faces_of(cells, lines)
    faces, beside = lax.optimization_barrier((faces, beside))
    faces = [
        lax.ppermute(value, ("height", "cols"), matching(heights, groups, "height", odd, False))
        for value, odd in zip(faces, (False, True))
    ]
    settled, leaving = particles(picks, *beside, own_parts)
    own, shared = deposits(settled, slots, weights, owners)
    near = exchanged(shared, "cols", True)
    parcel = jnp.concatenate([shared, *near, leaving.reshape(-1, LANES)], axis=0)
    parcels = exchanged(parcel, "height", True)
    rhs, mid, part, ends = right_side_of(own, shared, near, cells, scaling, lines)
    first, second, dots = products_of(parcels, rhs, mid, part, ends, scaling, faces, heights * groups)
    dots = lax.all_to_all(dots, ("height", "cols"), 0, 0, tiled=True)
    return results_of(keeps, places, dots, rhs, first, second, scaling, settled, parcels)


def solution(mesh):
    in_specs = (
        P(None, "height", "cols", None),
        P(None, "height", "cols", None),
        P(None, "height", "cols"),
        P("height", "cols"),
        P("height", "cols"),
        P("height", "cols"),
        P("height", "cols", None),
        P("height", "cols", None),
        P("height", "cols", None),
    )
    out_specs = (
        P(None, "height", "cols", None),
        P(None, "height", "cols", None),
        P("height", "cols", None),
        P("height", "cols", None),
    )
    return jax.shard_map(
        on_device, mesh=mesh, in_specs=in_specs, out_specs=out_specs, check_vma=False
    )
```
